256 devices in a mesh: fsdp: 16 (over z, core), sp: 16 (over x, y).
Axes of the slice: x: 4, y: 4, z: 8, core: 2. Of those that a mesh axis runs over, the one named last changes fastest.
Arguments:
- query_raw: bfloat16 [16, 2048, 2560], P('fsdp', 'sp'), may hold values from -100 to 100
- key_raw: bfloat16 [16, 2048, 2560], P('fsdp', 'sp'), may hold values from -100 to 100
- value_in: bfloat16 [16, 2048, 2560], P('fsdp', 'sp'), may hold values from -6 to 6
- grad_out: bfloat16 [16, 2048, 2560], P('fsdp', 'sp'), may hold values from -6 to 6
- norm_gains: float32 [16, 2, 2, 128], P('sp'), may hold values from 0.5 to 1.5
- head_owner: int32 [20], replicated, may hold values from 0 to 15, as said below
Outputs:
- grad_query: bfloat16 [16, 2048, 2560], P('fsdp', 'sp')
- grad_key: bfloat16 [16, 2048, 2560], P('fsdp', 'sp')
- grad_value: bfloat16 [16, 2048, 2560], P('fsdp', 'sp')
- grad_gains: float32 [16, 2, 2, 128], P('sp')
The draws below stay inside these ranges and needn't reach their ends.
Inputs may be any that keep to these rules, and one draw needn't show every extreme that they name: `head_owner`: no device is named by more than 2 heads, and some device by exactly 2.
All inputs are finite; a program needn't handle non-finite values.
Results may differ from the reference program's by a relative error of at most 0.012.
The reference program's roundings to bfloat16 on the way count: a program that leaves them out, or rounds other values in their place, can miss the bound.
Values may be sent and summed in bfloat16 or wider, within the bound.
No kernel may reach another device: no remote copies, remote signals or barrier semaphores. Data moves between devices by JAX's collectives and lax.ppermute only.
A program may use at most 128 MiB of HBM per device.

```python
import math
import jax
import jax.numpy as jnp
from jax import lax

HEADS = 20
DH = 128
INNER = 2560
VIDEOS = 16
SEQ = 2048
HMAX = 2
N_SP = 16


def make_field(rand_a, rand_b, rand_c, low_log, high_log):
    row_scale = jnp.exp(jax.random.uniform(rand_a, (VIDEOS, SEQ, 1), jnp.float32, low_log, high_log))
    col_scale = jnp.exp(jax.random.uniform(rand_b, (1, 1, INNER), jnp.float32, low_log, high_log))
    base_field = jnp.clip(jax.random.normal(rand_c, (VIDEOS, SEQ, INNER), jnp.float32), -6.0, 6.0)
    return base_field * row_scale * col_scale


def pair_fields(key):
    subkeys = jax.random.split(jax.random.fold_in(key, 17), 6)
    low_log, high_log = (math.log(0.3), math.log(3.0))
    query_field = make_field(subkeys[0], subkeys[1], subkeys[2], low_log, high_log)
    key_field = make_field(subkeys[3], subkeys[4], subkeys[5], low_log, high_log)
    return (query_field, key_field)


def draw_query_raw(key, part):
    return pair_fields(key)[0].astype(jnp.bfloat16)


def draw_key_raw(key, part):
    return pair_fields(key)[1].astype(jnp.bfloat16)


def draw_head_owner(key, part):
    rand_a, rand_b = jax.random.split(jax.random.fold_in(key, 29))
    device_order = jax.random.permutation(rand_a, N_SP).astype(jnp.int32)
    head_order = jax.random.permutation(rand_b, HEADS).astype(jnp.int32)
    ranks = jnp.arange(HEADS, dtype=jnp.int32)
    position = jnp.where(ranks < HMAX, 0, 1 + (ranks - HMAX) % (N_SP - 1))
    owner_by_rank = device_order[position]
    return jnp.zeros((HEADS,), jnp.int32).at[head_order].set(owner_by_rank)


def block_levels(key, shape, cuts, least, largest):
    level = 1.0
    for dim, shards_of in cuts:
        steps = jax.random.uniform(jax.random.fold_in(jax.random.fold_in(key, 6), dim), (shards_of,), jnp.float32, least / len(cuts), largest / len(cuts))
        level = level * jnp.repeat(jnp.exp(steps), shape[dim] // shards_of).reshape((-1,) + (1,) * (len(shape) - 1 - dim))
    return level


def scatter_about(stream_key, shape, scale, limit, shards=(), kind=jnp.bfloat16):
    level = block_levels(stream_key, shape, shards, -0.22, 0.18) if shards else 1.0
    values = jax.random.normal(stream_key, shape, jnp.float32) * scale * level
    return jnp.minimum(jnp.maximum(values, -limit), limit).astype(kind)


def setup_inputs(seed: int = 0) -> dict:
    splits = jax.random.split(jax.random.key(seed), 7)
    return {
        "query_raw": draw_query_raw(jax.random.fold_in(splits[6], 71), 0),
        "key_raw": draw_key_raw(jax.random.fold_in(splits[6], 71), 0),
        "value_in": scatter_about(splits[2], (VIDEOS, SEQ, INNER), 1.0, 6.0, ((0, 16), (1, 16))),
        "grad_out": scatter_about(splits[3], (VIDEOS, SEQ, INNER), 1.0, 6.0, ((0, 16), (1, 16))),
        "norm_gains": jnp.clip(0.5 + 1.0 * jax.random.uniform(splits[4], (N_SP, HMAX, 2, DH), jnp.float32) ** block_levels(splits[4], (N_SP, HMAX, 2, DH), ((0, 16),), -0.2, 0.2), 0.5, 1.5),
        "head_owner": draw_head_owner(jax.random.fold_in(splits[6], 71), 0),
    }


EPSILON = 1e-06

def owner_slots(head_owner):
    head_ids = jnp.arange(HEADS, dtype=jnp.int32)
    same_owner = head_owner[:, None] == head_owner[None, :]
    earlier = head_ids[None, :] < head_ids[:, None]
    head_slot = lax.optimization_barrier(jnp.sum((same_owner & earlier).astype(jnp.int32), axis=1)).astype(jnp.int32)
    return (head_owner * HMAX + head_slot).astype(jnp.int32)

def head_backward(operands):
    query_norm, key_norm, value_head, grad_head = operands
    score_scale = DH ** (-0.5)
    scores = jnp.dot(query_norm, key_norm.T, preferred_element_type=jnp.float32) * score_scale
    row_max = lax.optimization_barrier(jnp.max(scores, axis=-1, keepdims=True))
    exp_scores = jnp.exp(scores - row_max)
    probs = exp_scores / lax.optimization_barrier(jnp.sum(exp_scores, axis=-1, keepdims=True))
    dprobs = jnp.dot(grad_head, value_head.T, preferred_element_type=jnp.float32)
    row_delta = lax.optimization_barrier(jnp.sum(probs * dprobs, axis=-1, keepdims=True))
    dscores = (probs * (dprobs - row_delta) * score_scale).astype(jnp.bfloat16)
    grad_qn = jnp.dot(dscores, key_norm, preferred_element_type=jnp.float32).astype(jnp.bfloat16)
    grad_kn = jnp.dot(dscores.T, query_norm, preferred_element_type=jnp.float32).astype(jnp.bfloat16)
    grad_vh = jnp.dot(probs.astype(jnp.bfloat16).T, grad_head, preferred_element_type=jnp.float32).astype(jnp.bfloat16)
    return (grad_qn, grad_kn, grad_vh)

def to_heads(field):
    return field.reshape(VIDEOS, SEQ, HEADS, DH).transpose(0, 2, 1, 3).reshape(VIDEOS * HEADS, SEQ, DH)

def to_tokens(field):
    return field.reshape(VIDEOS, HEADS, SEQ, DH).transpose(0, 2, 1, 3).reshape(VIDEOS, SEQ, INNER)

def norm_forward(raw, gain):
    raw_f32 = raw.astype(jnp.float32)
    row_scale = lax.rsqrt(lax.optimization_barrier(jnp.mean(raw_f32 * raw_f32, axis=-1, keepdims=True)) + EPSILON)
    return (raw_f32, row_scale, (raw_f32 * row_scale * gain).astype(jnp.bfloat16))

def norm_backward(raw_f32, row_scale, gain, grad_norm):
    grad_f32 = grad_norm.astype(jnp.float32)
    inner_sum = lax.optimization_barrier(jnp.sum(grad_f32 * gain * raw_f32, axis=-1, keepdims=True))
    grad_raw = row_scale * gain * grad_f32 - row_scale ** 3 / INNER * raw_f32 * inner_sum
    gain_part = lax.optimization_barrier(jnp.sum(grad_f32 * raw_f32 * row_scale, axis=(0, 1)))
    return (grad_raw.astype(jnp.bfloat16), gain_part)

def reference(query_raw, key_raw, value_in, grad_out, norm_gains, head_owner):
    flat_slot = owner_slots(head_owner)
    per_head = norm_gains.reshape(N_SP * HMAX, 2, DH)[flat_slot]
    gain_query = per_head[:, 0, :].reshape(INNER)
    gain_key = per_head[:, 1, :].reshape(INNER)
    query_f32, query_scale, query_norm = norm_forward(query_raw, gain_query)
    key_f32, key_scale, key_norm = norm_forward(key_raw, gain_key)
    grad_qn, grad_kn, grad_vh = lax.map(head_backward, (to_heads(query_norm), to_heads(key_norm), to_heads(value_in), to_heads(grad_out)))
    grad_query, query_part = norm_backward(query_f32, query_scale, gain_query, to_tokens(grad_qn))
    grad_key, key_part = norm_backward(key_f32, key_scale, gain_key, to_tokens(grad_kn))
    gain_parts = jnp.stack([query_part.reshape(HEADS, DH), key_part.reshape(HEADS, DH)], axis=1)
    placed = jnp.zeros((N_SP * HMAX, 2, DH), jnp.float32).at[flat_slot].set(gain_parts)
    grad_gains = placed.reshape(N_SP, HMAX, 2, DH) * (1.0 / math.sqrt(VIDEOS * SEQ))
    return (grad_query, grad_key, to_tokens(grad_vh), grad_gains)
```

```python
import functools
import math

import jax
import jax.numpy as jnp
from jax import lax
from jax.experimental import pallas as pl
from jax.experimental.pallas import tpu as pltpu
from jax.sharding import PartitionSpec as P

EPSILON = 1e-06
LOG2E = math.log2(math.e)
f32 = jnp.float32
bf16 = jnp.bfloat16

HEADS = 20
DH = 128
INNER = HEADS * DH
SP = 16
TOK = 128
SEQ = SP * TOK
EXTRA_HEADS = HEADS - SP
GROUP = SP // EXTRA_HEADS
QTOK = TOK // GROUP
MAIN_ROWS = 4 * TOK + 32
SHARE_ROWS = 2 * TOK + 2 * QTOK + 16
MAIN_BACK = 3 * TOK
SHARE_BACK = 2 * TOK + QTOK + 32
VMEM_LIMIT = 48 * 2**20


def split3(x):
    hi = x.astype(bf16).astype(f32)
    mid = (x - hi).astype(bf16).astype(f32)
    return hi, mid, x - hi - mid


def stack_rows(rows, count):
    width = rows[0].shape[-1]
    return jnp.concatenate(
        rows + [jnp.zeros((count - len(rows), width), f32)], axis=0
    ).astype(bf16)


def contract(a, b, da, db):
    return lax.dot_general(a, b, (((da,), (db,)), ((), ())), preferred_element_type=f32)


def row_scale(raw):
    return lax.rsqrt(jnp.sum(raw * raw, axis=-1, keepdims=True) * (1.0 / INNER) + EPSILON)


def to_row(column):
    return jnp.broadcast_to(column, (TOK, TOK)).T[0:1]


def pack_kernel(q_ref, k_ref, v_ref, do_ref, gain_ref, main_ref, share_ref):
    q_row = to_row(row_scale(q_ref[0].astype(f32)))
    k_row = to_row(row_scale(k_ref[0].astype(f32)))
    gains = gain_ref[0]
    rows = [*split3(q_row), *split3(k_row)]
    for slot in range(2):
        for which in range(2):
            rows += [*split3(gains[slot, which : which + 1])]
    extra = stack_rows(rows, 32)
    for d in range(SP):
        cols = slice(d * DH, (d + 1) * DH)
        for part, ref in enumerate((q_ref, k_ref, v_ref, do_ref)):
            main_ref[d, part * TOK : (part + 1) * TOK] = ref[0, :, cols]
        main_ref[d, 4 * TOK :] = extra
        head = SP + d // GROUP
        cols = slice(head * DH, (head + 1) * DH)
        quarter = slice(d % GROUP * QTOK, (d % GROUP + 1) * QTOK)
        share_ref[d, :TOK] = k_ref[0, :, cols]
        share_ref[d, TOK : 2 * TOK] = v_ref[0, :, cols]
        share_ref[d, 2 * TOK : 2 * TOK + QTOK] = q_ref[0, quarter, cols]
        share_ref[d, 2 * TOK + QTOK : 2 * TOK + 2 * QTOK] = do_ref[0, quarter, cols]
        q_own = jnp.concatenate([q_row[:, quarter]] * GROUP, axis=1)
        share_ref[d, 2 * TOK + 2 * QTOK :] = stack_rows([*split3(q_own), *split3(k_row)], 16)


def pack(q, k, v, do, gains):
    return pl.pallas_call(
        pack_kernel,
        out_shape=[
            jax.ShapeDtypeStruct((SP, MAIN_ROWS, DH), bf16),
            jax.ShapeDtypeStruct((SP, SHARE_ROWS, DH), bf16),
        ],
        compiler_params=pltpu.CompilerParams(vmem_limit_bytes=VMEM_LIMIT),
        name="pack",
    )(q, k, v, do, gains)


def owner_slot(owner_ref, head):
    owner = owner_ref[head]
    slot = jnp.int32(0)
    for other in range(HEADS):
        same = (owner_ref[other] == owner) & (other < head)
        slot = slot + same.astype(jnp.int32)
    return owner, slot


def picked_gains(owner_ref, gain_ref, head):
    owner, slot = owner_slot(owner_ref, head)
    rows = gain_ref[owner].astype(f32)
    sums = []
    for which in range(2):
        both = []
        for s in range(2):
            at = 6 + (s * 2 + which) * 3
            both.append(rows[at : at + 1] + rows[at + 1 : at + 2] + rows[at + 2 : at + 3])
        sums.append(jnp.where(slot == 0, both[0], both[1]))
    return sums


def scale_columns(scale_ref, at):
    rows = scale_ref[...].astype(f32)
    return (rows[:, at] + rows[:, at + 1] + rows[:, at + 2]).T


def attention_kernel(
    first_head,
    head_step,
    blocks,
    rows_per_source,
    owner_ref,
    q_ref,
    k_ref,
    v_ref,
    do_ref,
    scale_ref,
    gain_ref,
    *rest,
):
    (back_refs, scratch) = (rest[:4], rest[4:])
    dq_ref, dk_ref, dv_ref, part_ref = back_refs
    s_sc, dp_sc, kn_sc, dk_acc, dv_acc, qg_acc, qn_sc, qu_sc = scratch
    step = pl.program_id(0)
    chunk = 256
    chunks = SEQ // chunk
    head = first_head + lax.axis_index("sp") // head_step
    gain_q, gain_k = picked_gains(owner_ref, gain_ref, head)
    sources = q_ref.shape[0]
    query_rows = sources * rows_per_source
    score_scale = DH**-0.5

    q_cols = scale_columns(scale_ref, 0)
    k_cols = scale_columns(scale_ref, 3)

    @pl.when(step == 0)
    def _():
        for j in range(SP):
            r = slice(j * TOK, (j + 1) * TOK)
            kn_sc[r] = (k_ref[j].astype(f32) * k_cols[:, j : j + 1] * gain_k).astype(bf16)
        qg_acc[...] = jnp.zeros_like(qg_acc)

    for b in range(blocks):

        @pl.when(step == b)
        def _():
            for j in range(sources):
                r = slice(j * rows_per_source, (j + 1) * rows_per_source)
                col = q_cols[:rows_per_source, b * sources + j : b * sources + j + 1]
                unit = q_ref[j].astype(f32) * col
                qu_sc[r] = unit
                qn_sc[r] = (unit * gain_q).astype(bf16)

    qn = qn_sc[...]
    do = do_ref[...].reshape(query_rows, DH)
    top = None
    for c in range(chunks):
        r = slice(c * chunk, (c + 1) * chunk)
        s = contract(kn_sc[r], qn, 1, 1)
        s_sc[r] = s
        part = jnp.max(s.reshape(chunk // 8, 8, query_rows), axis=0)
        top = part if top is None else jnp.maximum(top, part)
    top = jnp.max(top, axis=0, keepdims=True) * (score_scale * LOG2E)
    total = delta = None
    for c in range(chunks):
        r = slice(c * chunk, (c + 1) * chunk)
        vc = v_ref[c * 2 : (c + 1) * 2].reshape(chunk, DH)
        dp = contract(vc, do, 1, 1)
        e = jnp.exp2(s_sc[r] * (score_scale * LOG2E) - top)
        s_sc[r] = e
        dp_sc[r] = dp
        e_part = jnp.sum(e.reshape(chunk // 8, 8, query_rows), axis=0)
        d_part = jnp.sum((e * dp).reshape(chunk // 8, 8, query_rows), axis=0)
        total = e_part if total is None else total + e_part
        delta = d_part if delta is None else delta + d_part
    inv = 1.0 / jnp.sum(total, axis=0, keepdims=True)
    delta = jnp.sum(delta, axis=0, keepdims=True) * inv
    dq = None
    for c in range(chunks):
        r = slice(c * chunk, (c + 1) * chunk)
        p = s_sc[r] * inv
        ds = (p * (dp_sc[r] - delta) * score_scale).astype(bf16)
        dv_part = contract(p.astype(bf16), do, 1, 0)
        dk_part = contract(ds, qn, 1, 0)
        if blocks == 1:
            dv_acc[r] = dv_part
            dk_acc[r] = dk_part
        else:

            @pl.when(step == 0)
            def _():
                dv_acc[r] = dv_part
                dk_acc[r] = dk_part

            @pl.when(step > 0)
            def _():
                dv_acc[r] += dv_part
                dk_acc[r] += dk_part

        dq_part = contract(ds, kn_sc[r], 0, 0)
        dq = dq_part if dq is None else dq + dq_part
    dq_ref[...] = (dq * gain_q).astype(bf16).reshape(dq_ref.shape)
    qg_acc[...] += jnp.sum((dq * qu_sc[...]).reshape(query_rows // 8, 8, DH), axis=0)

    @pl.when(step == blocks - 1)
    def _():
        key_part = jnp.zeros((8, DH), f32)
        for j in range(SP):
            r = slice(j * TOK, (j + 1) * TOK)
            dk = dk_acc[r]
            unit = k_ref[j].astype(f32) * k_cols[:, j : j + 1]
            key_part += jnp.sum((dk * unit).reshape(TOK // 8, 8, DH), axis=0)
            dk_ref[j] = (dk * gain_k).astype(bf16)
            dv_ref[j] = dv_acc[r].astype(bf16)
        part_ref[0:1] = jnp.sum(qg_acc[...], axis=0, keepdims=True)
        part_ref[1:2] = jnp.sum(key_part, axis=0, keepdims=True)


def attention(name, owner, field, gain_field, rows_per_source, order, extra_rows, blocks, first_head, head_step):
    sources = SP // blocks
    query_rows = sources * rows_per_source
    starts = {}
    at = 0
    for key, rows in order:
        starts[key] = (at, rows)
        at += rows

    def whole(key):
        start, rows = starts[key]
        return pl.BlockSpec((SP, rows, DH), lambda i, o: (0, start // rows, 0))

    def sliced(key):
        start, rows = starts[key]
        return pl.BlockSpec((sources, rows, DH), lambda i, o: (i, start // rows, 0))

    extra = pl.BlockSpec((SP, extra_rows, DH), lambda i, o: (0, at // extra_rows, 0))
    gains = pl.BlockSpec((SP, 32, DH), lambda i, o: (0, 4 * TOK // 32, 0))
    back = pl.BlockSpec((sources, rows_per_source, DH), lambda i, o: (i, 0, 0))
    back_all = pl.BlockSpec((SP, TOK, DH), lambda i, o: (0, 0, 0))
    grid_spec = pltpu.PrefetchScalarGridSpec(
        num_scalar_prefetch=1,
        grid=(blocks,),
        in_specs=[sliced("q"), whole("k"), whole("v"), sliced("do"), extra, gains],
        out_specs=[back, back_all, back_all, pl.BlockSpec((2, DH), lambda i, o: (0, 0))],
        scratch_shapes=[
            pltpu.VMEM((SEQ, query_rows), f32),
            pltpu.VMEM((SEQ, query_rows), f32),
            pltpu.VMEM((SEQ, DH), bf16),
            pltpu.VMEM((SEQ, DH), f32),
            pltpu.VMEM((SEQ, DH), f32),
            pltpu.VMEM((8, DH), f32),
            pltpu.VMEM((query_rows, DH), bf16),
            pltpu.VMEM((query_rows, DH), f32),
        ],
    )
    work = blocks * query_rows * SEQ
    return pl.pallas_call(
        functools.partial(attention_kernel, first_head, head_step, blocks, rows_per_source),
        grid_spec=grid_spec,
        out_shape=[
            jax.ShapeDtypeStruct((SP, rows_per_source, DH), bf16),
            jax.ShapeDtypeStruct((SP, TOK, DH), bf16),
            jax.ShapeDtypeStruct((SP, TOK, DH), bf16),
            jax.ShapeDtypeStruct((2, DH), f32),
        ],
        compiler_params=pltpu.CompilerParams(vmem_limit_bytes=VMEM_LIMIT),
        cost_estimate=pl.CostEstimate(
            flops=10 * DH * work, bytes_accessed=4 * 2**20, transcendentals=work
        ),
        name=name,
    )(owner, field, field, field, field, field, gain_field)


def unpack_kernel(
    owner_ref, q_ref, k_ref, main_ref, share_ref, gq_ref, gk_ref, gv_ref, gain_ref, dq_sc, dk_sc
):
    for d in range(SP):
        cols = slice(d * DH, (d + 1) * DH)
        dq_sc[:, cols] = main_ref[d, :TOK]
        dk_sc[:, cols] = main_ref[d, TOK : 2 * TOK]
        gv_ref[0, :, cols] = main_ref[d, 2 * TOK : 3 * TOK]
    for g in range(EXTRA_HEADS):
        cols = slice((SP + g) * DH, (SP + g + 1) * DH)
        members = range(g * GROUP, (g + 1) * GROUP)
        dk_sc[:, cols] = sum(share_ref[d, :TOK].astype(f32) for d in members).astype(bf16)
        gv_ref[0, :, cols] = sum(
            share_ref[d, TOK : 2 * TOK].astype(f32) for d in members
        ).astype(bf16)
        for r, d in enumerate(members):
            dq_sc[r * QTOK : (r + 1) * QTOK, cols] = share_ref[d, 2 * TOK : 2 * TOK + QTOK]
    for raw_ref, grad_sc, out_ref in ((q_ref, dq_sc, gq_ref), (k_ref, dk_sc, gk_ref)):
        raw = raw_ref[0].astype(f32)
        grad = grad_sc[...].astype(f32)
        scale = row_scale(raw)
        inner = jnp.sum(grad * raw, axis=-1, keepdims=True)
        out_ref[0] = (scale * grad - (scale * scale * scale * (1.0 / INNER) * inner) * raw).astype(bf16)
    me = lax.axis_index("sp")
    sums = [jnp.zeros((2, DH), f32) for _ in range(2)]
    at = 2 * TOK + QTOK
    for head in range(HEADS):
        owner, slot = owner_slot(owner_ref, head)
        members = [(head, 0)] if head < SP else [
            (d, 1) for d in range((head - SP) * GROUP, (head - SP + 1) * GROUP)
        ]
        value = jnp.zeros((2, DH), f32)
        for d, kind in members:
            rows = share_ref[d, at : at + 32].astype(f32)
            base = kind * 6
            value += jnp.concatenate(
                [
                    rows[base + 3 * w : base + 3 * w + 1]
                    + rows[base + 3 * w + 1 : base + 3 * w + 2]
                    + rows[base + 3 * w + 2 : base + 3 * w + 3]
                    for w in range(2)
                ],
                axis=0,
            )
        for s in range(2):
            sums[s] = sums[s] + jnp.where((owner == me) & (slot == s), value, 0.0)
    factor = 1.0 / math.sqrt(SP * SEQ)
    for s in range(2):
        gain_ref[0, s] = sums[s] * factor


def unpack(owner, q, k, main_back, share_back):
    vmem = pl.BlockSpec(memory_space=pltpu.VMEM)
    return pl.pallas_call(
        unpack_kernel,
        in_specs=[pl.BlockSpec(memory_space=pltpu.SMEM), vmem, vmem, vmem, vmem],
        out_specs=[vmem, vmem, vmem, vmem],
        out_shape=[
            jax.ShapeDtypeStruct((1, TOK, INNER), bf16),
            jax.ShapeDtypeStruct((1, TOK, INNER), bf16),
            jax.ShapeDtypeStruct((1, TOK, INNER), bf16),
            jax.ShapeDtypeStruct((1, 2, 2, DH), f32),
        ],
        scratch_shapes=[pltpu.VMEM((TOK, INNER), bf16), pltpu.VMEM((TOK, INNER), bf16)],
        compiler_params=pltpu.CompilerParams(vmem_limit_bytes=VMEM_LIMIT),
        name="unpack",
    )(owner, q, k, main_back, share_back)


def join_kernel(dk_ref, dv_ref, dq_ref, sum_ref, out_ref):
    rows = []
    for i in range(4):
        rows += [*split3(sum_ref[i : i + 1])]
    extra = stack_rows(rows, 32)
    for d in range(SP):
        out_ref[d, :TOK] = dk_ref[d]
        out_ref[d, TOK : 2 * TOK] = dv_ref[d]
        out_ref[d, 2 * TOK : 2 * TOK + QTOK] = dq_ref[d]
        out_ref[d, 2 * TOK + QTOK :] = extra


def exchange(field):
    return lax.all_to_all(field, "sp", split_axis=0, concat_axis=0, tiled=True)


def per_device(query_raw, key_raw, value_in, grad_out, norm_gains, head_owner):
    main_send, share_send = pack(query_raw, key_raw, value_in, grad_out, norm_gains)
    main = exchange(main_send)
    share = exchange(share_send)
    dq, dk, dv, part = attention(
        "main_heads", head_owner, main, main, TOK,
        [("q", TOK), ("k", TOK), ("v", TOK), ("do", TOK)], 32, 2, 0, 1,
    )
    dq_s, dk_s, dv_s, part_s = attention(
        "shared_heads", head_owner, share, main, QTOK,
        [("k", TOK), ("v", TOK), ("q", QTOK), ("do", QTOK)], 16, 1, SP, GROUP,
    )
    gain_sums = lax.psum(jnp.concatenate([part, part_s], axis=0), "fsdp")
    main_back = exchange(jnp.concatenate([dq, dk, dv], axis=1))
    share_out = pl.pallas_call(
        join_kernel,
        out_shape=jax.ShapeDtypeStruct((SP, SHARE_BACK, DH), bf16),
        name="join_shared",
    )(dk_s, dv_s, dq_s, gain_sums)
    share_back = exchange(share_out)
    return tuple(unpack(head_owner, query_raw, key_raw, main_back, share_back))


def solution(mesh):
    return jax.shard_map(
        per_device,
        mesh=mesh,
        in_specs=(
            P("fsdp", "sp", None),
            P("fsdp", "sp", None),
            P("fsdp", "sp", None),
            P("fsdp", "sp", None),
            P("sp", None, None, None),
            P(),
        ),
        out_specs=(
            P("fsdp", "sp", None),
            P("fsdp", "sp", None),
            P("fsdp", "sp", None),
            P("sp", None, None, None),
        ),
        check_vma=False,
    )
```

```python
import functools
import math

import jax
import jax.numpy as jnp
from jax import lax
from jax.experimental import pallas as pl
from jax.experimental.pallas import tpu as pltpu
from jax.sharding import PartitionSpec as P

EPSILON = 1e-06
LOG2E = math.log2(math.e)
f32 = jnp.float32
bf16 = jnp.bfloat16

HEADS = 20
DH = 128
INNER = HEADS * DH
SP = 16
TOK = 128
SEQ = SP * TOK
EXTRA_HEADS = HEADS - SP
GROUP = SP // EXTRA_HEADS
QTOK = TOK // GROUP
MAIN_ROWS = 4 * TOK + 32
SHARE_ROWS = 2 * TOK + 2 * QTOK + 16
MAIN_BACK = 3 * TOK
SHARE_BACK = 2 * TOK + QTOK + 32
VMEM_LIMIT = 60 * 2**20


def split3(x):
    hi = x.astype(bf16).astype(f32)
    mid = (x - hi).astype(bf16).astype(f32)
    return hi, mid, x - hi - mid


def stack_rows(rows, count):
    width = rows[0].shape[-1]
    return jnp.concatenate(
        rows + [jnp.zeros((count - len(rows), width), f32)], axis=0
    ).astype(bf16)


def contract(a, b, da, db):
    return lax.dot_general(a, b, (((da,), (db,)), ((), ())), preferred_element_type=f32)


def row_scale(raw):
    return lax.rsqrt(jnp.sum(raw * raw, axis=-1, keepdims=True) * (1.0 / INNER) + EPSILON)


def to_row(column):
    return jnp.broadcast_to(column, (TOK, TOK)).T[0:1]


def pack_kernel(
    q_hbm, k_hbm, v_hbm, do_hbm, gain_hbm, main_ref, share_ref, q_ref, k_ref, v_ref, do_ref, gain_ref, sems
):
    pairs = (
        (q_hbm, q_ref), (k_hbm, k_ref), (gain_hbm, gain_ref), (v_hbm, v_ref), (do_hbm, do_ref),
    )
    copies = [
        pltpu.make_async_copy(src, dst, sems.at[i]) for i, (src, dst) in enumerate(pairs)
    ]
    for copy in copies:
        copy.start()
    for copy in copies:
        copy.wait()
    q_row = to_row(row_scale(q_ref[0].astype(f32)))
    k_row = to_row(row_scale(k_ref[0].astype(f32)))
    gains = gain_ref[0]
    rows = [*split3(q_row), *split3(k_row)]
    for slot in range(2):
        for which in range(2):
            rows += [*split3(gains[slot, which : which + 1])]
    extra = stack_rows(rows, 32)
    for d in range(SP):
        cols = slice(d * DH, (d + 1) * DH)
        for part, ref in enumerate((q_ref, k_ref, v_ref, do_ref)):
            main_ref[d, part * TOK : (part + 1) * TOK] = ref[0, :, cols]
        main_ref[d, 4 * TOK :] = extra
        head = SP + d // GROUP
        cols = slice(head * DH, (head + 1) * DH)
        quarter = slice(d % GROUP * QTOK, (d % GROUP + 1) * QTOK)
        share_ref[d, :TOK] = k_ref[0, :, cols]
        share_ref[d, TOK : 2 * TOK] = v_ref[0, :, cols]
        share_ref[d, 2 * TOK : 2 * TOK + QTOK] = q_ref[0, quarter, cols]
        share_ref[d, 2 * TOK + QTOK : 2 * TOK + 2 * QTOK] = do_ref[0, quarter, cols]
        q_own = jnp.concatenate([q_row[:, quarter]] * GROUP, axis=1)
        share_ref[d, 2 * TOK + 2 * QTOK :] = stack_rows([*split3(q_own), *split3(k_row)], 16)


def pack(q, k, v, do, gains):
    return pl.pallas_call(
        pack_kernel,
        in_specs=[pl.BlockSpec(memory_space=pltpu.HBM)] * 5,
        scratch_shapes=[pltpu.VMEM((1, TOK, INNER), bf16)] * 4
        + [pltpu.VMEM((1, 2, 2, DH), f32), pltpu.SemaphoreType.DMA((5,))],
        out_shape=[
            jax.ShapeDtypeStruct((SP, MAIN_ROWS, DH), bf16),
            jax.ShapeDtypeStruct((SP, SHARE_ROWS, DH), bf16),
        ],
        compiler_params=pltpu.CompilerParams(vmem_limit_bytes=VMEM_LIMIT),
        name="pack",
    )(q, k, v, do, gains)


def owner_slot(owner_ref, head):
    owner = owner_ref[head]
    slot = jnp.int32(0)
    for other in range(HEADS):
        same = (owner_ref[other] == owner) & (other < head)
        slot = slot + same.astype(jnp.int32)
    return owner, slot


def picked_gains(owner_ref, gain_ref, head):
    owner, slot = owner_slot(owner_ref, head)
    rows = gain_ref[owner].astype(f32)
    sums = []
    for which in range(2):
        both = []
        for s in range(2):
            at = 6 + (s * 2 + which) * 3
            both.append(rows[at : at + 1] + rows[at + 1 : at + 2] + rows[at + 2 : at + 3])
        sums.append(jnp.where(slot == 0, both[0], both[1]))
    return sums


def scale_columns(scale_ref, at):
    rows = scale_ref[...].astype(f32)
    return (rows[:, at] + rows[:, at + 1] + rows[:, at + 2]).T


def attention_kernel(
    first_head,
    head_step,
    blocks,
    rows_per_source,
    owner_ref,
    q_ref,
    k_ref,
    v_ref,
    do_ref,
    scale_ref,
    gain_ref,
    *rest,
):
    back_ref, part_ref = rest[:2]
    scratch = rest[2:]
    s_sc, dp_sc, kn_sc, dk_acc, dv_acc, qg_acc, qn_sc, qu_sc = scratch
    step = pl.program_id(0)
    chunk = 256
    chunks = SEQ // chunk
    head = first_head + lax.axis_index("sp") // head_step
    gain_q, gain_k = picked_gains(owner_ref, gain_ref, head)
    sources = q_ref.shape[0]
    query_rows = sources * rows_per_source
    score_scale = DH**-0.5

    q_cols = scale_columns(scale_ref, 0)
    k_cols = scale_columns(scale_ref, 3)

    @pl.when(step == 0)
    def _():
        for j in range(SP):
            r = slice(j * TOK, (j + 1) * TOK)
            kn_sc[r] = (k_ref[j].astype(f32) * k_cols[:, j : j + 1] * gain_k).astype(bf16)
        qg_acc[...] = jnp.zeros_like(qg_acc)

    for b in range(blocks):

        @pl.when(step == b)
        def _():
            for j in range(sources):
                r = slice(j * rows_per_source, (j + 1) * rows_per_source)
                col = q_cols[:rows_per_source, b * sources + j : b * sources + j + 1]
                unit = q_ref[j].astype(f32) * col
                qu_sc[r] = unit
                qn_sc[r] = (unit * gain_q).astype(bf16)

    qn = qn_sc[...]
    do = do_ref[...].reshape(query_rows, DH)
    top = None
    for c in range(chunks):
        r = slice(c * chunk, (c + 1) * chunk)
        s = contract(kn_sc[r], qn, 1, 1)
        s_sc[r] = s
        part = jnp.max(s.reshape(chunk // 8, 8, query_rows), axis=0)
        top = part if top is None else jnp.maximum(top, part)
    top = jnp.max(top, axis=0, keepdims=True) * (score_scale * LOG2E)
    total = delta = None
    for c in range(chunks):
        r = slice(c * chunk, (c + 1) * chunk)
        vc = v_ref[c * 2 : (c + 1) * 2].reshape(chunk, DH)
        dp = contract(vc, do, 1, 1)
        e = jnp.exp2(s_sc[r] * (score_scale * LOG2E) - top)
        s_sc[r] = e
        dp_sc[r] = dp
        e_part = jnp.sum(e.reshape(chunk // 8, 8, query_rows), axis=0)
        d_part = jnp.sum((e * dp).reshape(chunk // 8, 8, query_rows), axis=0)
        total = e_part if total is None else total + e_part
        delta = d_part if delta is None else delta + d_part
    inv = 1.0 / jnp.sum(total, axis=0, keepdims=True)
    delta = jnp.sum(delta, axis=0, keepdims=True) * inv
    dq = None
    for c in range(chunks):
        r = slice(c * chunk, (c + 1) * chunk)
        p = s_sc[r] * inv
        ds = (p * (dp_sc[r] - delta) * score_scale).astype(bf16)
        dv_part = contract(p.astype(bf16), do, 1, 0)
        dk_part = contract(ds, qn, 1, 0)
        if blocks == 1:
            dv_acc[r] = dv_part
            dk_acc[r] = dk_part
        else:

            @pl.when(step == 0)
            def _():
                dv_acc[r] = dv_part
                dk_acc[r] = dk_part

            @pl.when(step > 0)
            def _():
                dv_acc[r] += dv_part
                dk_acc[r] += dk_part

        dq_part = contract(ds, kn_sc[r], 0, 0)
        dq = dq_part if dq is None else dq + dq_part
    back_ref[pl.ds(step * sources, sources), 2 * TOK : 2 * TOK + rows_per_source] = (
        (dq * gain_q).astype(bf16).reshape(sources, rows_per_source, DH)
    )
    qg_acc[...] += jnp.sum((dq * qu_sc[...]).reshape(query_rows // 8, 8, DH), axis=0)

    @pl.when(step == blocks - 1)
    def _():
        key_part = jnp.zeros((8, DH), f32)
        for j in range(SP):
            r = slice(j * TOK, (j + 1) * TOK)
            dk = dk_acc[r]
            unit = k_ref[j].astype(f32) * k_cols[:, j : j + 1]
            key_part += jnp.sum((dk * unit).reshape(TOK // 8, 8, DH), axis=0)
            back_ref[j, :TOK] = (dk * gain_k).astype(bf16)
            back_ref[j, TOK : 2 * TOK] = dv_acc[r].astype(bf16)
        part_ref[0:1] = jnp.sum(qg_acc[...], axis=0, keepdims=True)
        part_ref[1:2] = jnp.sum(key_part, axis=0, keepdims=True)


def attention(name, owner, field, gain_field, rows_per_source, order, extra_rows, blocks, first_head, head_step, back_rows):
    sources = SP // blocks
    query_rows = sources * rows_per_source
    starts = {}
    at = 0
    for key, rows in order:
        starts[key] = (at, rows)
        at += rows

    def whole(key):
        start, rows = starts[key]
        return pl.BlockSpec((SP, rows, DH), lambda i, o: (0, start // rows, 0))

    def sliced(key):
        start, rows = starts[key]
        return pl.BlockSpec((sources, rows, DH), lambda i, o: (i, start // rows, 0))

    extra = pl.BlockSpec((SP, extra_rows, DH), lambda i, o: (0, at // extra_rows, 0))
    gains = pl.BlockSpec((SP, 32, DH), lambda i, o: (0, 4 * TOK // 32, 0))
    back = pl.BlockSpec((SP, back_rows, DH), lambda i, o: (0, 0, 0))
    grid_spec = pltpu.PrefetchScalarGridSpec(
        num_scalar_prefetch=1,
        grid=(blocks,),
        in_specs=[sliced("q"), whole("k"), whole("v"), sliced("do"), extra, gains],
        out_specs=[back, pl.BlockSpec((2, DH), lambda i, o: (0, 0))],
        scratch_shapes=[
            pltpu.VMEM((SEQ, query_rows), f32),
            pltpu.VMEM((SEQ, query_rows), f32),
            pltpu.VMEM((SEQ, DH), bf16),
            pltpu.VMEM((SEQ, DH), f32),
            pltpu.VMEM((SEQ, DH), f32),
            pltpu.VMEM((8, DH), f32),
            pltpu.VMEM((query_rows, DH), bf16),
            pltpu.VMEM((query_rows, DH), f32),
        ],
    )
    work = blocks * query_rows * SEQ
    return pl.pallas_call(
        functools.partial(attention_kernel, first_head, head_step, blocks, rows_per_source),
        grid_spec=grid_spec,
        out_shape=[
            jax.ShapeDtypeStruct((SP, back_rows, DH), bf16),
            jax.ShapeDtypeStruct((2, DH), f32),
        ],
        compiler_params=pltpu.CompilerParams(vmem_limit_bytes=VMEM_LIMIT),
        cost_estimate=pl.CostEstimate(
            flops=10 * DH * work, bytes_accessed=4 * 2**20, transcendentals=work
        ),
        name=name,
    )(owner, field, field, field, field, field, gain_field)


def unpack_kernel(
    owner_ref, q_ref, k_ref, main_ref, share_ref, gq_ref, gk_ref, gv_ref, gain_ref, dq_sc, dk_sc
):
    for d in range(SP):
        cols = slice(d * DH, (d + 1) * DH)
        dk_sc[:, cols] = main_ref[d, :TOK]
        gv_ref[0, :, cols] = main_ref[d, TOK : 2 * TOK]
        dq_sc[:, cols] = main_ref[d, 2 * TOK : 3 * TOK]
    for g in range(EXTRA_HEADS):
        cols = slice((SP + g) * DH, (SP + g + 1) * DH)
        members = range(g * GROUP, (g + 1) * GROUP)
        dk_sc[:, cols] = sum(share_ref[d, :TOK].astype(f32) for d in members).astype(bf16)
        gv_ref[0, :, cols] = sum(
            share_ref[d, TOK : 2 * TOK].astype(f32) for d in members
        ).astype(bf16)
        for r, d in enumerate(members):
            dq_sc[r * QTOK : (r + 1) * QTOK, cols] = share_ref[d, 2 * TOK : 2 * TOK + QTOK]
    for raw_ref, grad_sc, out_ref in ((q_ref, dq_sc, gq_ref), (k_ref, dk_sc, gk_ref)):
        raw = raw_ref[0].astype(f32)
        grad = grad_sc[...].astype(f32)
        scale = row_scale(raw)
        inner = jnp.sum(grad * raw, axis=-1, keepdims=True)
        out_ref[0] = (scale * grad - (scale * scale * scale * (1.0 / INNER) * inner) * raw).astype(bf16)
    me = lax.axis_index("sp")
    sums = [jnp.zeros((2, DH), f32) for _ in range(2)]
    at = 2 * TOK + QTOK
    for head in range(HEADS):
        owner, slot = owner_slot(owner_ref, head)
        members = [(head, 0)] if head < SP else [
            (d, 1) for d in range((head - SP) * GROUP, (head - SP + 1) * GROUP)
        ]
        value = jnp.zeros((2, DH), f32)
        for d, kind in members:
            rows = share_ref[d, at : at + 32].astype(f32)
            base = kind * 6
            value += jnp.concatenate(
                [
                    rows[base + 3 * w : base + 3 * w + 1]
                    + rows[base + 3 * w + 1 : base + 3 * w + 2]
                    + rows[base + 3 * w + 2 : base + 3 * w + 3]
                    for w in range(2)
                ],
                axis=0,
            )
        for s in range(2):
            sums[s] = sums[s] + jnp.where((owner == me) & (slot == s), value, 0.0)
    factor = 1.0 / math.sqrt(SP * SEQ)
    for s in range(2):
        gain_ref[0, s] = sums[s] * factor


def unpack(owner, q, k, main_back, share_back):
    vmem = pl.BlockSpec(memory_space=pltpu.VMEM)
    return pl.pallas_call(
        unpack_kernel,
        in_specs=[pl.BlockSpec(memory_space=pltpu.SMEM), vmem, vmem, vmem, vmem],
        out_specs=[vmem, vmem, vmem, vmem],
        out_shape=[
            jax.ShapeDtypeStruct((1, TOK, INNER), bf16),
            jax.ShapeDtypeStruct((1, TOK, INNER), bf16),
            jax.ShapeDtypeStruct((1, TOK, INNER), bf16),
            jax.ShapeDtypeStruct((1, 2, 2, DH), f32),
        ],
        scratch_shapes=[pltpu.VMEM((TOK, INNER), bf16), pltpu.VMEM((TOK, INNER), bf16)],
        compiler_params=pltpu.CompilerParams(vmem_limit_bytes=VMEM_LIMIT),
        name="unpack",
    )(owner, q, k, main_back, share_back)


def add_sums_kernel(sum_ref, share_ref, after_ref, out_ref):
    rows = []
    for i in range(4):
        rows += [*split3(sum_ref[i : i + 1])]
    extra = stack_rows(rows, 32)
    for d in range(SP):
        out_ref[d] = extra


def add_sums(sums, share_back, after):
    anywhere = pl.BlockSpec(memory_space=pl.ANY)
    last = (2 * TOK + QTOK) // 32
    return pl.pallas_call(
        add_sums_kernel,
        grid=(1,),
        in_specs=[pl.BlockSpec((4, DH), lambda i: (0, 0)), anywhere, anywhere],
        out_specs=pl.BlockSpec((SP, 32, DH), lambda i: (0, last, 0)),
        out_shape=jax.ShapeDtypeStruct((SP, SHARE_BACK, DH), bf16),
        input_output_aliases={1: 0},
        name="add_sums",
    )(sums, share_back, after)


def fsdp_sum(x):
    for bit in (1, 8, 4, 2):
        x = x + lax.ppermute(x, "fsdp", [(i, i ^ bit) for i in range(16)])
    return x


def exchange(field):
    return lax.all_to_all(field, "sp", split_axis=0, concat_axis=0, tiled=True)


def per_device(query_raw, key_raw, value_in, grad_out, norm_gains, head_owner):
    main_send, share_send = pack(query_raw, key_raw, value_in, grad_out, norm_gains)
    main = exchange(main_send)
    share = exchange(share_send)
    main_out, part = attention(
        "main_heads", head_owner, main, main, TOK,
        [("q", TOK), ("k", TOK), ("v", TOK), ("do", TOK)], 32, 2, 0, 1, MAIN_BACK,
    )
    share_out, part_s = attention(
        "shared_heads", head_owner, share, main, QTOK,
        [("k", TOK), ("v", TOK), ("q", QTOK), ("do", QTOK)], 16, 1, SP, GROUP, SHARE_BACK,
    )
    main_back = exchange(main_out)
    sums = fsdp_sum(jnp.concatenate([part, part_s], axis=0))
    share_back = exchange(add_sums(sums, share_out, main_back))
    return tuple(unpack(head_owner, query_raw, key_raw, main_back, share_back))


def solution(mesh):
    return jax.shard_map(
        per_device,
        mesh=mesh,
        in_specs=(
            P("fsdp", "sp", None),
            P("fsdp", "sp", None),
            P("fsdp", "sp", None),
            P("fsdp", "sp", None),
            P("sp", None, None, None),
            P(),
        ),
        out_specs=(
            P("fsdp", "sp", None),
            P("fsdp", "sp", None),
            P("fsdp", "sp", None),
            P("sp", None, None, None),
        ),
        check_vma=False,
    )
```

```python
import functools
import math

import jax
import jax.numpy as jnp
from jax import lax
from jax.experimental import pallas as pl
from jax.experimental.pallas import tpu as pltpu
from jax.sharding import PartitionSpec as P

EPSILON = 1e-06
LOG2E = math.log2(math.e)
f32 = jnp.float32
bf16 = jnp.bfloat16

HEADS = 20
DH = 128
INNER = HEADS * DH
SP = 16
TOK = 128
SEQ = SP * TOK
EXTRA_HEADS = HEADS - SP
HALF = SP // 2
QHALF = TOK // 2
QTOK = TOK // 4
MAIN_ROWS = 4 * TOK + 32
SHARE_ROWS = TOK + QHALF + 16
MAIN_BACK = 3 * TOK
SHARE_BACK = TOK + QTOK + 16
MIB = 2**20
SCORE_SCALE = DH**-0.5
SAFE = 60.0
CHUNK = 256


def core_index():
    return lax.rem(lax.axis_index("fsdp"), 2)


def split3(x):
    hi = x.astype(bf16).astype(f32)
    mid = (x - hi).astype(bf16).astype(f32)
    return hi, mid, x - hi - mid


def stack_rows(rows, count):
    width = rows[0].shape[-1]
    return jnp.concatenate(
        rows + [jnp.zeros((count - len(rows), width), f32)], axis=0
    ).astype(bf16)


def contract(a, b, da, db):
    return lax.dot_general(a, b, (((da,), (db,)), ((), ())), preferred_element_type=f32)


def row_scale(raw):
    return lax.rsqrt(jnp.sum(raw * raw, axis=-1, keepdims=True) * (1.0 / INNER) + EPSILON)


def to_row(column):
    return jnp.broadcast_to(column, (TOK, TOK)).T[0:1]


def pack_kernel(
    q_hbm, k_hbm, v_hbm, do_hbm, gain_hbm, main_ref, share_ref, give_ref,
    q_ref, k_ref, v_ref, do_ref, gain_ref, sems,
):
    pairs = (
        (q_hbm, q_ref), (k_hbm, k_ref), (gain_hbm, gain_ref), (v_hbm, v_ref), (do_hbm, do_ref),
    )
    copies = [
        pltpu.make_async_copy(src, dst, sems.at[i]) for i, (src, dst) in enumerate(pairs)
    ]
    for copy in copies:
        copy.start()
    for copy in copies:
        copy.wait()
    q_row = to_row(row_scale(q_ref[0].astype(f32)))
    k_row = to_row(row_scale(k_ref[0].astype(f32)))
    gains = gain_ref[0]
    rows = [*split3(q_row), *split3(k_row)]
    for slot in range(2):
        for which in range(2):
            rows += [*split3(gains[slot, which : which + 1])]
    extra = stack_rows(rows, 32)
    for d in range(SP):
        cols = slice(d * DH, (d + 1) * DH)
        for part, ref in enumerate((q_ref, k_ref, v_ref, do_ref)):
            main_ref[d, part * TOK : (part + 1) * TOK] = ref[0, :, cols]
        main_ref[d, 4 * TOK :] = extra
    core = core_index()

    def fill(out_ref, base, first_ref, second_ref, with_scales):
        for p in range(HALF):
            cols = slice((SP + p // 2) * DH, (SP + p // 2 + 1) * DH)
            half = slice(p % 2 * QHALF, (p % 2 + 1) * QHALF)
            out_ref[base + p, :TOK] = first_ref[0, :, cols]
            out_ref[base + p, TOK : TOK + QHALF] = second_ref[0, half, cols]
            if with_scales:
                q_own = jnp.concatenate([q_row[:, half]] * 2, axis=1)
                tail = stack_rows([*split3(q_own), *split3(k_row)], 16)
            else:
                tail = jnp.zeros((16, DH), bf16)
            out_ref[base + p, TOK + QHALF :] = tail

    @pl.when(core == 0)
    def _():
        fill(share_ref, 0, k_ref, q_ref, True)
        fill(give_ref, 0, v_ref, do_ref, False)

    @pl.when(core == 1)
    def _():
        fill(share_ref, HALF, v_ref, do_ref, False)
        fill(give_ref, 0, k_ref, q_ref, True)


def pack(q, k, v, do, gains):
    return pl.pallas_call(
        pack_kernel,
        in_specs=[pl.BlockSpec(memory_space=pltpu.HBM)] * 5,
        scratch_shapes=[pltpu.VMEM((1, TOK, INNER), bf16)] * 4
        + [pltpu.VMEM((1, 2, 2, DH), f32), pltpu.SemaphoreType.DMA((5,))],
        out_shape=[
            jax.ShapeDtypeStruct((SP, MAIN_ROWS, DH), bf16),
            jax.ShapeDtypeStruct((SP, SHARE_ROWS, DH), bf16),
            jax.ShapeDtypeStruct((HALF, SHARE_ROWS, DH), bf16),
        ],
        compiler_params=pltpu.CompilerParams(vmem_limit_bytes=60 * MIB),
        name="pack",
    )(q, k, v, do, gains)


def owner_slot(owner_ref, head):
    owner = owner_ref[head]
    slot = jnp.int32(0)
    for other in range(HEADS):
        same = (owner_ref[other] == owner) & (other < head)
        slot = slot + same.astype(jnp.int32)
    return owner, slot


def picked_gains(owner_ref, gain_ref, head):
    owner, slot = owner_slot(owner_ref, head)
    rows = gain_ref[owner].astype(f32)
    sums = []
    for which in range(2):
        both = []
        for s in range(2):
            at = 6 + (s * 2 + which) * 3
            both.append(rows[at : at + 1] + rows[at + 1 : at + 2] + rows[at + 2 : at + 3])
        sums.append(jnp.where(slot == 0, both[0], both[1]))
    return sums


def scale_columns(rows, at):
    return (rows[:, at] + rows[:, at + 1] + rows[:, at + 2]).T


def largest_square(x):
    return jnp.max(jnp.sum(x * x, axis=-1, keepdims=True))


def fold(x):
    return jnp.sum(x.reshape(x.shape[0] // 8, 8, x.shape[1]), axis=0)


def prepare_keys(key_at, k_cols, gain_k, kn_sc, kt_sc, bound_sm):
    most = jnp.float32(0.0)
    for j in range(SP):
        r = slice(j * TOK, (j + 1) * TOK)
        normed = (key_at(j).astype(f32) * k_cols[:, j : j + 1] * gain_k).astype(bf16)
        kn_sc[r] = normed
        most = jnp.maximum(most, largest_square(normed.astype(f32)))
    bound_sm[0] = most
    kt_sc[...] = kn_sc[...].T


def soften(qn_sc, do, value_at, kn_sc, e_sc, dp_sc, stat_sc, bound_sm):
    qn = qn_sc[...]
    square = largest_square(qn.astype(f32)) * bound_sm[0]
    small = square * (SCORE_SCALE * SCORE_SCALE) <= SAFE * SAFE

    def run(top):
        total = delta = None
        for c in range(SEQ // CHUNK):
            r = slice(c * CHUNK, (c + 1) * CHUNK)
            s = contract(kn_sc[r], qn, 1, 1) * (SCORE_SCALE * LOG2E)
            e = jnp.exp2(s if top is None else s - top)
            e_sc[r] = e
            dp = contract(value_at(c), do, 1, 1)
            dp_sc[r] = dp
            total = fold(e) if total is None else total + fold(e)
            delta = fold(e * dp) if delta is None else delta + fold(e * dp)
        inv = 1.0 / jnp.sum(total, axis=0, keepdims=True)
        stat_sc[0:1] = inv
        stat_sc[1:2] = jnp.sum(delta, axis=0, keepdims=True) * inv

    @pl.when(small)
    def _():
        run(None)

    @pl.when(jnp.logical_not(small))
    def _():
        top = None
        for c in range(SEQ // CHUNK):
            r = slice(c * CHUNK, (c + 1) * CHUNK)
            s = contract(kn_sc[r], qn, 1, 1) * (SCORE_SCALE * LOG2E)
            part = jnp.max(s.reshape(CHUNK // 8, 8, s.shape[1]), axis=0)
            top = part if top is None else jnp.maximum(top, part)
        run(jnp.max(top, axis=0, keepdims=True))


def gradients(qn_sc, do, kt_sc, e_sc, dp_sc, stat_sc, store):
    qn = qn_sc[...]
    inv = stat_sc[0:1]
    delta = stat_sc[1:2]
    dq_t = None
    for c in range(SEQ // CHUNK):
        r = slice(c * CHUNK, (c + 1) * CHUNK)
        p = e_sc[r] * inv
        ds = (p * (dp_sc[r] - delta)).astype(bf16)
        store(r, contract(ds, qn, 1, 0), contract(p.astype(bf16), do, 1, 0))
        part = contract(kt_sc[:, r], ds, 1, 0)
        dq_t = part if dq_t is None else dq_t + part
    return dq_t.T * SCORE_SCALE


def attention_scratch(query_rows):
    return [
        pltpu.VMEM((SEQ, query_rows), f32),
        pltpu.VMEM((SEQ, query_rows), f32),
        pltpu.VMEM((8, query_rows), f32),
        pltpu.SMEM((1,), f32),
        pltpu.VMEM((SEQ, DH), bf16),
        pltpu.VMEM((DH, SEQ), bf16),
        pltpu.VMEM((SEQ, DH), f32),
        pltpu.VMEM((SEQ, DH), f32),
        pltpu.VMEM((query_rows, DH), bf16),
        pltpu.VMEM((query_rows, DH), f32),
    ]


def cost(query_rows):
    work = query_rows * SEQ
    return pl.CostEstimate(flops=10 * DH * work, bytes_accessed=4 * 2**20, transcendentals=work)


STEPS = 2


def main_kernel(
    owner_ref, field_ref, back_ref, part_ref, qg_acc,
    e_sc, dp_sc, stat_sc, bound_sm, kn_sc, kt_sc, dk_acc, dv_acc, qn_sc, qu_sc,
):
    sources = SP // STEPS
    rows = sources * TOK
    blocks = CHUNK // TOK
    gain_q, gain_k = picked_gains(owner_ref, field_ref.at[:, 4 * TOK :], lax.axis_index("sp"))
    scales = field_ref[:, 4 * TOK :].astype(f32)
    q_cols = scale_columns(scales, 0)
    k_cols = scale_columns(scales, 3)
    qg_acc[...] = jnp.zeros_like(qg_acc)

    def key_at(j):
        return field_ref[j, TOK : 2 * TOK]

    def value_at(c):
        return field_ref[c * blocks : (c + 1) * blocks, 2 * TOK : 3 * TOK].reshape(CHUNK, DH)

    prepare_keys(key_at, k_cols, gain_k, kn_sc, kt_sc, bound_sm)

    @pl.loop(0, STEPS)
    def _(step):
        for b in range(STEPS):

            @pl.when(step == b)
            def _():
                for j in range(sources):
                    at = b * sources + j
                    r = slice(j * TOK, (j + 1) * TOK)
                    unit = field_ref[at, :TOK].astype(f32) * q_cols[:, at : at + 1]
                    qu_sc[r] = unit
                    qn_sc[r] = (unit * gain_q).astype(bf16)

        mine = pl.ds(step * sources, sources)
        do = field_ref[mine, 3 * TOK : 4 * TOK].reshape(rows, DH)
        soften(qn_sc, do, value_at, kn_sc, e_sc, dp_sc, stat_sc, bound_sm)

        def store(r, dk_part, dv_part):
            @pl.when(step == 0)
            def _():
                dk_acc[r] = dk_part
                dv_acc[r] = dv_part

            @pl.when(step > 0)
            def _():
                dk_acc[r] += dk_part
                dv_acc[r] += dv_part

        dq = gradients(qn_sc, do, kt_sc, e_sc, dp_sc, stat_sc, store)
        back_ref[mine, 2 * TOK :] = (dq * gain_q).astype(bf16).reshape(sources, TOK, DH)
        qg_acc[...] += fold(dq * qu_sc[...])

    key_part = jnp.zeros((8, DH), f32)
    for j in range(SP):
        r = slice(j * TOK, (j + 1) * TOK)
        dk = dk_acc[r] * SCORE_SCALE
        key_part += fold(dk * (key_at(j).astype(f32) * k_cols[:, j : j + 1]))
        back_ref[j, :TOK] = (dk * gain_k).astype(bf16)
        back_ref[j, TOK : 2 * TOK] = dv_acc[r].astype(bf16)
    part_ref[0:1] = jnp.sum(qg_acc[...], axis=0, keepdims=True)
    part_ref[1:2] = jnp.sum(key_part, axis=0, keepdims=True)


def main_heads(owner, field):
    return pl.pallas_call(
        main_kernel,
        in_specs=[
            pl.BlockSpec(memory_space=pltpu.SMEM),
            pl.BlockSpec(memory_space=pltpu.VMEM),
        ],
        out_shape=[
            jax.ShapeDtypeStruct((SP, MAIN_BACK, DH), bf16),
            jax.ShapeDtypeStruct((2, DH), f32),
        ],
        scratch_shapes=[pltpu.VMEM((8, DH), f32)] + attention_scratch(SEQ // STEPS),
        compiler_params=pltpu.CompilerParams(vmem_limit_bytes=40 * MIB),
        cost_estimate=cost(SEQ),
        name="main_heads",
    )(owner, field)


def shared_kernel(
    owner_ref, extra_ref, mine_ref, other_ref, keep_ref, give_ref, part_ref,
    kq_ref, vd_ref, v_sc,
    e_sc, dp_sc, stat_sc, bound_sm, kn_sc, kt_sc, dk_acc, dv_acc, qn_sc, qu_sc,
):
    core = core_index()

    def load(kq_src, vd_src):
        kq_ref[...] = kq_src[...]
        vd_ref[...] = vd_src[...]

    @pl.when(core == 0)
    def _():
        load(mine_ref, other_ref)

    @pl.when(core == 1)
    def _():
        load(other_ref, mine_ref)

    head = SP + lax.rem(lax.axis_index("sp") // 2, EXTRA_HEADS)
    gain_q, gain_k = picked_gains(owner_ref, extra_ref, head)
    scales = kq_ref[:, TOK + QHALF :].astype(f32)
    q_cols = scale_columns(scales, 0)
    q_cols = jnp.where(core == 0, q_cols[:QTOK], q_cols[QTOK:QHALF])
    k_cols = scale_columns(scales, 3)
    prepare_keys(lambda j: kq_ref[j, :TOK], k_cols, gain_k, kn_sc, kt_sc, bound_sm)

    def quarter(ref):
        low = ref[:, TOK : TOK + QTOK]
        high = ref[:, TOK + QTOK : TOK + QHALF]
        return jnp.where(core == 0, low, high)

    q = quarter(kq_ref)
    do = quarter(vd_ref).reshape(SP * QTOK, DH)
    for j in range(SP):
        r = slice(j * QTOK, (j + 1) * QTOK)
        unit = q[j].astype(f32) * q_cols[:, j : j + 1]
        qu_sc[r] = unit
        qn_sc[r] = (unit * gain_q).astype(bf16)
        v_sc[j * TOK : (j + 1) * TOK] = vd_ref[j, :TOK]
    soften(qn_sc, do, lambda c: v_sc[c * CHUNK : (c + 1) * CHUNK], kn_sc, e_sc, dp_sc, stat_sc, bound_sm)

    def store(r, dk_part, dv_part):
        dk_acc[r] = dk_part
        dv_acc[r] = dv_part

    dq = gradients(qn_sc, do, kt_sc, e_sc, dp_sc, stat_sc, store)
    keep_ref[:, TOK : TOK + QTOK] = (dq * gain_q).astype(bf16).reshape(SP, QTOK, DH)
    keep_ref[:, TOK + QTOK :] = jnp.zeros((SP, 16, DH), bf16)
    key_part = jnp.zeros((8, DH), f32)
    for j in range(SP):
        r = slice(j * TOK, (j + 1) * TOK)
        dk = dk_acc[r] * SCORE_SCALE
        key_part += fold(dk * (kq_ref[j, :TOK].astype(f32) * k_cols[:, j : j + 1]))
        dk = (dk * gain_k).astype(bf16)
        dv = dv_acc[r].astype(bf16)

        keep_ref[j, :TOK] = jnp.where(core == 0, dk, dv)
        give_ref[j] = jnp.where(core == 0, dv, dk)
    part_ref[0:1] = jnp.sum(fold(dq * qu_sc[...]), axis=0, keepdims=True)
    part_ref[1:2] = jnp.sum(key_part, axis=0, keepdims=True)


def shared_heads(owner, extra, mine, other):
    vmem = pl.BlockSpec(memory_space=pltpu.VMEM)
    return pl.pallas_call(
        shared_kernel,
        in_specs=[
            pl.BlockSpec(memory_space=pltpu.SMEM),
            vmem,
            vmem,
            vmem,
        ],
        out_shape=[
            jax.ShapeDtypeStruct((SP, SHARE_BACK, DH), bf16),
            jax.ShapeDtypeStruct((SP, TOK, DH), bf16),
            jax.ShapeDtypeStruct((2, DH), f32),
        ],
        scratch_shapes=[
            pltpu.VMEM((SP, SHARE_ROWS, DH), bf16),
            pltpu.VMEM((SP, SHARE_ROWS, DH), bf16),
            pltpu.VMEM((SEQ, DH), bf16),
        ]
        + attention_scratch(SP * QTOK),
        compiler_params=pltpu.CompilerParams(vmem_limit_bytes=40 * MIB),
        cost_estimate=cost(SP * QTOK),
        name="shared_heads",
    )(owner, extra, mine, other)


def unpack_kernel(
    owner_ref, q_ref, k_ref, main_ref, share_ref, other_ref, gq_ref, gk_ref, gv_ref, gain_ref, dq_sc, dk_sc
):
    for d in range(SP):
        cols = slice(d * DH, (d + 1) * DH)
        dk_sc[:, cols] = main_ref[d, :TOK]
        gv_ref[0, :, cols] = main_ref[d, TOK : 2 * TOK]
        dq_sc[:, cols] = main_ref[d, 2 * TOK : 3 * TOK]
    core = core_index()

    def take(base, first_ref, second_ref):
        for g in range(EXTRA_HEADS):
            cols = slice((SP + g) * DH, (SP + g + 1) * DH)
            x = base + 2 * g

            def both(ref):
                return (ref[x, :TOK].astype(f32) + ref[x + 1, :TOK].astype(f32)).astype(bf16)

            dk_sc[:, cols] = both(first_ref)
            gv_ref[0, :, cols] = both(second_ref)
            for half in range(2):
                for c, ref in enumerate((first_ref, second_ref)):
                    at = (2 * half + c) * QTOK
                    dq_sc[at : at + QTOK, cols] = ref[x + half, TOK : TOK + QTOK]

    @pl.when(core == 0)
    def _():
        take(0, share_ref, other_ref)

    @pl.when(core == 1)
    def _():
        take(HALF, other_ref, share_ref)

    for raw_ref, grad_sc, out_ref in ((q_ref, dq_sc, gq_ref), (k_ref, dk_sc, gk_ref)):
        raw = raw_ref[0].astype(f32)
        grad = grad_sc[...].astype(f32)
        scale = row_scale(raw)
        inner = jnp.sum(grad * raw, axis=-1, keepdims=True)
        out_ref[0] = (scale * grad - (scale * scale * scale * (1.0 / INNER) * inner) * raw).astype(bf16)
    me = lax.axis_index("sp")
    sums = [jnp.zeros((2, DH), f32) for _ in range(2)]
    at = TOK + QTOK
    for head in range(HEADS):
        owner, slot = owner_slot(owner_ref, head)
        members = [(head, 0)] if head < SP else [
            (2 * (head - SP) + d, 1) for d in (0, 1, HALF, HALF + 1)
        ]
        value = jnp.zeros((2, DH), f32)
        for d, kind in members:
            rows = share_ref[d, at : at + 16].astype(f32)
            base = kind * 6
            value += jnp.concatenate(
                [
                    rows[base + 3 * w : base + 3 * w + 1]
                    + rows[base + 3 * w + 1 : base + 3 * w + 2]
                    + rows[base + 3 * w + 2 : base + 3 * w + 3]
                    for w in range(2)
                ],
                axis=0,
            )
        for s in range(2):
            sums[s] = sums[s] + jnp.where((owner == me) & (slot == s), value, 0.0)
    factor = 1.0 / math.sqrt(SP * SEQ)
    for s in range(2):
        gain_ref[0, s] = sums[s] * factor


def unpack(owner, q, k, main_back, share_back, other_back):
    vmem = pl.BlockSpec(memory_space=pltpu.VMEM)
    return pl.pallas_call(
        unpack_kernel,
        in_specs=[pl.BlockSpec(memory_space=pltpu.SMEM), vmem, vmem, vmem, vmem, vmem],
        out_specs=[vmem, vmem, vmem, vmem],
        out_shape=[
            jax.ShapeDtypeStruct((1, TOK, INNER), bf16),
            jax.ShapeDtypeStruct((1, TOK, INNER), bf16),
            jax.ShapeDtypeStruct((1, TOK, INNER), bf16),
            jax.ShapeDtypeStruct((1, 2, 2, DH), f32),
        ],
        scratch_shapes=[pltpu.VMEM((TOK, INNER), bf16), pltpu.VMEM((TOK, INNER), bf16)],
        compiler_params=pltpu.CompilerParams(vmem_limit_bytes=40 * MIB),
        name="unpack",
    )(owner, q, k, main_back, share_back, other_back)


def add_sums_kernel(sum_ref, keep_ref, got_ref, after_ref, out_ref):
    rows = []
    for i in range(4):
        rows += [*split3(sum_ref[i : i + 1])]
    extra = stack_rows(rows, 16)
    for d in range(SP):
        total = keep_ref[d, :TOK].astype(f32) + got_ref[d].astype(f32)
        out_ref[d, :TOK] = total.astype(bf16)
        out_ref[d, TOK : TOK + QTOK] = keep_ref[d, TOK : TOK + QTOK]
        out_ref[d, TOK + QTOK :] = extra


def add_sums(sums, keep, got, after):
    vmem = pl.BlockSpec(memory_space=pltpu.VMEM)
    return pl.pallas_call(
        add_sums_kernel,
        in_specs=[vmem, vmem, vmem, pl.BlockSpec(memory_space=pl.ANY)],
        out_shape=jax.ShapeDtypeStruct((SP, SHARE_BACK, DH), bf16),
        compiler_params=pltpu.CompilerParams(vmem_limit_bytes=40 * MIB),
        name="add_sums",
    )(sums, keep, got, after)


def fsdp_sum(x):
    for bit in (1, 8, 4, 2):
        x = x + lax.ppermute(x, "fsdp", [(i, i ^ bit) for i in range(16)])
    return x


def gate_kernel(main_ref, x_ref, extra_ref, out_ref):
    extra_ref[...] = main_ref[:, 4 * TOK :]


def gate(main, x):
    anywhere = pl.BlockSpec(memory_space=pl.ANY)
    vmem = pl.BlockSpec(memory_space=pltpu.VMEM)
    return pl.pallas_call(
        gate_kernel,
        in_specs=[vmem, anywhere],
        out_specs=[vmem, anywhere],
        out_shape=[
            jax.ShapeDtypeStruct((SP, 32, DH), bf16),
            jax.ShapeDtypeStruct(x.shape, x.dtype),
        ],
        input_output_aliases={1: 1},
        compiler_params=pltpu.CompilerParams(vmem_limit_bytes=40 * MIB),
        name="gate",
    )(main, x)


def after_kernel(x_ref, before_ref, out_ref):
    pass


def after(x, before):
    anywhere = pl.BlockSpec(memory_space=pl.ANY)
    return pl.pallas_call(
        after_kernel,
        in_specs=[anywhere, anywhere],
        out_specs=anywhere,
        out_shape=jax.ShapeDtypeStruct(x.shape, x.dtype),
        input_output_aliases={0: 0},
        compiler_params=pltpu.CompilerParams(vmem_limit_bytes=40 * MIB),
        name="after",
    )(x, before)


def swap(x):
    return lax.ppermute(x, "fsdp", [(i, i ^ 1) for i in range(16)])


def exchange(field):
    return lax.all_to_all(field, "sp", split_axis=0, concat_axis=0, tiled=True)


def per_device(query_raw, key_raw, value_in, grad_out, norm_gains, head_owner):
    main_send, share_half, give = pack(query_raw, key_raw, value_in, grad_out, norm_gains)
    main = exchange(main_send)
    other_half = (1 - core_index()) * HALF
    share_send = lax.dynamic_update_slice(share_half, swap(give), (other_half, 0, 0))
    extra, share_send = gate(main, share_send)
    share = exchange(share_send)
    main_out, part = main_heads(head_owner, main)
    main_back = exchange(main_out)
    share = after(share, part)
    keep, give_back, part_s = shared_heads(head_owner, extra, share, swap(share))
    sums = fsdp_sum(jnp.concatenate([part, part_s], axis=0))
    share_back = exchange(add_sums(sums, keep, swap(give_back), main_back[:1, :16]))
    return tuple(
        unpack(head_owner, query_raw, key_raw, main_back, share_back, swap(share_back))
    )


def solution(mesh):
    return jax.shard_map(
        per_device,
        mesh=mesh,
        in_specs=(
            P("fsdp", "sp", None),
            P("fsdp", "sp", None),
            P("fsdp", "sp", None),
            P("fsdp", "sp", None),
            P("sp", None, None, None),
            P(),
        ),
        out_specs=(
            P("fsdp", "sp", None),
            P("fsdp", "sp", None),
            P("fsdp", "sp", None),
            P("sp", None, None, None),
        ),
        check_vma=False,
    )
```

```python
import functools
import math

import jax
import jax.numpy as jnp
from jax import lax
from jax.experimental import pallas as pl
from jax.experimental.pallas import tpu as pltpu
from jax.sharding import PartitionSpec as P

EPSILON = 1e-06
LOG2E = math.log2(math.e)
f32 = jnp.float32
bf16 = jnp.bfloat16

HEADS = 20
DH = 128
INNER = HEADS * DH
SP = 16
TOK = 128
SEQ = SP * TOK
EXTRA_HEADS = HEADS - SP
HALF = SP // 2
QHALF = TOK // 2
QTOK = TOK // 4
MAIN_ROWS = 4 * TOK + 32
SHARE_ROWS = TOK + QHALF + 16
MAIN_BACK = 3 * TOK
SHARE_BACK = TOK + QTOK + 16
MIB = 2**20
SCORE_SCALE = DH**-0.5
SAFE = 60.0
CHUNK = 256


def core_index():
    return lax.rem(lax.axis_index("fsdp"), 2)


def split3(x):
    hi = x.astype(bf16).astype(f32)
    mid = (x - hi).astype(bf16).astype(f32)
    return hi, mid, x - hi - mid


def stack_rows(rows, count):
    width = rows[0].shape[-1]
    return jnp.concatenate(
        rows + [jnp.zeros((count - len(rows), width), f32)], axis=0
    ).astype(bf16)


def contract(a, b, da, db):
    return lax.dot_general(a, b, (((da,), (db,)), ((), ())), preferred_element_type=f32)


def row_scale(raw):
    return lax.rsqrt(jnp.sum(raw * raw, axis=-1, keepdims=True) * (1.0 / INNER) + EPSILON)


def to_row(column):
    return jnp.broadcast_to(column, (TOK, TOK)).T[0:1]


def pack_kernel(
    q_hbm, k_hbm, v_hbm, do_hbm, gain_hbm, main_ref, share_ref, give_ref,
    q_ref, k_ref, v_ref, do_ref, gain_ref, sems,
):
    pairs = (
        (q_hbm, q_ref), (k_hbm, k_ref), (gain_hbm, gain_ref), (v_hbm, v_ref), (do_hbm, do_ref),
    )
    copies = [
        pltpu.make_async_copy(src, dst, sems.at[i]) for i, (src, dst) in enumerate(pairs)
    ]
    for copy in copies:
        copy.start()
    for copy in copies:
        copy.wait()
    q_row = to_row(row_scale(q_ref[0].astype(f32)))
    k_row = to_row(row_scale(k_ref[0].astype(f32)))
    gains = gain_ref[0]
    rows = [*split3(q_row), *split3(k_row)]
    for slot in range(2):
        for which in range(2):
            rows += [*split3(gains[slot, which : which + 1])]
    extra = stack_rows(rows, 32)
    for d in range(SP):
        cols = slice(d * DH, (d + 1) * DH)
        for part, ref in enumerate((q_ref, k_ref, v_ref, do_ref)):
            main_ref[d, part * TOK : (part + 1) * TOK] = ref[0, :, cols]
        main_ref[d, 4 * TOK :] = extra
    core = core_index()

    def fill(out_ref, base, first_ref, second_ref, with_scales):
        for p in range(HALF):
            cols = slice((SP + p // 2) * DH, (SP + p // 2 + 1) * DH)
            half = slice(p % 2 * QHALF, (p % 2 + 1) * QHALF)
            out_ref[base + p, :TOK] = first_ref[0, :, cols]
            out_ref[base + p, TOK : TOK + QHALF] = second_ref[0, half, cols]
            if with_scales:
                q_own = jnp.concatenate([q_row[:, half]] * 2, axis=1)
                tail = stack_rows([*split3(q_own), *split3(k_row)], 16)
            else:
                tail = jnp.zeros((16, DH), bf16)
            out_ref[base + p, TOK + QHALF :] = tail

    @pl.when(core == 0)
    def _():
        fill(share_ref, 0, k_ref, q_ref, True)
        fill(give_ref, 0, v_ref, do_ref, False)

    @pl.when(core == 1)
    def _():
        fill(share_ref, HALF, v_ref, do_ref, False)
        fill(give_ref, 0, k_ref, q_ref, True)


def pack(q, k, v, do, gains):
    return pl.pallas_call(
        pack_kernel,
        in_specs=[pl.BlockSpec(memory_space=pltpu.HBM)] * 5,
        scratch_shapes=[pltpu.VMEM((1, TOK, INNER), bf16)] * 4
        + [pltpu.VMEM((1, 2, 2, DH), f32), pltpu.SemaphoreType.DMA((5,))],
        out_shape=[
            jax.ShapeDtypeStruct((SP, MAIN_ROWS, DH), bf16),
            jax.ShapeDtypeStruct((SP, SHARE_ROWS, DH), bf16),
            jax.ShapeDtypeStruct((HALF, SHARE_ROWS, DH), bf16),
        ],
        compiler_params=pltpu.CompilerParams(vmem_limit_bytes=60 * MIB),
        name="pack",
    )(q, k, v, do, gains)


def owner_slot(owner_ref, head):
    owner = owner_ref[head]
    slot = jnp.int32(0)
    for other in range(HEADS):
        same = (owner_ref[other] == owner) & (other < head)
        slot = slot + same.astype(jnp.int32)
    return owner, slot


def picked_gains(owner_ref, gain_ref, head):
    owner, slot = owner_slot(owner_ref, head)
    rows = gain_ref[owner].astype(f32)
    sums = []
    for which in range(2):
        both = []
        for s in range(2):
            at = 6 + (s * 2 + which) * 3
            both.append(rows[at : at + 1] + rows[at + 1 : at + 2] + rows[at + 2 : at + 3])
        sums.append(jnp.where(slot == 0, both[0], both[1]))
    return sums


def scale_columns(rows, at):
    return (rows[:, at] + rows[:, at + 1] + rows[:, at + 2]).T


def largest_square(x):
    return jnp.max(contract(jnp.ones((8, DH), bf16), x * x, 1, 1))


def fold(x):
    return jnp.sum(x.reshape(x.shape[0] // 8, 8, x.shape[1]), axis=0)


def prepare_keys(key_at, k_cols, gain_k, kn_sc, kt_sc, bound_sm):
    for j in range(SP):
        r = slice(j * TOK, (j + 1) * TOK)
        kn_sc[r] = (key_at(j).astype(f32) * k_cols[:, j : j + 1] * gain_k).astype(bf16)
    bound_sm[0] = largest_square(kn_sc[...])
    kt_sc[...] = kn_sc[...].T


def soften(qn_sc, do, value_at, kn_sc, e_sc, dp_sc, stat_sc, bound_sm):
    qn = qn_sc[...]
    square = largest_square(qn) * bound_sm[0]
    small = square * (SCORE_SCALE * SCORE_SCALE) <= SAFE * SAFE

    def run(top):
        total = delta = None
        for c in range(SEQ // CHUNK):
            r = slice(c * CHUNK, (c + 1) * CHUNK)
            s = contract(kn_sc[r], qn, 1, 1) * (SCORE_SCALE * LOG2E)
            e = jnp.exp2(s if top is None else s - top)
            e_sc[r] = e
            dp = contract(value_at(c), do, 1, 1)
            dp_sc[r] = dp
            total = fold(e) if total is None else total + fold(e)
            delta = fold(e * dp) if delta is None else delta + fold(e * dp)
        inv = 1.0 / jnp.sum(total, axis=0, keepdims=True)
        stat_sc[0:1] = inv
        stat_sc[1:2] = jnp.sum(delta, axis=0, keepdims=True) * inv

    @pl.when(small)
    def _():
        run(None)

    @pl.when(jnp.logical_not(small))
    def _():
        top = None
        for c in range(SEQ // CHUNK):
            r = slice(c * CHUNK, (c + 1) * CHUNK)
            s = contract(kn_sc[r], qn, 1, 1) * (SCORE_SCALE * LOG2E)
            part = jnp.max(s.reshape(CHUNK // 8, 8, s.shape[1]), axis=0)
            top = part if top is None else jnp.maximum(top, part)
        run(jnp.max(top, axis=0, keepdims=True))


def gradients(qn_sc, do, kt_sc, e_sc, dp_sc, stat_sc, store):
    qn = qn_sc[...]
    inv = stat_sc[0:1]
    delta = stat_sc[1:2]
    dq_t = None
    for c in range(SEQ // CHUNK):
        r = slice(c * CHUNK, (c + 1) * CHUNK)
        p = e_sc[r] * inv
        ds = (p * (dp_sc[r] - delta)).astype(bf16)
        store(r, contract(ds, qn, 1, 0), contract(p.astype(bf16), do, 1, 0))
        part = contract(kt_sc[:, r], ds, 1, 0)
        dq_t = part if dq_t is None else dq_t + part
    return dq_t.T * SCORE_SCALE


def attention_scratch(query_rows):
    return [
        pltpu.VMEM((SEQ, query_rows), f32),
        pltpu.VMEM((SEQ, query_rows), f32),
        pltpu.VMEM((8, query_rows), f32),
        pltpu.SMEM((1,), f32),
        pltpu.VMEM((SEQ, DH), bf16),
        pltpu.VMEM((DH, SEQ), bf16),
        pltpu.VMEM((SEQ, DH), f32),
        pltpu.VMEM((SEQ, DH), f32),
        pltpu.VMEM((query_rows, DH), bf16),
        pltpu.VMEM((query_rows, DH), f32),
    ]


def cost(query_rows):
    work = query_rows * SEQ
    return pl.CostEstimate(flops=10 * DH * work, bytes_accessed=4 * 2**20, transcendentals=work)


STEPS = 2


def main_kernel(
    owner_ref, field_ref, back_hbm, part_ref, back_ref, sems, qg_acc,
    e_sc, dp_sc, stat_sc, bound_sm, kn_sc, kt_sc, dk_acc, dv_acc, qn_sc, qu_sc,
):
    sources = SP // STEPS
    rows = sources * TOK
    blocks = CHUNK // TOK
    gain_q, gain_k = picked_gains(owner_ref, field_ref.at[:, 4 * TOK :], lax.axis_index("sp"))
    scales = field_ref[:, 4 * TOK :].astype(f32)
    q_cols = scale_columns(scales, 0)
    k_cols = scale_columns(scales, 3)
    qg_acc[...] = jnp.zeros_like(qg_acc)

    def key_at(j):
        return field_ref[j, TOK : 2 * TOK]

    def value_at(c):
        return field_ref[c * blocks : (c + 1) * blocks, 2 * TOK : 3 * TOK].reshape(CHUNK, DH)

    def query_copy(step):
        at = (pl.ds(step * sources, sources), pl.ds(2 * TOK, TOK))
        return pltpu.make_async_copy(back_ref.at[at], back_hbm.at[at], sems.at[step])

    def key_copy(j):
        at = (j, pl.ds(0, 2 * TOK))
        return pltpu.make_async_copy(back_ref.at[at], back_hbm.at[at], sems.at[STEPS + j])

    prepare_keys(key_at, k_cols, gain_k, kn_sc, kt_sc, bound_sm)
    dk_acc[...] = jnp.zeros_like(dk_acc)
    dv_acc[...] = jnp.zeros_like(dv_acc)

    @pl.loop(0, STEPS)
    def _(step):
        for b in range(STEPS):

            @pl.when(step == b)
            def _():
                for j in range(sources):
                    at = b * sources + j
                    r = slice(j * TOK, (j + 1) * TOK)
                    unit = field_ref[at, :TOK].astype(f32) * q_cols[:, at : at + 1]
                    qu_sc[r] = unit
                    qn_sc[r] = (unit * gain_q).astype(bf16)

        mine = pl.ds(step * sources, sources)
        do = field_ref[mine, 3 * TOK : 4 * TOK].reshape(rows, DH)
        soften(qn_sc, do, value_at, kn_sc, e_sc, dp_sc, stat_sc, bound_sm)

        def store(r, dk_part, dv_part):
            dk_acc[r] += dk_part
            dv_acc[r] += dv_part

        dq = gradients(qn_sc, do, kt_sc, e_sc, dp_sc, stat_sc, store)
        back_ref[mine, 2 * TOK :] = (dq * gain_q).astype(bf16).reshape(sources, TOK, DH)
        query_copy(step).start()
        qg_acc[...] += fold(dq * qu_sc[...])

    key_part = jnp.zeros((8, DH), f32)
    for j in range(SP):
        r = slice(j * TOK, (j + 1) * TOK)
        dk = dk_acc[r] * SCORE_SCALE
        key_part += fold(dk * (key_at(j).astype(f32) * k_cols[:, j : j + 1]))
        back_ref[j, :TOK] = (dk * gain_k).astype(bf16)
        back_ref[j, TOK : 2 * TOK] = dv_acc[r].astype(bf16)
        key_copy(j).start()
    part_ref[0:1] = jnp.sum(qg_acc[...], axis=0, keepdims=True)
    part_ref[1:2] = jnp.sum(key_part, axis=0, keepdims=True)
    for step in range(STEPS):
        query_copy(step).wait()
    for j in range(SP):
        key_copy(j).wait()


def main_heads(owner, field):
    return pl.pallas_call(
        main_kernel,
        in_specs=[
            pl.BlockSpec(memory_space=pltpu.SMEM),
            pl.BlockSpec(memory_space=pltpu.VMEM),
        ],
        out_shape=[
            jax.ShapeDtypeStruct((SP, MAIN_BACK, DH), bf16),
            jax.ShapeDtypeStruct((2, DH), f32),
        ],
        out_specs=[
            pl.BlockSpec(memory_space=pltpu.HBM),
            pl.BlockSpec(memory_space=pltpu.VMEM),
        ],
        scratch_shapes=[
            pltpu.VMEM((SP, MAIN_BACK, DH), bf16),
            pltpu.SemaphoreType.DMA((STEPS + SP,)),
            pltpu.VMEM((8, DH), f32),
        ]
        + attention_scratch(SEQ // STEPS),
        compiler_params=pltpu.CompilerParams(vmem_limit_bytes=40 * MIB),
        cost_estimate=cost(SEQ),
        name="main_heads",
    )(owner, field)


def shared_kernel(
    owner_ref, extra_ref, mine_ref, other_ref, keep_ref, give_ref, part_ref,
    kq_ref, vd_ref, v_sc,
    e_sc, dp_sc, stat_sc, bound_sm, kn_sc, kt_sc, dk_acc, dv_acc, qn_sc, qu_sc,
):
    core = core_index()

    def load(kq_src, vd_src):
        kq_ref[...] = kq_src[...]
        vd_ref[...] = vd_src[...]

    @pl.when(core == 0)
    def _():
        load(mine_ref, other_ref)

    @pl.when(core == 1)
    def _():
        load(other_ref, mine_ref)

    head = SP + lax.rem(lax.axis_index("sp") // 2, EXTRA_HEADS)
    gain_q, gain_k = picked_gains(owner_ref, extra_ref, head)
    scales = kq_ref[:, TOK + QHALF :].astype(f32)
    q_cols = scale_columns(scales, 0)
    q_cols = jnp.where(core == 0, q_cols[:QTOK], q_cols[QTOK:QHALF])
    k_cols = scale_columns(scales, 3)
    prepare_keys(lambda j: kq_ref[j, :TOK], k_cols, gain_k, kn_sc, kt_sc, bound_sm)

    def quarter(ref):
        low = ref[:, TOK : TOK + QTOK]
        high = ref[:, TOK + QTOK : TOK + QHALF]
        return jnp.where(core == 0, low, high)

    q = quarter(kq_ref)
    do = quarter(vd_ref).reshape(SP * QTOK, DH)
    for j in range(SP):
        r = slice(j * QTOK, (j + 1) * QTOK)
        unit = q[j].astype(f32) * q_cols[:, j : j + 1]
        qu_sc[r] = unit
        qn_sc[r] = (unit * gain_q).astype(bf16)
        v_sc[j * TOK : (j + 1) * TOK] = vd_ref[j, :TOK]
    soften(qn_sc, do, lambda c: v_sc[c * CHUNK : (c + 1) * CHUNK], kn_sc, e_sc, dp_sc, stat_sc, bound_sm)

    def store(r, dk_part, dv_part):
        dk_acc[r] = dk_part
        dv_acc[r] = dv_part

    dq = gradients(qn_sc, do, kt_sc, e_sc, dp_sc, stat_sc, store)
    keep_ref[:, TOK : TOK + QTOK] = (dq * gain_q).astype(bf16).reshape(SP, QTOK, DH)
    keep_ref[:, TOK + QTOK :] = jnp.zeros((SP, 16, DH), bf16)
    key_part = jnp.zeros((8, DH), f32)
    for j in range(SP):
        r = slice(j * TOK, (j + 1) * TOK)
        dk = dk_acc[r] * SCORE_SCALE
        key_part += fold(dk * (kq_ref[j, :TOK].astype(f32) * k_cols[:, j : j + 1]))
        dk = (dk * gain_k).astype(bf16)
        dv = dv_acc[r].astype(bf16)

        keep_ref[j, :TOK] = jnp.where(core == 0, dk, dv)
        give_ref[j] = jnp.where(core == 0, dv, dk)
    part_ref[0:1] = jnp.sum(fold(dq * qu_sc[...]), axis=0, keepdims=True)
    part_ref[1:2] = jnp.sum(key_part, axis=0, keepdims=True)


def shared_heads(owner, extra, mine, other):
    vmem = pl.BlockSpec(memory_space=pltpu.VMEM)
    return pl.pallas_call(
        shared_kernel,
        in_specs=[
            pl.BlockSpec(memory_space=pltpu.SMEM),
            vmem,
            vmem,
            vmem,
        ],
        out_shape=[
            jax.ShapeDtypeStruct((SP, SHARE_BACK, DH), bf16),
            jax.ShapeDtypeStruct((SP, TOK, DH), bf16),
            jax.ShapeDtypeStruct((2, DH), f32),
        ],
        scratch_shapes=[
            pltpu.VMEM((SP, SHARE_ROWS, DH), bf16),
            pltpu.VMEM((SP, SHARE_ROWS, DH), bf16),
            pltpu.VMEM((SEQ, DH), bf16),
        ]
        + attention_scratch(SP * QTOK),
        compiler_params=pltpu.CompilerParams(vmem_limit_bytes=40 * MIB),
        cost_estimate=cost(SP * QTOK),
        name="shared_heads",
    )(owner, extra, mine, other)


def unpack_kernel(
    owner_ref, q_ref, k_ref, main_ref, share_ref, other_ref, gq_ref, gk_ref, gv_ref, gain_ref, dq_sc, dk_sc
):
    for d in range(SP):
        cols = slice(d * DH, (d + 1) * DH)
        dk_sc[:, cols] = main_ref[d, :TOK]
        gv_ref[0, :, cols] = main_ref[d, TOK : 2 * TOK]
        dq_sc[:, cols] = main_ref[d, 2 * TOK : 3 * TOK]
    core = core_index()

    def take(base, first_ref, second_ref):
        for g in range(EXTRA_HEADS):
            cols = slice((SP + g) * DH, (SP + g + 1) * DH)
            x = base + 2 * g

            def both(ref):
                return (ref[x, :TOK].astype(f32) + ref[x + 1, :TOK].astype(f32)).astype(bf16)

            dk_sc[:, cols] = both(first_ref)
            gv_ref[0, :, cols] = both(second_ref)
            for half in range(2):
                for c, ref in enumerate((first_ref, second_ref)):
                    at = (2 * half + c) * QTOK
                    dq_sc[at : at + QTOK, cols] = ref[x + half, TOK : TOK + QTOK]

    @pl.when(core == 0)
    def _():
        take(0, share_ref, other_ref)

    @pl.when(core == 1)
    def _():
        take(HALF, other_ref, share_ref)

    for raw_ref, grad_sc, out_ref in ((q_ref, dq_sc, gq_ref), (k_ref, dk_sc, gk_ref)):
        raw = raw_ref[0].astype(f32)
        grad = grad_sc[...].astype(f32)
        scale = row_scale(raw)
        inner = jnp.sum(grad * raw, axis=-1, keepdims=True)
        out_ref[0] = (scale * grad - (scale * scale * scale * (1.0 / INNER) * inner) * raw).astype(bf16)
    me = lax.axis_index("sp")
    sums = [jnp.zeros((2, DH), f32) for _ in range(2)]
    at = TOK + QTOK
    for head in range(HEADS):
        owner, slot = owner_slot(owner_ref, head)
        members = [(head, 0)] if head < SP else [
            (2 * (head - SP) + d, 1) for d in (0, 1, HALF, HALF + 1)
        ]
        value = jnp.zeros((2, DH), f32)
        for d, kind in members:
            rows = share_ref[d, at : at + 16].astype(f32)
            base = kind * 6
            value += jnp.concatenate(
                [
                    rows[base + 3 * w : base + 3 * w + 1]
                    + rows[base + 3 * w + 1 : base + 3 * w + 2]
                    + rows[base + 3 * w + 2 : base + 3 * w + 3]
                    for w in range(2)
                ],
                axis=0,
            )
        for s in range(2):
            sums[s] = sums[s] + jnp.where((owner == me) & (slot == s), value, 0.0)
    factor = 1.0 / math.sqrt(SP * SEQ)
    for s in range(2):
        gain_ref[0, s] = sums[s] * factor


def unpack(owner, q, k, main_back, share_back, other_back):
    vmem = pl.BlockSpec(memory_space=pltpu.VMEM)
    return pl.pallas_call(
        unpack_kernel,
        in_specs=[pl.BlockSpec(memory_space=pltpu.SMEM), vmem, vmem, vmem, vmem, vmem],
        out_specs=[vmem, vmem, vmem, vmem],
        out_shape=[
            jax.ShapeDtypeStruct((1, TOK, INNER), bf16),
            jax.ShapeDtypeStruct((1, TOK, INNER), bf16),
            jax.ShapeDtypeStruct((1, TOK, INNER), bf16),
            jax.ShapeDtypeStruct((1, 2, 2, DH), f32),
        ],
        scratch_shapes=[pltpu.VMEM((TOK, INNER), bf16), pltpu.VMEM((TOK, INNER), bf16)],
        compiler_params=pltpu.CompilerParams(vmem_limit_bytes=40 * MIB),
        name="unpack",
    )(owner, q, k, main_back, share_back, other_back)


def add_pair_kernel(keep_ref, got_ref, x_ref, out_ref, same_ref):
    same_ref[...] = x_ref[...]
    for d in range(SP):
        total = keep_ref[d, :TOK].astype(f32) + got_ref[d].astype(f32)
        out_ref[d, :TOK] = total.astype(bf16)
        out_ref[d, TOK:] = keep_ref[d, TOK:]


def add_pair(keep, got, x):
    vmem = pl.BlockSpec(memory_space=pltpu.VMEM)
    return pl.pallas_call(
        add_pair_kernel,
        in_specs=[vmem, vmem, vmem],
        out_shape=[
            jax.ShapeDtypeStruct((SP, SHARE_BACK, DH), bf16),
            jax.ShapeDtypeStruct(x.shape, x.dtype),
        ],
        compiler_params=pltpu.CompilerParams(vmem_limit_bytes=40 * MIB),
        name="add_pair",
    )(keep, got, x)


def add_sums_kernel(sum_ref, pair_ref, after_ref, out_ref):
    rows = []
    for i in range(4):
        rows += [*split3(sum_ref[i : i + 1])]
    extra = stack_rows(rows, 16)
    for d in range(SP):
        out_ref[d, TOK + QTOK :] = extra


def add_sums(sums, pair, after):
    vmem = pl.BlockSpec(memory_space=pltpu.VMEM)
    return pl.pallas_call(
        add_sums_kernel,
        in_specs=[vmem, vmem, pl.BlockSpec(memory_space=pl.ANY)],
        out_specs=vmem,
        out_shape=jax.ShapeDtypeStruct((SP, SHARE_BACK, DH), bf16),
        input_output_aliases={1: 0},
        compiler_params=pltpu.CompilerParams(vmem_limit_bytes=40 * MIB),
        name="add_sums",
    )(sums, pair, after)


def gate_kernel(main_ref, x_ref, extra_ref, out_ref):
    extra_ref[...] = main_ref[:, 4 * TOK :]


def gate(main, x):
    hbm = pl.BlockSpec(memory_space=pltpu.HBM)
    vmem = pl.BlockSpec(memory_space=pltpu.VMEM)
    return pl.pallas_call(
        gate_kernel,
        in_specs=[vmem, hbm],
        out_specs=[vmem, hbm],
        out_shape=[
            jax.ShapeDtypeStruct((SP, 32, DH), bf16),
            jax.ShapeDtypeStruct(x.shape, x.dtype),
        ],
        input_output_aliases={1: 1},
        compiler_params=pltpu.CompilerParams(vmem_limit_bytes=40 * MIB),
        name="gate",
    )(main, x)


def after_kernel(x_ref, before_ref, out_ref):
    pass


def after(x, before):
    anywhere = pl.BlockSpec(memory_space=pl.ANY)
    return pl.pallas_call(
        after_kernel,
        in_specs=[anywhere, anywhere],
        out_specs=anywhere,
        out_shape=jax.ShapeDtypeStruct(x.shape, x.dtype),
        input_output_aliases={0: 0},
        compiler_params=pltpu.CompilerParams(vmem_limit_bytes=40 * MIB),
        name="after",
    )(x, before)


def swap(x):
    return lax.ppermute(x, "fsdp", [(i, i ^ 1) for i in range(16)])


def exchange(field):
    return lax.all_to_all(field, "sp", split_axis=0, concat_axis=0, tiled=True)


def fsdp_sum(x, steps):
    across = (6, 7, 4, 5, 2, 3, 0, 1)
    partners = [
        [i ^ 1 for i in range(16)],
        [i ^ 2 for i in range(16)],
        [i ^ 4 for i in range(16)],
        [across[i // 2] * 2 + i % 2 for i in range(16)],
    ]
    for partner in partners[steps]:
        x = x + lax.ppermute(x, "fsdp", list(enumerate(partner)))
    return x


def per_device(query_raw, key_raw, value_in, grad_out, norm_gains, head_owner):
    main_send, share_half, give = pack(query_raw, key_raw, value_in, grad_out, norm_gains)
    main = exchange(main_send)
    other_half = (1 - core_index()) * HALF
    share_send = lax.dynamic_update_slice(share_half, swap(give), (other_half, 0, 0))
    extra, share_send = gate(main, share_send)
    share = exchange(share_send)
    main_out, part = main_heads(head_owner, main)
    main_back = exchange(main_out)
    share = after(share, part)
    keep, give_back, part_s = shared_heads(head_owner, extra, share, swap(share))
    sums = fsdp_sum(jnp.concatenate([part, part_s], axis=0), slice(0, 2))
    pair, sums = add_pair(keep, swap(give_back), sums)
    sums = fsdp_sum(sums, slice(2, 4))
    share_back = exchange(add_sums(sums, pair, main_back[:1, :16]))
    return tuple(
        unpack(head_owner, query_raw, key_raw, main_back, share_back, swap(share_back))
    )


def solution(mesh):
    return jax.shard_map(
        per_device,
        mesh=mesh,
        in_specs=(
            P("fsdp", "sp", None),
            P("fsdp", "sp", None),
            P("fsdp", "sp", None),
            P("fsdp", "sp", None),
            P("sp", None, None, None),
            P(),
        ),
        out_specs=(
            P("fsdp", "sp", None),
            P("fsdp", "sp", None),
            P("fsdp", "sp", None),
            P("sp", None, None, None),
        ),
        check_vma=False,
    )
```

```python
import functools
import math

import jax
import jax.numpy as jnp
from jax import lax
from jax.experimental import pallas as pl
from jax.experimental.pallas import tpu as pltpu
from jax.sharding import PartitionSpec as P

EPSILON = 1e-06
LOG2E = math.log2(math.e)
f32 = jnp.float32
bf16 = jnp.bfloat16

HEADS = 20
DH = 128
INNER = HEADS * DH
SP = 16
TOK = 128
SEQ = SP * TOK
EXTRA_HEADS = HEADS - SP
HALF = SP // 2
QHALF = TOK // 2
QTOK = TOK // 4
MAIN_ROWS = 4 * TOK + 16
SHARE_ROWS = TOK + QHALF + 16
MAIN_BACK = 3 * TOK
SHARE_BACK = TOK + QTOK + 16
MIB = 2**20
GATE_LIMIT = 53760 * 1024
SCORE_SCALE = DH**-0.5
SAFE = 60.0
CHUNK = 256


def core_index():
    return lax.rem(lax.axis_index("fsdp"), 2)


def split3(x):
    hi = x.astype(bf16).astype(f32)
    mid = (x - hi).astype(bf16).astype(f32)
    return hi, mid, x - hi - mid


def split2(x):
    hi = x.astype(bf16).astype(f32)
    return hi, x - hi


def stack_rows(rows, count):
    if len(rows) < count:
        rows = rows + [jnp.zeros((count - len(rows), rows[0].shape[-1]), f32)]
    return jnp.concatenate(rows, axis=0).astype(bf16)


def contract(a, b, da, db):
    return lax.dot_general(a, b, (((da,), (db,)), ((), ())), preferred_element_type=f32)


def row_scale(raw):
    return lax.rsqrt(jnp.sum(raw * raw, axis=-1, keepdims=True) * (1.0 / INNER) + EPSILON)


def to_row(column):
    return jnp.broadcast_to(column, (TOK, TOK)).T[0:1]


def pack_main_kernel(
    q_hbm, k_hbm, v_hbm, do_hbm, gain_ref, main_ref, row_ref, q_ref, k_ref, v_ref, do_ref, sems
):
    pairs = ((q_hbm, q_ref), (k_hbm, k_ref), (v_hbm, v_ref), (do_hbm, do_ref))
    copies = [
        pltpu.make_async_copy(src, dst, sems.at[i]) for i, (src, dst) in enumerate(pairs)
    ]
    for copy in copies:
        copy.start()
    copies[0].wait()
    q_row = to_row(row_scale(q_ref[0].astype(f32)))
    copies[1].wait()
    k_row = to_row(row_scale(k_ref[0].astype(f32)))
    row_ref[0:1] = q_row
    row_ref[1:2] = k_row
    gains = gain_ref[0]
    rows = [*split2(q_row), *split2(k_row)]
    for slot in range(2):
        for which in range(2):
            rows += [*split3(gains[slot, which : which + 1])]
    extra = stack_rows(rows, 16)
    copies[2].wait()
    copies[3].wait()
    for d in range(SP):
        cols = slice(d * DH, (d + 1) * DH)
        for part, ref in enumerate((q_ref, k_ref, v_ref, do_ref)):
            main_ref[d, part * TOK : (part + 1) * TOK] = ref[0, :, cols]
        main_ref[d, 4 * TOK :] = extra


def pack_main(q, k, v, do, gains):
    hbm = pl.BlockSpec(memory_space=pltpu.HBM)
    return pl.pallas_call(
        pack_main_kernel,
        in_specs=[hbm, hbm, hbm, hbm, pl.BlockSpec(memory_space=pltpu.VMEM)],
        scratch_shapes=[pltpu.VMEM((1, TOK, INNER), bf16)] * 4 + [pltpu.SemaphoreType.DMA((4,))],
        out_shape=[
            jax.ShapeDtypeStruct((SP, MAIN_ROWS, DH), bf16),
            jax.ShapeDtypeStruct((8, DH), f32),
        ],
        compiler_params=pltpu.CompilerParams(vmem_limit_bytes=60 * MIB),
        name="pack_main",
    )(q, k, v, do, gains)


def pack_share_kernel(
    q_hbm, k_hbm, v_hbm, do_hbm, row_ref, share_ref, give_ref, q_ref, k_ref, v_ref, do_ref, sems
):
    pairs = ((q_hbm, q_ref), (k_hbm, k_ref), (v_hbm, v_ref), (do_hbm, do_ref))
    last = pl.ds(SP * DH, EXTRA_HEADS * DH)
    copies = [
        pltpu.make_async_copy(src.at[:, :, last], dst, sems.at[i])
        for i, (src, dst) in enumerate(pairs)
    ]
    for copy in copies:
        copy.start()
    for copy in copies:
        copy.wait()
    q_row = row_ref[0:1]
    k_row = row_ref[1:2]
    core = core_index()

    def fill(out_ref, base, first_ref, second_ref, with_scales):
        for p in range(HALF):
            cols = slice(p // 2 * DH, (p // 2 + 1) * DH)
            half = slice(p % 2 * QHALF, (p % 2 + 1) * QHALF)
            out_ref[base + p, :TOK] = first_ref[0, :, cols]
            out_ref[base + p, TOK : TOK + QHALF] = second_ref[0, half, cols]
            if with_scales:
                q_own = jnp.concatenate([q_row[:, half]] * 2, axis=1)
                tail = stack_rows([*split3(q_own), *split3(k_row)], 16)
            else:
                tail = jnp.zeros((16, DH), bf16)
            out_ref[base + p, TOK + QHALF :] = tail

    @pl.when(core == 0)
    def _():
        fill(share_ref, 0, k_ref, q_ref, True)
        fill(give_ref, 0, v_ref, do_ref, False)

    @pl.when(core == 1)
    def _():
        fill(share_ref, HALF, v_ref, do_ref, False)
        fill(give_ref, 0, k_ref, q_ref, True)


def pack_share(q, k, v, do, rows):
    hbm = pl.BlockSpec(memory_space=pltpu.HBM)
    return pl.pallas_call(
        pack_share_kernel,
        in_specs=[hbm, hbm, hbm, hbm, pl.BlockSpec(memory_space=pltpu.VMEM)],
        scratch_shapes=[pltpu.VMEM((1, TOK, EXTRA_HEADS * DH), bf16)] * 4
        + [pltpu.SemaphoreType.DMA((4,))],
        out_shape=[
            jax.ShapeDtypeStruct((SP, SHARE_ROWS, DH), bf16),
            jax.ShapeDtypeStruct((HALF, SHARE_ROWS, DH), bf16),
        ],
        compiler_params=pltpu.CompilerParams(vmem_limit_bytes=60 * MIB),
        name="pack_share",
    )(q, k, v, do, rows)


def owner_slot(owner_ref, head):
    owner = owner_ref[head]
    slot = jnp.int32(0)
    for other in range(HEADS):
        same = (owner_ref[other] == owner) & (other < head)
        slot = slot + same.astype(jnp.int32)
    return owner, slot


def picked_gains(owner_ref, gain_ref, head):
    owner, slot = owner_slot(owner_ref, head)
    rows = gain_ref[owner].astype(f32)
    sums = []
    for which in range(2):
        both = []
        for s in range(2):
            at = 4 + (s * 2 + which) * 3
            both.append(rows[at : at + 1] + rows[at + 1 : at + 2] + rows[at + 2 : at + 3])
        sums.append(jnp.where(slot == 0, both[0], both[1]))
    return sums


def scale_columns(rows, at, parts):
    return sum(rows[:, at + i] for i in range(parts)).T


def largest_square(x):
    return jnp.max(contract(jnp.ones((8, DH), bf16), x * x, 1, 1))


def fold(x):
    return jnp.sum(x.reshape(x.shape[0] // 8, 8, x.shape[1]), axis=0)


def prepare_keys(key_at, k_cols, gain_k, kn_sc, kt_sc, bound_sm):
    for j in range(SP):
        r = slice(j * TOK, (j + 1) * TOK)
        kn_sc[r] = (key_at(j).astype(f32) * k_cols[:, j : j + 1] * gain_k).astype(bf16)
    bound_sm[0] = largest_square(kn_sc[...])
    kt_sc[...] = kn_sc[...].T


def soften(qn_sc, do, value_at, kn_sc, e_sc, dp_sc, stat_sc, bound_sm):
    qn = qn_sc[...]
    square = largest_square(qn) * bound_sm[0]
    small = square * (SCORE_SCALE * SCORE_SCALE) <= SAFE * SAFE

    def run(top):
        total = delta = None
        for c in range(SEQ // CHUNK):
            r = slice(c * CHUNK, (c + 1) * CHUNK)
            s = contract(kn_sc[r], qn, 1, 1) * (SCORE_SCALE * LOG2E)
            e = jnp.exp2(s if top is None else s - top)
            e_sc[r] = e
            dp = contract(value_at(c), do, 1, 1)
            dp_sc[r] = dp
            total = fold(e) if total is None else total + fold(e)
            delta = fold(e * dp) if delta is None else delta + fold(e * dp)
        inv = 1.0 / jnp.sum(total, axis=0, keepdims=True)
        stat_sc[0:1] = inv
        stat_sc[1:2] = jnp.sum(delta, axis=0, keepdims=True) * inv

    @pl.when(small)
    def _():
        run(None)

    @pl.when(jnp.logical_not(small))
    def _():
        top = None
        for c in range(SEQ // CHUNK):
            r = slice(c * CHUNK, (c + 1) * CHUNK)
            s = contract(kn_sc[r], qn, 1, 1) * (SCORE_SCALE * LOG2E)
            part = jnp.max(s.reshape(CHUNK // 8, 8, s.shape[1]), axis=0)
            top = part if top is None else jnp.maximum(top, part)
        run(jnp.max(top, axis=0, keepdims=True))


def gradients(qn_sc, do, kt_sc, e_sc, dp_sc, stat_sc, store):
    qn = qn_sc[...]
    inv = stat_sc[0:1]
    delta = stat_sc[1:2]
    dq_t = None
    for c in range(SEQ // CHUNK):
        r = slice(c * CHUNK, (c + 1) * CHUNK)
        p = e_sc[r] * inv
        ds = (p * (dp_sc[r] - delta)).astype(bf16)
        store(r, contract(ds, qn, 1, 0), contract(p.astype(bf16), do, 1, 0))
        part = contract(kt_sc[:, r], ds, 1, 0)
        dq_t = part if dq_t is None else dq_t + part
    return dq_t.T * SCORE_SCALE


def attention_scratch(query_rows):
    return [
        pltpu.VMEM((SEQ, query_rows), f32),
        pltpu.VMEM((SEQ, query_rows), f32),
        pltpu.VMEM((8, query_rows), f32),
        pltpu.SMEM((1,), f32),
        pltpu.VMEM((SEQ, DH), bf16),
        pltpu.VMEM((DH, SEQ), bf16),
        pltpu.VMEM((SEQ, DH), f32),
        pltpu.VMEM((SEQ, DH), f32),
        pltpu.VMEM((query_rows, DH), bf16),
        pltpu.VMEM((query_rows, DH), f32),
    ]


def cost(query_rows):
    work = query_rows * SEQ
    return pl.CostEstimate(flops=10 * DH * work, bytes_accessed=4 * 2**20, transcendentals=work)


STEPS = 2


def main_kernel(
    owner_ref, field_hbm, back_hbm, part_ref, field_ref, back_ref, in_sems, sems, qg_acc,
    e_sc, dp_sc, stat_sc, bound_sm, kn_sc, kt_sc, dk_acc, dv_acc, qn_sc, qu_sc,
):
    sources = SP // STEPS
    rows = sources * TOK
    blocks = CHUNK // TOK

    def fetch(part, rows):
        at = (slice(None), pl.ds(part * TOK, rows))
        return pltpu.make_async_copy(field_hbm.at[at], field_ref.at[at], in_sems.at[part])

    fetches = [fetch(part, TOK) for part in range(4)] + [fetch(4, 16)]
    for part in (4, 1, 0, 2, 3):
        fetches[part].start()
    fetches[4].wait()
    gain_q, gain_k = picked_gains(owner_ref, field_ref.at[:, 4 * TOK :], lax.axis_index("sp"))
    scales = field_ref[:, 4 * TOK :].astype(f32)
    q_cols = scale_columns(scales, 0, 2)
    k_cols = scale_columns(scales, 2, 2)
    qg_acc[...] = jnp.zeros_like(qg_acc)

    def key_at(j):
        return field_ref[j, TOK : 2 * TOK]

    def value_at(c):
        return field_ref[c * blocks : (c + 1) * blocks, 2 * TOK : 3 * TOK].reshape(CHUNK, DH)

    fetches[1].wait()

    def query_copy(step):
        at = (pl.ds(step * sources, sources), pl.ds(2 * TOK, TOK))
        return pltpu.make_async_copy(back_ref.at[at], back_hbm.at[at], sems.at[step])

    def key_copy(j):
        at = (j, pl.ds(0, 2 * TOK))
        return pltpu.make_async_copy(back_ref.at[at], back_hbm.at[at], sems.at[STEPS + j])

    prepare_keys(key_at, k_cols, gain_k, kn_sc, kt_sc, bound_sm)
    dk_acc[...] = jnp.zeros_like(dk_acc)
    dv_acc[...] = jnp.zeros_like(dv_acc)

    for part in (0, 2, 3):
        fetches[part].wait()

    @pl.loop(0, STEPS)
    def _(step):
        for b in range(STEPS):

            @pl.when(step == b)
            def _():
                for j in range(sources):
                    at = b * sources + j
                    r = slice(j * TOK, (j + 1) * TOK)
                    unit = field_ref[at, :TOK].astype(f32) * q_cols[:, at : at + 1]
                    qu_sc[r] = unit
                    qn_sc[r] = (unit * gain_q).astype(bf16)

        mine = pl.ds(step * sources, sources)
        do = field_ref[mine, 3 * TOK : 4 * TOK].reshape(rows, DH)
        soften(qn_sc, do, value_at, kn_sc, e_sc, dp_sc, stat_sc, bound_sm)

        def store(r, dk_part, dv_part):
            dk_acc[r] += dk_part
            dv_acc[r] += dv_part

        dq = gradients(qn_sc, do, kt_sc, e_sc, dp_sc, stat_sc, store)
        back_ref[mine, 2 * TOK :] = (dq * gain_q).astype(bf16).reshape(sources, TOK, DH)
        query_copy(step).start()
        qg_acc[...] += fold(dq * qu_sc[...])

    key_part = jnp.zeros((8, DH), f32)
    for j in range(SP):
        r = slice(j * TOK, (j + 1) * TOK)
        dk = dk_acc[r] * SCORE_SCALE
        key_part += fold(dk * (key_at(j).astype(f32) * k_cols[:, j : j + 1]))
        back_ref[j, :TOK] = (dk * gain_k).astype(bf16)
        back_ref[j, TOK : 2 * TOK] = dv_acc[r].astype(bf16)
        key_copy(j).start()
    part_ref[0:1] = jnp.sum(qg_acc[...], axis=0, keepdims=True)
    part_ref[1:2] = jnp.sum(key_part, axis=0, keepdims=True)
    for step in range(STEPS):
        query_copy(step).wait()
    for j in range(SP):
        key_copy(j).wait()


def main_heads(owner, field):
    return pl.pallas_call(
        main_kernel,
        in_specs=[
            pl.BlockSpec(memory_space=pltpu.SMEM),
            pl.BlockSpec(memory_space=pl.ANY),
        ],
        out_shape=[
            jax.ShapeDtypeStruct((SP, MAIN_BACK, DH), bf16),
            jax.ShapeDtypeStruct((2, DH), f32),
        ],
        out_specs=[
            pl.BlockSpec(memory_space=pltpu.HBM),
            pl.BlockSpec(memory_space=pltpu.VMEM),
        ],
        scratch_shapes=[
            pltpu.VMEM((SP, MAIN_ROWS, DH), bf16),
            pltpu.VMEM((SP, MAIN_BACK, DH), bf16),
            pltpu.SemaphoreType.DMA((5,)),
            pltpu.SemaphoreType.DMA((STEPS + SP,)),
            pltpu.VMEM((8, DH), f32),
        ]
        + attention_scratch(SEQ // STEPS),
        compiler_params=pltpu.CompilerParams(vmem_limit_bytes=53760 * 1024),
        cost_estimate=cost(SEQ),
        name="main_heads",
    )(owner, field)


def shared_kernel(
    owner_ref, extra_ref, mine_ref, other_ref, keep_ref, give_ref, part_ref,
    kq_ref, vd_ref, v_sc,
    e_sc, dp_sc, stat_sc, bound_sm, kn_sc, kt_sc, dk_acc, dv_acc, qn_sc, qu_sc,
):
    core = core_index()

    def load(kq_src, vd_src):
        kq_ref[...] = kq_src[...]
        vd_ref[...] = vd_src[...]

    @pl.when(core == 0)
    def _():
        load(mine_ref, other_ref)

    @pl.when(core == 1)
    def _():
        load(other_ref, mine_ref)

    head = SP + lax.rem(lax.axis_index("sp") // 2, EXTRA_HEADS)
    gain_q, gain_k = picked_gains(owner_ref, extra_ref, head)
    scales = kq_ref[:, TOK + QHALF :].astype(f32)
    q_cols = scale_columns(scales, 0, 3)
    q_cols = jnp.where(core == 0, q_cols[:QTOK], q_cols[QTOK:QHALF])
    k_cols = scale_columns(scales, 3, 3)
    prepare_keys(lambda j: kq_ref[j, :TOK], k_cols, gain_k, kn_sc, kt_sc, bound_sm)

    def quarter(ref):
        low = ref[:, TOK : TOK + QTOK]
        high = ref[:, TOK + QTOK : TOK + QHALF]
        return jnp.where(core == 0, low, high)

    q = quarter(kq_ref)
    do = quarter(vd_ref).reshape(SP * QTOK, DH)
    for j in range(SP):
        r = slice(j * QTOK, (j + 1) * QTOK)
        unit = q[j].astype(f32) * q_cols[:, j : j + 1]
        qu_sc[r] = unit
        qn_sc[r] = (unit * gain_q).astype(bf16)
        v_sc[j * TOK : (j + 1) * TOK] = vd_ref[j, :TOK]
    soften(qn_sc, do, lambda c: v_sc[c * CHUNK : (c + 1) * CHUNK], kn_sc, e_sc, dp_sc, stat_sc, bound_sm)

    def store(r, dk_part, dv_part):
        dk_acc[r] = dk_part
        dv_acc[r] = dv_part

    dq = gradients(qn_sc, do, kt_sc, e_sc, dp_sc, stat_sc, store)
    keep_ref[:, TOK : TOK + QTOK] = (dq * gain_q).astype(bf16).reshape(SP, QTOK, DH)
    keep_ref[:, TOK + QTOK :] = jnp.zeros((SP, 16, DH), bf16)
    key_part = jnp.zeros((8, DH), f32)
    for j in range(SP):
        r = slice(j * TOK, (j + 1) * TOK)
        dk = dk_acc[r] * SCORE_SCALE
        key_part += fold(dk * (kq_ref[j, :TOK].astype(f32) * k_cols[:, j : j + 1]))
        dk = (dk * gain_k).astype(bf16)
        dv = dv_acc[r].astype(bf16)

        keep_ref[j, :TOK] = jnp.where(core == 0, dk, dv)
        give_ref[j] = jnp.where(core == 0, dv, dk)
    part_ref[0:1] = jnp.sum(fold(dq * qu_sc[...]), axis=0, keepdims=True)
    part_ref[1:2] = jnp.sum(key_part, axis=0, keepdims=True)


def shared_heads(owner, extra, mine, other):
    vmem = pl.BlockSpec(memory_space=pltpu.VMEM)
    return pl.pallas_call(
        shared_kernel,
        in_specs=[
            pl.BlockSpec(memory_space=pltpu.SMEM),
            vmem,
            vmem,
            vmem,
        ],
        out_shape=[
            jax.ShapeDtypeStruct((SP, SHARE_BACK, DH), bf16),
            jax.ShapeDtypeStruct((SP, TOK, DH), bf16),
            jax.ShapeDtypeStruct((2, DH), f32),
        ],
        scratch_shapes=[
            pltpu.VMEM((SP, SHARE_ROWS, DH), bf16),
            pltpu.VMEM((SP, SHARE_ROWS, DH), bf16),
            pltpu.VMEM((SEQ, DH), bf16),
        ]
        + attention_scratch(SP * QTOK),
        compiler_params=pltpu.CompilerParams(vmem_limit_bytes=40 * MIB),
        cost_estimate=cost(SP * QTOK),
        name="shared_heads",
    )(owner, extra, mine, other)


def unpack_kernel(
    owner_ref, q_ref, k_ref, main_ref, share_ref, other_ref, gq_ref, gk_ref, gv_ref, gain_ref, dq_sc, dk_sc
):
    for d in range(SP):
        cols = slice(d * DH, (d + 1) * DH)
        dk_sc[:, cols] = main_ref[d, :TOK]
        gv_ref[0, :, cols] = main_ref[d, TOK : 2 * TOK]
        dq_sc[:, cols] = main_ref[d, 2 * TOK : 3 * TOK]
    core = core_index()

    def take(base, first_ref, second_ref):
        for g in range(EXTRA_HEADS):
            cols = slice((SP + g) * DH, (SP + g + 1) * DH)
            x = base + 2 * g

            def both(ref):
                return (ref[x, :TOK].astype(f32) + ref[x + 1, :TOK].astype(f32)).astype(bf16)

            dk_sc[:, cols] = both(first_ref)
            gv_ref[0, :, cols] = both(second_ref)
            for half in range(2):
                for c, ref in enumerate((first_ref, second_ref)):
                    at = (2 * half + c) * QTOK
                    dq_sc[at : at + QTOK, cols] = ref[x + half, TOK : TOK + QTOK]

    @pl.when(core == 0)
    def _():
        take(0, share_ref, other_ref)

    @pl.when(core == 1)
    def _():
        take(HALF, other_ref, share_ref)

    for raw_ref, grad_sc, out_ref in ((q_ref, dq_sc, gq_ref), (k_ref, dk_sc, gk_ref)):
        raw = raw_ref[0].astype(f32)
        grad = grad_sc[...].astype(f32)
        scale = row_scale(raw)
        inner = jnp.sum(grad * raw, axis=-1, keepdims=True)
        out_ref[0] = (scale * grad - (scale * scale * scale * (1.0 / INNER) * inner) * raw).astype(bf16)
    me = lax.axis_index("sp")
    sums = [jnp.zeros((2, DH), f32) for _ in range(2)]
    at = TOK + QTOK
    for head in range(HEADS):
        owner, slot = owner_slot(owner_ref, head)
        members = [(head, 0)] if head < SP else [
            (2 * (head - SP) + d, 1) for d in (0, 1, HALF, HALF + 1)
        ]
        value = jnp.zeros((2, DH), f32)
        for d, kind in members:
            rows = share_ref[d, at : at + 16].astype(f32)
            base = kind * 6
            value += jnp.concatenate(
                [
                    rows[base + 3 * w : base + 3 * w + 1]
                    + rows[base + 3 * w + 1 : base + 3 * w + 2]
                    + rows[base + 3 * w + 2 : base + 3 * w + 3]
                    for w in range(2)
                ],
                axis=0,
            )
        for s in range(2):
            sums[s] = sums[s] + jnp.where((owner == me) & (slot == s), value, 0.0)
    factor = 1.0 / math.sqrt(SP * SEQ)
    for s in range(2):
        gain_ref[0, s] = sums[s] * factor


def unpack(owner, q, k, main_back, share_back, other_back):
    vmem = pl.BlockSpec(memory_space=pltpu.VMEM)
    return pl.pallas_call(
        unpack_kernel,
        in_specs=[pl.BlockSpec(memory_space=pltpu.SMEM), vmem, vmem, vmem, vmem, vmem],
        out_specs=[vmem, vmem, vmem, vmem],
        out_shape=[
            jax.ShapeDtypeStruct((1, TOK, INNER), bf16),
            jax.ShapeDtypeStruct((1, TOK, INNER), bf16),
            jax.ShapeDtypeStruct((1, TOK, INNER), bf16),
            jax.ShapeDtypeStruct((1, 2, 2, DH), f32),
        ],
        scratch_shapes=[pltpu.VMEM((TOK, INNER), bf16), pltpu.VMEM((TOK, INNER), bf16)],
        compiler_params=pltpu.CompilerParams(vmem_limit_bytes=51712 * 1024),
        name="unpack",
    )(owner, q, k, main_back, share_back, other_back)


def add_pair_kernel(keep_ref, got_ref, x_ref, out_ref, same_ref):
    same_ref[...] = x_ref[...]
    for d in range(SP):
        total = keep_ref[d, :TOK].astype(f32) + got_ref[d].astype(f32)
        out_ref[d, :TOK] = total.astype(bf16)
        out_ref[d, TOK:] = keep_ref[d, TOK:]


def add_pair(keep, got, x):
    vmem = pl.BlockSpec(memory_space=pltpu.VMEM)
    return pl.pallas_call(
        add_pair_kernel,
        in_specs=[vmem, vmem, vmem],
        out_shape=[
            jax.ShapeDtypeStruct((SP, SHARE_BACK, DH), bf16),
            jax.ShapeDtypeStruct(x.shape, x.dtype),
        ],
        compiler_params=pltpu.CompilerParams(vmem_limit_bytes=40 * MIB),
        name="add_pair",
    )(keep, got, x)


def add_sums_kernel(sum_ref, pair_ref, after_ref, out_ref):
    rows = []
    for i in range(4):
        rows += [*split3(sum_ref[i : i + 1])]
    extra = stack_rows(rows, 16)
    for d in range(SP):
        out_ref[d, TOK + QTOK :] = extra


def add_sums(sums, pair, after):
    vmem = pl.BlockSpec(memory_space=pltpu.VMEM)
    return pl.pallas_call(
        add_sums_kernel,
        in_specs=[vmem, vmem, pl.BlockSpec(memory_space=pl.ANY)],
        out_specs=vmem,
        out_shape=jax.ShapeDtypeStruct((SP, SHARE_BACK, DH), bf16),
        input_output_aliases={1: 0},
        compiler_params=pltpu.CompilerParams(vmem_limit_bytes=40 * MIB),
        name="add_sums",
    )(sums, pair, after)


def gate_kernel(main_ref, x_ref, extra_ref, out_ref, sem):
    copy = pltpu.make_async_copy(main_ref.at[:, pl.ds(4 * TOK, 16)], extra_ref, sem)
    copy.start()
    copy.wait()


def gate(main, x):
    anywhere = pl.BlockSpec(memory_space=pl.ANY)
    return pl.pallas_call(
        gate_kernel,
        in_specs=[anywhere, anywhere],
        out_specs=[pl.BlockSpec(memory_space=pltpu.VMEM), anywhere],
        out_shape=[
            jax.ShapeDtypeStruct((SP, 16, DH), bf16),
            jax.ShapeDtypeStruct(x.shape, x.dtype),
        ],
        scratch_shapes=[pltpu.SemaphoreType.DMA],
        input_output_aliases={1: 1},
        compiler_params=pltpu.CompilerParams(vmem_limit_bytes=GATE_LIMIT),
        name="gate",
    )(main, x)


def after_kernel(x_ref, before_ref, out_ref):
    pass


def after(x, before):
    anywhere = pl.BlockSpec(memory_space=pl.ANY)
    return pl.pallas_call(
        after_kernel,
        in_specs=[anywhere, anywhere],
        out_specs=anywhere,
        out_shape=jax.ShapeDtypeStruct(x.shape, x.dtype),
        input_output_aliases={0: 0},
        compiler_params=pltpu.CompilerParams(vmem_limit_bytes=40 * MIB),
        name="after",
    )(x, before)


def swap(x):
    return lax.ppermute(x, "fsdp", [(i, i ^ 1) for i in range(16)])


def exchange(field):
    return lax.all_to_all(field, "sp", split_axis=0, concat_axis=0, tiled=True)


def fsdp_sum(x, steps):
    across = (6, 7, 4, 5, 2, 3, 0, 1)
    partners = [
        [i ^ 1 for i in range(16)],
        [i ^ 2 for i in range(16)],
        [i ^ 4 for i in range(16)],
        [across[i // 2] * 2 + i % 2 for i in range(16)],
    ]
    for partner in partners[steps]:
        x = x + lax.ppermute(x, "fsdp", list(enumerate(partner)))
    return x


def per_device(query_raw, key_raw, value_in, grad_out, norm_gains, head_owner):
    main_send, rows = pack_main(query_raw, key_raw, value_in, grad_out, norm_gains)
    share_half, give = pack_share(query_raw, key_raw, value_in, grad_out, rows)
    main = exchange(main_send)
    other_half = (1 - core_index()) * HALF
    extra, got = gate(main, swap(give))
    share_send = lax.dynamic_update_slice(share_half, got, (other_half, 0, 0))
    share = exchange(share_send)
    main_out, part = main_heads(head_owner, main)
    main_back = exchange(main_out)
    share = after(share, part)
    keep, give_back, part_s = shared_heads(head_owner, extra, share, swap(share))
    sums = fsdp_sum(jnp.concatenate([part, part_s], axis=0), slice(0, 2))
    pair, sums = add_pair(keep, swap(give_back), sums)
    sums = fsdp_sum(sums, slice(2, 4))
    share_back = exchange(add_sums(sums, pair, main_back[:1, :16]))
    return tuple(
        unpack(head_owner, query_raw, key_raw, main_back, share_back, swap(share_back))
    )


def solution(mesh):
    return jax.shard_map(
        per_device,
        mesh=mesh,
        in_specs=(
            P("fsdp", "sp", None),
            P("fsdp", "sp", None),
            P("fsdp", "sp", None),
            P("fsdp", "sp", None),
            P("sp", None, None, None),
            P(),
        ),
        out_specs=(
            P("fsdp", "sp", None),
            P("fsdp", "sp", None),
            P("fsdp", "sp", None),
            P("sp", None, None, None),
        ),
        check_vma=False,
    )
```

```python
import functools
import math

import jax
import jax.numpy as jnp
from jax import lax
from jax.experimental import pallas as pl
from jax.experimental.pallas import tpu as pltpu
from jax.sharding import PartitionSpec as P

EPSILON = 1e-06
LOG2E = math.log2(math.e)
f32 = jnp.float32
bf16 = jnp.bfloat16

HEADS = 20
DH = 128
INNER = HEADS * DH
SP = 16
TOK = 128
SEQ = SP * TOK
EXTRA_HEADS = HEADS - SP
HALF = SP // 2
QHALF = TOK // 2
QTOK = TOK // 4
MAIN_ROWS = 4 * TOK + 16
SHARE_ROWS = TOK + QHALF + 16
MAIN_BACK = 3 * TOK
SHARE_BACK = TOK + QTOK + 16
MIB = 2**20
UNPACK_LIMIT = 48 * 1024 * 1024
SCORE_SCALE = DH**-0.5
SAFE = 60.0
CHUNK = 256


def core_index():
    return lax.rem(lax.axis_index("fsdp"), 2)


def split3(x):
    hi = x.astype(bf16).astype(f32)
    mid = (x - hi).astype(bf16).astype(f32)
    return hi, mid, x - hi - mid


def split2(x):
    hi = x.astype(bf16).astype(f32)
    return hi, x - hi


def stack_rows(rows, count):
    if len(rows) < count:
        rows = rows + [jnp.zeros((count - len(rows), rows[0].shape[-1]), f32)]
    return jnp.concatenate(rows, axis=0).astype(bf16)


def contract(a, b, da, db):
    return lax.dot_general(a, b, (((da,), (db,)), ((), ())), preferred_element_type=f32)


def row_scale(raw):
    return lax.rsqrt(jnp.sum(raw * raw, axis=-1, keepdims=True) * (1.0 / INNER) + EPSILON)


def to_row(column):
    return jnp.broadcast_to(column, (TOK, TOK)).T[0:1]


def pack_main_kernel(
    q_hbm, k_hbm, v_hbm, do_hbm, gain_ref, main_ref, row_ref, q_ref, k_ref, v_ref, do_ref, sems
):
    pairs = ((q_hbm, q_ref), (k_hbm, k_ref), (v_hbm, v_ref), (do_hbm, do_ref))
    copies = [
        pltpu.make_async_copy(src, dst, sems.at[i]) for i, (src, dst) in enumerate(pairs)
    ]
    for copy in copies:
        copy.start()
    copies[0].wait()
    q_row = to_row(row_scale(q_ref[0].astype(f32)))
    copies[1].wait()
    k_row = to_row(row_scale(k_ref[0].astype(f32)))
    row_ref[0:1] = q_row
    row_ref[1:2] = k_row
    gains = gain_ref[0]
    rows = [*split2(q_row), *split2(k_row)]
    for slot in range(2):
        for which in range(2):
            rows += [*split3(gains[slot, which : which + 1])]
    extra = stack_rows(rows, 16)
    copies[2].wait()
    copies[3].wait()
    for d in range(SP):
        cols = slice(d * DH, (d + 1) * DH)
        for part, ref in enumerate((q_ref, k_ref, v_ref, do_ref)):
            main_ref[d, part * TOK : (part + 1) * TOK] = ref[0, :, cols]
        main_ref[d, 4 * TOK :] = extra


def pack_main(q, k, v, do, gains):
    hbm = pl.BlockSpec(memory_space=pltpu.HBM)
    return pl.pallas_call(
        pack_main_kernel,
        in_specs=[hbm, hbm, hbm, hbm, pl.BlockSpec(memory_space=pltpu.VMEM)],
        scratch_shapes=[pltpu.VMEM((1, TOK, INNER), bf16)] * 4 + [pltpu.SemaphoreType.DMA((4,))],
        out_shape=[
            jax.ShapeDtypeStruct((SP, MAIN_ROWS, DH), bf16),
            jax.ShapeDtypeStruct((8, DH), f32),
        ],
        compiler_params=pltpu.CompilerParams(vmem_limit_bytes=60 * MIB),
        name="pack_main",
    )(q, k, v, do, gains)


def pack_share_kernel(
    q_hbm, k_hbm, v_hbm, do_hbm, row_ref, share_ref, give_ref, q_ref, k_ref, v_ref, do_ref, sems
):
    pairs = ((q_hbm, q_ref), (k_hbm, k_ref), (v_hbm, v_ref), (do_hbm, do_ref))
    last = pl.ds(SP * DH, EXTRA_HEADS * DH)
    copies = [
        pltpu.make_async_copy(src.at[:, :, last], dst, sems.at[i])
        for i, (src, dst) in enumerate(pairs)
    ]
    for copy in copies:
        copy.start()
    for copy in copies:
        copy.wait()
    q_row = row_ref[0:1]
    k_row = row_ref[1:2]
    core = core_index()

    def fill(out_ref, base, first_ref, second_ref, with_scales):
        for p in range(HALF):
            cols = slice(p // 2 * DH, (p // 2 + 1) * DH)
            half = slice(p % 2 * QHALF, (p % 2 + 1) * QHALF)
            out_ref[base + p, :TOK] = first_ref[0, :, cols]
            out_ref[base + p, TOK : TOK + QHALF] = second_ref[0, half, cols]
            if with_scales:
                q_own = jnp.concatenate([q_row[:, half]] * 2, axis=1)
                tail = stack_rows([*split3(q_own), *split3(k_row)], 16)
            else:
                tail = jnp.zeros((16, DH), bf16)
            out_ref[base + p, TOK + QHALF :] = tail

    @pl.when(core == 0)
    def _():
        fill(share_ref, 0, k_ref, q_ref, True)
        fill(give_ref, 0, v_ref, do_ref, False)

    @pl.when(core == 1)
    def _():
        fill(share_ref, HALF, v_ref, do_ref, False)
        fill(give_ref, 0, k_ref, q_ref, True)


def pack_share(q, k, v, do, rows):
    hbm = pl.BlockSpec(memory_space=pltpu.HBM)
    return pl.pallas_call(
        pack_share_kernel,
        in_specs=[hbm, hbm, hbm, hbm, pl.BlockSpec(memory_space=pltpu.VMEM)],
        scratch_shapes=[pltpu.VMEM((1, TOK, EXTRA_HEADS * DH), bf16)] * 4
        + [pltpu.SemaphoreType.DMA((4,))],
        out_shape=[
            jax.ShapeDtypeStruct((SP, SHARE_ROWS, DH), bf16),
            jax.ShapeDtypeStruct((HALF, SHARE_ROWS, DH), bf16),
        ],
        compiler_params=pltpu.CompilerParams(vmem_limit_bytes=60 * MIB),
        name="pack_share",
    )(q, k, v, do, rows)


def owner_slot(owner_ref, head):
    owner = owner_ref[head]
    slot = jnp.int32(0)
    for other in range(HEADS):
        same = (owner_ref[other] == owner) & (other < head)
        slot = slot + same.astype(jnp.int32)
    return owner, slot


def picked_gains(owner_ref, gain_ref, head):
    owner, slot = owner_slot(owner_ref, head)
    rows = gain_ref[owner].astype(f32)
    sums = []
    for which in range(2):
        both = []
        for s in range(2):
            at = 4 + (s * 2 + which) * 3
            both.append(rows[at : at + 1] + rows[at + 1 : at + 2] + rows[at + 2 : at + 3])
        sums.append(jnp.where(slot == 0, both[0], both[1]))
    return sums


def scale_columns(rows, at, parts):
    return sum(rows[:, at + i] for i in range(parts)).T


def largest_square(x):
    return jnp.max(contract(jnp.ones((8, DH), bf16), x * x, 1, 1))


def fold(x):
    return jnp.sum(x.reshape(x.shape[0] // 8, 8, x.shape[1]), axis=0)


def prepare_keys(key_at, k_cols, gain_k, kn_sc, kt_sc, bound_sm):
    for j in range(SP):
        r = slice(j * TOK, (j + 1) * TOK)
        kn_sc[r] = (key_at(j).astype(f32) * k_cols[:, j : j + 1] * gain_k).astype(bf16)
    bound_sm[0] = largest_square(kn_sc[...])
    kt_sc[...] = kn_sc[...].T


def soften(qn_sc, do, value_at, kn_sc, e_sc, dp_sc, stat_sc, bound_sm):
    qn = qn_sc[...]
    square = largest_square(qn) * bound_sm[0]
    small = square * (SCORE_SCALE * SCORE_SCALE) <= SAFE * SAFE

    def run(top):
        total = delta = None
        for c in range(SEQ // CHUNK):
            r = slice(c * CHUNK, (c + 1) * CHUNK)
            s = contract(kn_sc[r], qn, 1, 1) * (SCORE_SCALE * LOG2E)
            e = jnp.exp2(s if top is None else s - top)
            e_sc[r] = e
            dp = contract(value_at(c), do, 1, 1)
            dp_sc[r] = dp
            total = fold(e) if total is None else total + fold(e)
            delta = fold(e * dp) if delta is None else delta + fold(e * dp)
        inv = 1.0 / jnp.sum(total, axis=0, keepdims=True)
        stat_sc[0:1] = inv
        stat_sc[1:2] = jnp.sum(delta, axis=0, keepdims=True) * inv

    @pl.when(small)
    def _():
        run(None)

    @pl.when(jnp.logical_not(small))
    def _():
        top = None
        for c in range(SEQ // CHUNK):
            r = slice(c * CHUNK, (c + 1) * CHUNK)
            s = contract(kn_sc[r], qn, 1, 1) * (SCORE_SCALE * LOG2E)
            part = jnp.max(s.reshape(CHUNK // 8, 8, s.shape[1]), axis=0)
            top = part if top is None else jnp.maximum(top, part)
        run(jnp.max(top, axis=0, keepdims=True))


def gradients(qn_sc, do, kt_sc, e_sc, dp_sc, stat_sc, store):
    qn = qn_sc[...]
    inv = stat_sc[0:1]
    delta = stat_sc[1:2]
    dq_t = None
    for c in range(SEQ // CHUNK):
        r = slice(c * CHUNK, (c + 1) * CHUNK)
        p = e_sc[r] * inv
        ds = (p * (dp_sc[r] - delta)).astype(bf16)
        store(r, contract(ds, qn, 1, 0), contract(p.astype(bf16), do, 1, 0))
        part = contract(kt_sc[:, r], ds, 1, 0)
        dq_t = part if dq_t is None else dq_t + part
    return dq_t.T * SCORE_SCALE


def attention_scratch(query_rows):
    return [
        pltpu.VMEM((SEQ, query_rows), f32),
        pltpu.VMEM((SEQ, query_rows), f32),
        pltpu.VMEM((8, query_rows), f32),
        pltpu.SMEM((1,), f32),
        pltpu.VMEM((SEQ, DH), bf16),
        pltpu.VMEM((DH, SEQ), bf16),
        pltpu.VMEM((SEQ, DH), f32),
        pltpu.VMEM((SEQ, DH), f32),
        pltpu.VMEM((query_rows, DH), bf16),
        pltpu.VMEM((query_rows, DH), f32),
    ]


def cost(query_rows):
    work = query_rows * SEQ
    return pl.CostEstimate(flops=10 * DH * work, bytes_accessed=4 * 2**20, transcendentals=work)


STEPS = 2


def main_kernel(
    owner_ref, field_hbm, back_hbm, part_ref, extra_ref, field_ref, back_ref, in_sems, sems, qg_acc,
    e_sc, dp_sc, stat_sc, bound_sm, kn_sc, kt_sc, dk_acc, dv_acc, qn_sc, qu_sc,
):
    sources = SP // STEPS
    rows = sources * TOK
    blocks = CHUNK // TOK

    def fetch(part, rows):
        at = (slice(None), pl.ds(part * TOK, rows))
        return pltpu.make_async_copy(field_hbm.at[at], field_ref.at[at], in_sems.at[part])

    fetches = [fetch(part, TOK) for part in range(4)] + [fetch(4, 16)]
    for part in (4, 1, 0, 2, 3):
        fetches[part].start()
    fetches[4].wait()
    extra_ref[...] = field_ref[:, 4 * TOK :]
    gain_q, gain_k = picked_gains(owner_ref, field_ref.at[:, 4 * TOK :], lax.axis_index("sp"))
    scales = field_ref[:, 4 * TOK :].astype(f32)
    q_cols = scale_columns(scales, 0, 2)
    k_cols = scale_columns(scales, 2, 2)
    qg_acc[...] = jnp.zeros_like(qg_acc)

    def key_at(j):
        return field_ref[j, TOK : 2 * TOK]

    def value_at(c):
        return field_ref[c * blocks : (c + 1) * blocks, 2 * TOK : 3 * TOK].reshape(CHUNK, DH)

    fetches[1].wait()

    def query_copy(step):
        at = (pl.ds(step * sources, sources), pl.ds(2 * TOK, TOK))
        return pltpu.make_async_copy(back_ref.at[at], back_hbm.at[at], sems.at[step])

    def key_copy(j):
        at = (j, pl.ds(0, 2 * TOK))
        return pltpu.make_async_copy(back_ref.at[at], back_hbm.at[at], sems.at[STEPS + j])

    prepare_keys(key_at, k_cols, gain_k, kn_sc, kt_sc, bound_sm)
    dk_acc[...] = jnp.zeros_like(dk_acc)
    dv_acc[...] = jnp.zeros_like(dv_acc)

    for part in (0, 2, 3):
        fetches[part].wait()

    @pl.loop(0, STEPS)
    def _(step):
        for b in range(STEPS):

            @pl.when(step == b)
            def _():
                for j in range(sources):
                    at = b * sources + j
                    r = slice(j * TOK, (j + 1) * TOK)
                    unit = field_ref[at, :TOK].astype(f32) * q_cols[:, at : at + 1]
                    qu_sc[r] = unit
                    qn_sc[r] = (unit * gain_q).astype(bf16)

        mine = pl.ds(step * sources, sources)
        do = field_ref[mine, 3 * TOK : 4 * TOK].reshape(rows, DH)
        soften(qn_sc, do, value_at, kn_sc, e_sc, dp_sc, stat_sc, bound_sm)

        def store(r, dk_part, dv_part):
            dk_acc[r] += dk_part
            dv_acc[r] += dv_part

        dq = gradients(qn_sc, do, kt_sc, e_sc, dp_sc, stat_sc, store)
        back_ref[mine, 2 * TOK :] = (dq * gain_q).astype(bf16).reshape(sources, TOK, DH)
        query_copy(step).start()
        qg_acc[...] += fold(dq * qu_sc[...])

    key_part = jnp.zeros((8, DH), f32)
    for j in range(SP):
        r = slice(j * TOK, (j + 1) * TOK)
        dk = dk_acc[r] * SCORE_SCALE
        key_part += fold(dk * (key_at(j).astype(f32) * k_cols[:, j : j + 1]))
        back_ref[j, :TOK] = (dk * gain_k).astype(bf16)
        back_ref[j, TOK : 2 * TOK] = dv_acc[r].astype(bf16)
        key_copy(j).start()
    part_ref[0:1] = jnp.sum(qg_acc[...], axis=0, keepdims=True)
    part_ref[1:2] = jnp.sum(key_part, axis=0, keepdims=True)
    for step in range(STEPS):
        query_copy(step).wait()
    for j in range(SP):
        key_copy(j).wait()


def main_heads(owner, field):
    return pl.pallas_call(
        main_kernel,
        in_specs=[
            pl.BlockSpec(memory_space=pltpu.SMEM),
            pl.BlockSpec(memory_space=pl.ANY),
        ],
        out_shape=[
            jax.ShapeDtypeStruct((SP, MAIN_BACK, DH), bf16),
            jax.ShapeDtypeStruct((2, DH), f32),
            jax.ShapeDtypeStruct((SP, 16, DH), bf16),
        ],
        out_specs=[
            pl.BlockSpec(memory_space=pltpu.HBM),
            pl.BlockSpec(memory_space=pltpu.VMEM),
            pl.BlockSpec(memory_space=pltpu.VMEM),
        ],
        scratch_shapes=[
            pltpu.VMEM((SP, MAIN_ROWS, DH), bf16),
            pltpu.VMEM((SP, MAIN_BACK, DH), bf16),
            pltpu.SemaphoreType.DMA((5,)),
            pltpu.SemaphoreType.DMA((STEPS + SP,)),
            pltpu.VMEM((8, DH), f32),
        ]
        + attention_scratch(SEQ // STEPS),
        compiler_params=pltpu.CompilerParams(vmem_limit_bytes=53760 * 1024),
        cost_estimate=cost(SEQ),
        name="main_heads",
    )(owner, field)


def shared_kernel(
    owner_ref, extra_ref, mine_ref, other_ref, keep_ref, give_ref, part_ref,
    kq_ref, vd_ref, v_sc,
    e_sc, dp_sc, stat_sc, bound_sm, kn_sc, kt_sc, dk_acc, dv_acc, qn_sc, qu_sc,
):
    core = core_index()

    def load(kq_src, vd_src):
        kq_ref[...] = kq_src[...]
        vd_ref[...] = vd_src[...]

    @pl.when(core == 0)
    def _():
        load(mine_ref, other_ref)

    @pl.when(core == 1)
    def _():
        load(other_ref, mine_ref)

    head = SP + lax.rem(lax.axis_index("sp") // 2, EXTRA_HEADS)
    gain_q, gain_k = picked_gains(owner_ref, extra_ref, head)
    scales = kq_ref[:, TOK + QHALF :].astype(f32)
    q_cols = scale_columns(scales, 0, 3)
    q_cols = jnp.where(core == 0, q_cols[:QTOK], q_cols[QTOK:QHALF])
    k_cols = scale_columns(scales, 3, 3)
    prepare_keys(lambda j: kq_ref[j, :TOK], k_cols, gain_k, kn_sc, kt_sc, bound_sm)

    def quarter(ref):
        low = ref[:, TOK : TOK + QTOK]
        high = ref[:, TOK + QTOK : TOK + QHALF]
        return jnp.where(core == 0, low, high)

    q = quarter(kq_ref)
    do = quarter(vd_ref).reshape(SP * QTOK, DH)
    for j in range(SP):
        r = slice(j * QTOK, (j + 1) * QTOK)
        unit = q[j].astype(f32) * q_cols[:, j : j + 1]
        qu_sc[r] = unit
        qn_sc[r] = (unit * gain_q).astype(bf16)
        v_sc[j * TOK : (j + 1) * TOK] = vd_ref[j, :TOK]
    soften(qn_sc, do, lambda c: v_sc[c * CHUNK : (c + 1) * CHUNK], kn_sc, e_sc, dp_sc, stat_sc, bound_sm)

    def store(r, dk_part, dv_part):
        dk_acc[r] = dk_part
        dv_acc[r] = dv_part

    dq = gradients(qn_sc, do, kt_sc, e_sc, dp_sc, stat_sc, store)
    keep_ref[:, TOK : TOK + QTOK] = (dq * gain_q).astype(bf16).reshape(SP, QTOK, DH)
    keep_ref[:, TOK + QTOK :] = jnp.zeros((SP, 16, DH), bf16)
    key_part = jnp.zeros((8, DH), f32)
    for j in range(SP):
        r = slice(j * TOK, (j + 1) * TOK)
        dk = dk_acc[r] * SCORE_SCALE
        key_part += fold(dk * (kq_ref[j, :TOK].astype(f32) * k_cols[:, j : j + 1]))
        dk = (dk * gain_k).astype(bf16)
        dv = dv_acc[r].astype(bf16)

        keep_ref[j, :TOK] = jnp.where(core == 0, dk, dv)
        give_ref[j] = jnp.where(core == 0, dv, dk)
    part_ref[0:1] = jnp.sum(fold(dq * qu_sc[...]), axis=0, keepdims=True)
    part_ref[1:2] = jnp.sum(key_part, axis=0, keepdims=True)


def shared_heads(owner, extra, mine, other):
    vmem = pl.BlockSpec(memory_space=pltpu.VMEM)
    return pl.pallas_call(
        shared_kernel,
        in_specs=[
            pl.BlockSpec(memory_space=pltpu.SMEM),
            vmem,
            vmem,
            vmem,
        ],
        out_shape=[
            jax.ShapeDtypeStruct((SP, SHARE_BACK, DH), bf16),
            jax.ShapeDtypeStruct((SP, TOK, DH), bf16),
            jax.ShapeDtypeStruct((2, DH), f32),
        ],
        scratch_shapes=[
            pltpu.VMEM((SP, SHARE_ROWS, DH), bf16),
            pltpu.VMEM((SP, SHARE_ROWS, DH), bf16),
            pltpu.VMEM((SEQ, DH), bf16),
        ]
        + attention_scratch(SP * QTOK),
        compiler_params=pltpu.CompilerParams(vmem_limit_bytes=40 * MIB),
        cost_estimate=cost(SP * QTOK),
        name="shared_heads",
    )(owner, extra, mine, other)


LAST = slice(SP * DH, INNER)


def unpack_main_kernel(q_ref, k_ref, main_ref, dq_ref, dk_ref, gv_ref, sum_ref):
    for d in range(SP):
        cols = slice(d * DH, (d + 1) * DH)
        dk_ref[:, cols] = main_ref[d, :TOK]
        gv_ref[0, :, cols] = main_ref[d, TOK : 2 * TOK]
        dq_ref[:, cols] = main_ref[d, 2 * TOK : 3 * TOK]
    for i, (raw_ref, grad_ref) in enumerate(((q_ref, dq_ref), (k_ref, dk_ref))):
        raw = raw_ref[0].astype(f32)
        squares = jnp.sum(raw * raw, axis=-1, keepdims=True)
        inner = jnp.sum(
            grad_ref[...].astype(f32) * raw[:, : SP * DH], axis=-1, keepdims=True
        )
        sum_ref[2 * i] = jnp.broadcast_to(squares, (TOK, DH))
        sum_ref[2 * i + 1] = jnp.broadcast_to(inner, (TOK, DH))


def unpack_main(q, k, main_back):
    return pl.pallas_call(
        unpack_main_kernel,
        out_shape=[
            jax.ShapeDtypeStruct((TOK, SP * DH), bf16),
            jax.ShapeDtypeStruct((TOK, SP * DH), bf16),
            jax.ShapeDtypeStruct((1, TOK, SP * DH), bf16),
            jax.ShapeDtypeStruct((4, TOK, DH), f32),
        ],
        compiler_params=pltpu.CompilerParams(vmem_limit_bytes=UNPACK_LIMIT),
        name="unpack_main",
    )(q, k, main_back)


def unpack_kernel(
    owner_ref, q_ref, k_ref, dq_ref, dk_ref, gvm_ref, sum_ref, share_ref, other_ref,
    gq_hbm, gk_hbm, gv_hbm, gain_ref, gq_sc, gk_sc, gv_sc, dqx_sc, dkx_sc, sems,
):
    main_cols = pl.ds(0, SP * DH)
    last_cols = pl.ds(SP * DH, EXTRA_HEADS * DH)
    out_copies = [
        pltpu.make_async_copy(gvm_ref, gv_hbm.at[:, :, main_cols], sems.at[0]),
        pltpu.make_async_copy(gv_sc, gv_hbm.at[:, :, last_cols], sems.at[1]),
        pltpu.make_async_copy(gq_sc, gq_hbm, sems.at[2]),
        pltpu.make_async_copy(gk_sc, gk_hbm, sems.at[3]),
    ]
    out_copies[0].start()
    core = core_index()

    def take(base, first_ref, second_ref):
        for g in range(EXTRA_HEADS):
            cols = slice(g * DH, (g + 1) * DH)
            x = base + 2 * g

            def both(ref):
                return (ref[x, :TOK].astype(f32) + ref[x + 1, :TOK].astype(f32)).astype(bf16)

            dkx_sc[:, cols] = both(first_ref)
            gv_sc[0, :, cols] = both(second_ref)
            for half in range(2):
                for c, ref in enumerate((first_ref, second_ref)):
                    at = (2 * half + c) * QTOK
                    dqx_sc[at : at + QTOK, cols] = ref[x + half, TOK : TOK + QTOK]

    @pl.when(core == 0)
    def _():
        take(0, share_ref, other_ref)

    @pl.when(core == 1)
    def _():
        take(HALF, other_ref, share_ref)

    out_copies[1].start()
    for i, (raw_ref, grad_ref, more_ref, out_ref) in enumerate(
        ((q_ref, dq_ref, dqx_sc, gq_sc), (k_ref, dk_ref, dkx_sc, gk_sc))
    ):
        scale = lax.rsqrt(sum_ref[2 * i] * (1.0 / INNER) + EPSILON)[:, :1]
        raw_last = raw_ref[0, :, LAST].astype(f32)
        grad_last = more_ref[...].astype(f32)
        inner = sum_ref[2 * i + 1][:, :1] + jnp.sum(grad_last * raw_last, axis=-1, keepdims=True)
        back = scale * scale * scale * (1.0 / INNER) * inner
        out_ref[0, :, LAST] = (scale * grad_last - back * raw_last).astype(bf16)
        raw = raw_ref[0, :, : SP * DH].astype(f32)
        out_ref[0, :, : SP * DH] = (scale * grad_ref[...].astype(f32) - back * raw).astype(bf16)
        out_copies[2 + i].start()
    me = lax.axis_index("sp")
    sums = [jnp.zeros((2, DH), f32) for _ in range(2)]
    at = TOK + QTOK
    for head in range(HEADS):
        owner, slot = owner_slot(owner_ref, head)
        members = [(head, 0)] if head < SP else [
            (2 * (head - SP) + d, 1) for d in (0, 1, HALF, HALF + 1)
        ]
        value = jnp.zeros((2, DH), f32)
        for d, kind in members:
            rows = share_ref[d, at : at + 16].astype(f32)
            base = kind * 6
            value += jnp.concatenate(
                [
                    rows[base + 3 * w : base + 3 * w + 1]
                    + rows[base + 3 * w + 1 : base + 3 * w + 2]
                    + rows[base + 3 * w + 2 : base + 3 * w + 3]
                    for w in range(2)
                ],
                axis=0,
            )
        for s in range(2):
            sums[s] = sums[s] + jnp.where((owner == me) & (slot == s), value, 0.0)
    factor = 1.0 / math.sqrt(SP * SEQ)
    for s in range(2):
        gain_ref[0, s] = sums[s] * factor
    for copy in out_copies:
        copy.wait()


def unpack(owner, q, k, dq, dk, gv, sums, share_back, other_back):
    vmem = pl.BlockSpec(memory_space=pltpu.VMEM)
    hbm = pl.BlockSpec(memory_space=pltpu.HBM)
    return pl.pallas_call(
        unpack_kernel,
        in_specs=[pl.BlockSpec(memory_space=pltpu.SMEM)] + [vmem] * 8,
        out_specs=[hbm, hbm, hbm, vmem],
        out_shape=[
            jax.ShapeDtypeStruct((1, TOK, INNER), bf16),
            jax.ShapeDtypeStruct((1, TOK, INNER), bf16),
            jax.ShapeDtypeStruct((1, TOK, INNER), bf16),
            jax.ShapeDtypeStruct((1, 2, 2, DH), f32),
        ],
        scratch_shapes=[
            pltpu.VMEM((1, TOK, INNER), bf16),
            pltpu.VMEM((1, TOK, INNER), bf16),
            pltpu.VMEM((1, TOK, EXTRA_HEADS * DH), bf16),
            pltpu.VMEM((TOK, EXTRA_HEADS * DH), bf16),
            pltpu.VMEM((TOK, EXTRA_HEADS * DH), bf16),
            pltpu.SemaphoreType.DMA((4,)),
        ],
        compiler_params=pltpu.CompilerParams(vmem_limit_bytes=UNPACK_LIMIT),
        name="unpack",
    )(owner, q, k, dq, dk, gv, sums, share_back, other_back)


def add_pair_kernel(keep_ref, got_ref, x_ref, out_ref, same_ref):
    same_ref[...] = x_ref[...]
    for d in range(SP):
        total = keep_ref[d, :TOK].astype(f32) + got_ref[d].astype(f32)
        out_ref[d, :TOK] = total.astype(bf16)
        out_ref[d, TOK:] = keep_ref[d, TOK:]


def add_pair(keep, got, x):
    vmem = pl.BlockSpec(memory_space=pltpu.VMEM)
    return pl.pallas_call(
        add_pair_kernel,
        in_specs=[vmem, vmem, vmem],
        out_shape=[
            jax.ShapeDtypeStruct((SP, SHARE_BACK, DH), bf16),
            jax.ShapeDtypeStruct(x.shape, x.dtype),
        ],
        compiler_params=pltpu.CompilerParams(vmem_limit_bytes=40 * MIB),
        name="add_pair",
    )(keep, got, x)


def add_sums_kernel(sum_ref, pair_ref, after_ref, out_ref):
    rows = []
    for i in range(4):
        rows += [*split3(sum_ref[i : i + 1])]
    extra = stack_rows(rows, 16)
    for d in range(SP):
        out_ref[d, TOK + QTOK :] = extra


def add_sums(sums, pair, after):
    vmem = pl.BlockSpec(memory_space=pltpu.VMEM)
    return pl.pallas_call(
        add_sums_kernel,
        in_specs=[vmem, vmem, pl.BlockSpec(memory_space=pl.ANY)],
        out_specs=vmem,
        out_shape=jax.ShapeDtypeStruct((SP, SHARE_BACK, DH), bf16),
        input_output_aliases={1: 0},
        compiler_params=pltpu.CompilerParams(vmem_limit_bytes=40 * MIB),
        name="add_sums",
    )(sums, pair, after)


def after_kernel(x_ref, before_ref, out_ref):
    pass


def after(x, before):
    anywhere = pl.BlockSpec(memory_space=pl.ANY)
    return pl.pallas_call(
        after_kernel,
        in_specs=[anywhere, anywhere],
        out_specs=anywhere,
        out_shape=jax.ShapeDtypeStruct(x.shape, x.dtype),
        input_output_aliases={0: 0},
        compiler_params=pltpu.CompilerParams(vmem_limit_bytes=40 * MIB),
        name="after",
    )(x, before)


def swap(x):
    return lax.ppermute(x, "fsdp", [(i, i ^ 1) for i in range(16)])


def exchange(field):
    return lax.all_to_all(field, "sp", split_axis=0, concat_axis=0, tiled=True)


def fsdp_sum(x, steps):
    across = (6, 7, 4, 5, 2, 3, 0, 1)
    partners = [
        [i ^ 1 for i in range(16)],
        [i ^ 2 for i in range(16)],
        [i ^ 4 for i in range(16)],
        [across[i // 2] * 2 + i % 2 for i in range(16)],
    ]
    for partner in partners[steps]:
        x = x + lax.ppermute(x, "fsdp", list(enumerate(partner)))
    return x


def per_device(query_raw, key_raw, value_in, grad_out, norm_gains, head_owner):
    main_send, rows = pack_main(query_raw, key_raw, value_in, grad_out, norm_gains)
    share_half, give = pack_share(query_raw, key_raw, value_in, grad_out, rows)
    main = exchange(main_send)
    other_half = (1 - core_index()) * HALF
    nothing = main[0, 4 * TOK, 0] * 0
    share_send = lax.dynamic_update_slice(share_half, swap(give) + nothing, (other_half, 0, 0))
    share = exchange(share_send)
    main_out, part, extra = main_heads(head_owner, main)
    main_back = exchange(main_out)
    share = after(share, part)
    keep, give_back, part_s = shared_heads(head_owner, extra, share, swap(share))
    sums = fsdp_sum(jnp.concatenate([part, part_s], axis=0), slice(0, 2))
    pair, sums = add_pair(keep, swap(give_back), sums)
    sums = fsdp_sum(sums, slice(2, 4))
    share_back = exchange(add_sums(sums, pair, main_back))
    parts = unpack_main(query_raw, key_raw, main_back)
    return tuple(
        unpack(head_owner, query_raw, key_raw, *parts, share_back, swap(share_back))
    )


def solution(mesh):
    return jax.shard_map(
        per_device,
        mesh=mesh,
        in_specs=(
            P("fsdp", "sp", None),
            P("fsdp", "sp", None),
            P("fsdp", "sp", None),
            P("fsdp", "sp", None),
            P("sp", None, None, None),
            P(),
        ),
        out_specs=(
            P("fsdp", "sp", None),
            P("fsdp", "sp", None),
            P("fsdp", "sp", None),
            P("sp", None, None, None),
        ),
        check_vma=False,
    )
```

```python
import functools
import math

import jax
import jax.numpy as jnp
from jax import lax
from jax.experimental import pallas as pl
from jax.experimental.pallas import tpu as pltpu
from jax.sharding import PartitionSpec as P

EPSILON = 1e-06
LOG2E = math.log2(math.e)
f32 = jnp.float32
bf16 = jnp.bfloat16

HEADS = 20
DH = 128
INNER = HEADS * DH
SP = 16
TOK = 128
SEQ = SP * TOK
EXTRA_HEADS = HEADS - SP
HALF = SP // 2
QHALF = TOK // 2
QTOK = TOK // 4
MAIN_ROWS = 4 * TOK + 16
SHARE_ROWS = TOK + QHALF + 16
MAIN_BACK = 3 * TOK
SHARE_BACK = TOK + QTOK + 16
MIB = 2**20
UNPACK_LIMIT = 48 * 1024 * 1024
SCORE_SCALE = DH**-0.5
SAFE = 60.0
CHUNK = 256


def core_index():
    return lax.rem(lax.axis_index("fsdp"), 2)


def split3(x):
    hi = x.astype(bf16).astype(f32)
    mid = (x - hi).astype(bf16).astype(f32)
    return hi, mid, x - hi - mid


def split2(x):
    hi = x.astype(bf16).astype(f32)
    return hi, x - hi


def stack_rows(rows, count):
    if len(rows) < count:
        rows = rows + [jnp.zeros((count - len(rows), rows[0].shape[-1]), f32)]
    return jnp.concatenate(rows, axis=0).astype(bf16)


def contract(a, b, da, db):
    return lax.dot_general(a, b, (((da,), (db,)), ((), ())), preferred_element_type=f32)


def row_scale(raw):
    return lax.rsqrt(jnp.sum(raw * raw, axis=-1, keepdims=True) * (1.0 / INNER) + EPSILON)


def to_row(column):
    return jnp.broadcast_to(column, (TOK, TOK)).T[0:1]


def pack_main_kernel(
    q_hbm, k_hbm, v_hbm, do_hbm, gain_ref, main_ref, row_ref, q_ref, k_ref, v_ref, do_ref, sems
):
    pairs = ((q_hbm, q_ref), (k_hbm, k_ref), (v_hbm, v_ref), (do_hbm, do_ref))
    copies = [
        pltpu.make_async_copy(src, dst, sems.at[i]) for i, (src, dst) in enumerate(pairs)
    ]
    for copy in copies:
        copy.start()
    copies[0].wait()
    q_row = to_row(row_scale(q_ref[0].astype(f32)))
    copies[1].wait()
    k_row = to_row(row_scale(k_ref[0].astype(f32)))
    row_ref[0:1] = q_row
    row_ref[1:2] = k_row
    gains = gain_ref[0]
    rows = [*split2(q_row), *split2(k_row)]
    for slot in range(2):
        for which in range(2):
            rows += [*split3(gains[slot, which : which + 1])]
    extra = stack_rows(rows, 16)
    copies[2].wait()
    copies[3].wait()
    for d in range(SP):
        cols = slice(d * DH, (d + 1) * DH)
        for part, ref in enumerate((q_ref, k_ref, v_ref, do_ref)):
            main_ref[d, part * TOK : (part + 1) * TOK] = ref[0, :, cols]
        main_ref[d, 4 * TOK :] = extra


def pack_main(q, k, v, do, gains):
    hbm = pl.BlockSpec(memory_space=pltpu.HBM)
    return pl.pallas_call(
        pack_main_kernel,
        in_specs=[hbm, hbm, hbm, hbm, pl.BlockSpec(memory_space=pltpu.VMEM)],
        scratch_shapes=[pltpu.VMEM((1, TOK, INNER), bf16)] * 4 + [pltpu.SemaphoreType.DMA((4,))],
        out_shape=[
            jax.ShapeDtypeStruct((SP, MAIN_ROWS, DH), bf16),
            jax.ShapeDtypeStruct((8, DH), f32),
        ],
        compiler_params=pltpu.CompilerParams(vmem_limit_bytes=60 * MIB),
        name="pack_main",
    )(q, k, v, do, gains)


def pack_share_kernel(
    q_hbm, k_hbm, v_hbm, do_hbm, row_ref, share_ref, give_ref, q_ref, k_ref, v_ref, do_ref, sems
):
    pairs = ((q_hbm, q_ref), (k_hbm, k_ref), (v_hbm, v_ref), (do_hbm, do_ref))
    last = pl.ds(SP * DH, EXTRA_HEADS * DH)
    copies = [
        pltpu.make_async_copy(src.at[:, :, last], dst, sems.at[i])
        for i, (src, dst) in enumerate(pairs)
    ]
    for copy in copies:
        copy.start()
    for copy in copies:
        copy.wait()
    q_row = row_ref[0:1]
    k_row = row_ref[1:2]
    core = core_index()

    def fill(out_ref, base, first_ref, second_ref, with_scales):
        for p in range(HALF):
            cols = slice(p // 2 * DH, (p // 2 + 1) * DH)
            half = slice(p % 2 * QHALF, (p % 2 + 1) * QHALF)
            out_ref[base + p, :TOK] = first_ref[0, :, cols]
            out_ref[base + p, TOK : TOK + QHALF] = second_ref[0, half, cols]
            if with_scales:
                q_own = jnp.concatenate([q_row[:, half]] * 2, axis=1)
                tail = stack_rows([*split3(q_own), *split3(k_row)], 16)
            else:
                tail = jnp.zeros((16, DH), bf16)
            out_ref[base + p, TOK + QHALF :] = tail

    @pl.when(core == 0)
    def _():
        fill(share_ref, 0, k_ref, q_ref, True)
        fill(give_ref, 0, v_ref, do_ref, False)

    @pl.when(core == 1)
    def _():
        fill(share_ref, HALF, v_ref, do_ref, False)
        fill(give_ref, 0, k_ref, q_ref, True)


def pack_share(q, k, v, do, rows):
    hbm = pl.BlockSpec(memory_space=pltpu.HBM)
    return pl.pallas_call(
        pack_share_kernel,
        in_specs=[hbm, hbm, hbm, hbm, pl.BlockSpec(memory_space=pltpu.VMEM)],
        scratch_shapes=[pltpu.VMEM((1, TOK, EXTRA_HEADS * DH), bf16)] * 4
        + [pltpu.SemaphoreType.DMA((4,))],
        out_shape=[
            jax.ShapeDtypeStruct((SP, SHARE_ROWS, DH), bf16),
            jax.ShapeDtypeStruct((HALF, SHARE_ROWS, DH), bf16),
        ],
        compiler_params=pltpu.CompilerParams(vmem_limit_bytes=60 * MIB),
        name="pack_share",
    )(q, k, v, do, rows)


def owner_slot(owner_ref, head):
    owner = owner_ref[head]
    slot = jnp.int32(0)
    for other in range(HEADS):
        same = (owner_ref[other] == owner) & (other < head)
        slot = slot + same.astype(jnp.int32)
    return owner, slot


def picked_gains(owner_ref, gain_ref, head):
    owner, slot = owner_slot(owner_ref, head)
    rows = gain_ref[owner].astype(f32)
    sums = []
    for which in range(2):
        both = []
        for s in range(2):
            at = 4 + (s * 2 + which) * 3
            both.append(rows[at : at + 1] + rows[at + 1 : at + 2] + rows[at + 2 : at + 3])
        sums.append(jnp.where(slot == 0, both[0], both[1]))
    return sums


def scale_columns(rows, at, parts):
    return sum(rows[:, at + i] for i in range(parts)).T


def largest_square(x):
    return jnp.max(contract(jnp.ones((8, DH), bf16), x * x, 1, 1))


def fold(x):
    return jnp.sum(x.reshape(x.shape[0] // 8, 8, x.shape[1]), axis=0)


def prepare_keys(key_at, k_cols, gain_k, kn_sc, kt_sc, bound_sm):
    for j in range(SP):
        r = slice(j * TOK, (j + 1) * TOK)
        kn_sc[r] = (key_at(j).astype(f32) * k_cols[:, j : j + 1] * gain_k).astype(bf16)
    bound_sm[0] = largest_square(kn_sc[...])
    kt_sc[...] = kn_sc[...].T


def soften(qn_sc, do, value_at, kn_sc, e_sc, dp_sc, stat_sc, bound_sm):
    qn = qn_sc[...]
    square = largest_square(qn) * bound_sm[0]
    small = square * (SCORE_SCALE * SCORE_SCALE) <= SAFE * SAFE

    def run(top):
        total = delta = None
        for c in range(SEQ // CHUNK):
            r = slice(c * CHUNK, (c + 1) * CHUNK)
            s = contract(kn_sc[r], qn, 1, 1) * (SCORE_SCALE * LOG2E)
            e = jnp.exp2(s if top is None else s - top)
            e_sc[r] = e
            dp = contract(value_at(c), do, 1, 1)
            dp_sc[r] = dp
            total = fold(e) if total is None else total + fold(e)
            delta = fold(e * dp) if delta is None else delta + fold(e * dp)
        inv = 1.0 / jnp.sum(total, axis=0, keepdims=True)
        stat_sc[0:1] = inv
        stat_sc[1:2] = jnp.sum(delta, axis=0, keepdims=True) * inv

    @pl.when(small)
    def _():
        run(None)

    @pl.when(jnp.logical_not(small))
    def _():
        top = None
        for c in range(SEQ // CHUNK):
            r = slice(c * CHUNK, (c + 1) * CHUNK)
            s = contract(kn_sc[r], qn, 1, 1) * (SCORE_SCALE * LOG2E)
            part = jnp.max(s.reshape(CHUNK // 8, 8, s.shape[1]), axis=0)
            top = part if top is None else jnp.maximum(top, part)
        run(jnp.max(top, axis=0, keepdims=True))


def gradients(qn_sc, do, kt_sc, e_sc, dp_sc, stat_sc, store):
    qn = qn_sc[...]
    inv = stat_sc[0:1]
    delta = stat_sc[1:2]
    dq_t = None
    for c in range(SEQ // CHUNK):
        r = slice(c * CHUNK, (c + 1) * CHUNK)
        p = e_sc[r] * inv
        ds = (p * (dp_sc[r] - delta)).astype(bf16)
        store(r, contract(ds, qn, 1, 0), contract(p.astype(bf16), do, 1, 0))
        part = contract(kt_sc[:, r], ds, 1, 0)
        dq_t = part if dq_t is None else dq_t + part
    return dq_t.T * SCORE_SCALE


def attention_scratch(query_rows):
    return [
        pltpu.VMEM((SEQ, query_rows), f32),
        pltpu.VMEM((SEQ, query_rows), f32),
        pltpu.VMEM((8, query_rows), f32),
        pltpu.SMEM((1,), f32),
        pltpu.VMEM((SEQ, DH), bf16),
        pltpu.VMEM((DH, SEQ), bf16),
        pltpu.VMEM((SEQ, DH), f32),
        pltpu.VMEM((SEQ, DH), f32),
        pltpu.VMEM((query_rows, DH), bf16),
        pltpu.VMEM((query_rows, DH), f32),
    ]


def cost(query_rows):
    work = query_rows * SEQ
    return pl.CostEstimate(flops=10 * DH * work, bytes_accessed=4 * 2**20, transcendentals=work)


STEPS = 2


def main_kernel(
    owner_ref, field_hbm, back_hbm, part_ref, extra_ref, field_ref, back_ref, in_sems, sems, qg_acc,
    e_sc, dp_sc, stat_sc, bound_sm, kn_sc, kt_sc, dk_acc, dv_acc, qn_sc, qu_sc,
):
    sources = SP // STEPS
    rows = sources * TOK
    blocks = CHUNK // TOK

    def fetch(part, rows):
        at = (slice(None), pl.ds(part * TOK, rows))
        return pltpu.make_async_copy(field_hbm.at[at], field_ref.at[at], in_sems.at[part])

    fetches = [fetch(part, TOK) for part in range(4)] + [fetch(4, 16)]
    for part in (4, 1, 0, 2, 3):
        fetches[part].start()
    fetches[4].wait()
    extra_ref[...] = field_ref[:, 4 * TOK :]
    gain_q, gain_k = picked_gains(owner_ref, field_ref.at[:, 4 * TOK :], lax.axis_index("sp"))
    scales = field_ref[:, 4 * TOK :].astype(f32)
    q_cols = scale_columns(scales, 0, 2)
    k_cols = scale_columns(scales, 2, 2)
    qg_acc[...] = jnp.zeros_like(qg_acc)

    def key_at(j):
        return field_ref[j, TOK : 2 * TOK]

    def value_at(c):
        return field_ref[c * blocks : (c + 1) * blocks, 2 * TOK : 3 * TOK].reshape(CHUNK, DH)

    fetches[1].wait()

    def query_copy(step):
        at = (pl.ds(step * sources, sources), pl.ds(2 * TOK, TOK))
        return pltpu.make_async_copy(back_ref.at[at], back_hbm.at[at], sems.at[step])

    def key_copy(j):
        at = (j, pl.ds(0, 2 * TOK))
        return pltpu.make_async_copy(back_ref.at[at], back_hbm.at[at], sems.at[STEPS + j])

    prepare_keys(key_at, k_cols, gain_k, kn_sc, kt_sc, bound_sm)
    dk_acc[...] = jnp.zeros_like(dk_acc)
    dv_acc[...] = jnp.zeros_like(dv_acc)

    for part in (0, 2, 3):
        fetches[part].wait()

    @pl.loop(0, STEPS)
    def _(step):
        for b in range(STEPS):

            @pl.when(step == b)
            def _():
                for j in range(sources):
                    at = b * sources + j
                    r = slice(j * TOK, (j + 1) * TOK)
                    unit = field_ref[at, :TOK].astype(f32) * q_cols[:, at : at + 1]
                    qu_sc[r] = unit
                    qn_sc[r] = (unit * gain_q).astype(bf16)

        mine = pl.ds(step * sources, sources)
        do = field_ref[mine, 3 * TOK : 4 * TOK].reshape(rows, DH)
        soften(qn_sc, do, value_at, kn_sc, e_sc, dp_sc, stat_sc, bound_sm)

        def store(r, dk_part, dv_part):
            dk_acc[r] += dk_part
            dv_acc[r] += dv_part

        dq = gradients(qn_sc, do, kt_sc, e_sc, dp_sc, stat_sc, store)
        back_ref[mine, 2 * TOK :] = (dq * gain_q).astype(bf16).reshape(sources, TOK, DH)
        query_copy(step).start()
        qg_acc[...] += fold(dq * qu_sc[...])

    key_part = jnp.zeros((8, DH), f32)
    for j in range(SP):
        r = slice(j * TOK, (j + 1) * TOK)
        dk = dk_acc[r] * SCORE_SCALE
        key_part += fold(dk * (key_at(j).astype(f32) * k_cols[:, j : j + 1]))
        back_ref[j, :TOK] = (dk * gain_k).astype(bf16)
        back_ref[j, TOK : 2 * TOK] = dv_acc[r].astype(bf16)
        key_copy(j).start()
    part_ref[0:1] = jnp.sum(qg_acc[...], axis=0, keepdims=True)
    part_ref[1:2] = jnp.sum(key_part, axis=0, keepdims=True)
    for step in range(STEPS):
        query_copy(step).wait()
    for j in range(SP):
        key_copy(j).wait()


def main_heads(owner, field):
    return pl.pallas_call(
        main_kernel,
        in_specs=[
            pl.BlockSpec(memory_space=pltpu.SMEM),
            pl.BlockSpec(memory_space=pl.ANY),
        ],
        out_shape=[
            jax.ShapeDtypeStruct((SP, MAIN_BACK, DH), bf16),
            jax.ShapeDtypeStruct((2, DH), f32),
            jax.ShapeDtypeStruct((SP, 16, DH), bf16),
        ],
        out_specs=[
            pl.BlockSpec(memory_space=pltpu.HBM),
            pl.BlockSpec(memory_space=pltpu.VMEM),
            pl.BlockSpec(memory_space=pltpu.VMEM),
        ],
        scratch_shapes=[
            pltpu.VMEM((SP, MAIN_ROWS, DH), bf16),
            pltpu.VMEM((SP, MAIN_BACK, DH), bf16),
            pltpu.SemaphoreType.DMA((5,)),
            pltpu.SemaphoreType.DMA((STEPS + SP,)),
            pltpu.VMEM((8, DH), f32),
        ]
        + attention_scratch(SEQ // STEPS),
        compiler_params=pltpu.CompilerParams(vmem_limit_bytes=53760 * 1024),
        cost_estimate=cost(SEQ),
        name="main_heads",
    )(owner, field)


def shared_kernel(
    owner_ref, extra_ref, mine_ref, other_ref, keep_ref, give_ref, part_ref,
    kq_ref, vd_ref, v_sc,
    e_sc, dp_sc, stat_sc, bound_sm, kn_sc, kt_sc, dk_acc, dv_acc, qn_sc, qu_sc,
):
    core = core_index()

    def load(kq_src, vd_src):
        kq_ref[...] = kq_src[...]
        vd_ref[...] = vd_src[...]

    @pl.when(core == 0)
    def _():
        load(mine_ref, other_ref)

    @pl.when(core == 1)
    def _():
        load(other_ref, mine_ref)

    head = SP + lax.rem(lax.axis_index("sp") // 2, EXTRA_HEADS)
    gain_q, gain_k = picked_gains(owner_ref, extra_ref, head)
    scales = kq_ref[:, TOK + QHALF :].astype(f32)
    q_cols = scale_columns(scales, 0, 3)
    q_cols = jnp.where(core == 0, q_cols[:QTOK], q_cols[QTOK:QHALF])
    k_cols = scale_columns(scales, 3, 3)
    prepare_keys(lambda j: kq_ref[j, :TOK], k_cols, gain_k, kn_sc, kt_sc, bound_sm)

    def quarter(ref):
        low = ref[:, TOK : TOK + QTOK]
        high = ref[:, TOK + QTOK : TOK + QHALF]
        return jnp.where(core == 0, low, high)

    q = quarter(kq_ref)
    do = quarter(vd_ref).reshape(SP * QTOK, DH)
    for j in range(SP):
        r = slice(j * QTOK, (j + 1) * QTOK)
        unit = q[j].astype(f32) * q_cols[:, j : j + 1]
        qu_sc[r] = unit
        qn_sc[r] = (unit * gain_q).astype(bf16)
        v_sc[j * TOK : (j + 1) * TOK] = vd_ref[j, :TOK]
    soften(qn_sc, do, lambda c: v_sc[c * CHUNK : (c + 1) * CHUNK], kn_sc, e_sc, dp_sc, stat_sc, bound_sm)

    def store(r, dk_part, dv_part):
        dk_acc[r] = dk_part
        dv_acc[r] = dv_part

    dq = gradients(qn_sc, do, kt_sc, e_sc, dp_sc, stat_sc, store)
    keep_ref[:, TOK : TOK + QTOK] = (dq * gain_q).astype(bf16).reshape(SP, QTOK, DH)
    keep_ref[:, TOK + QTOK :] = jnp.zeros((SP, 16, DH), bf16)
    key_part = jnp.zeros((8, DH), f32)
    for j in range(SP):
        r = slice(j * TOK, (j + 1) * TOK)
        dk = dk_acc[r] * SCORE_SCALE
        key_part += fold(dk * (kq_ref[j, :TOK].astype(f32) * k_cols[:, j : j + 1]))
        dk = (dk * gain_k).astype(bf16)
        dv = dv_acc[r].astype(bf16)

        keep_ref[j, :TOK] = jnp.where(core == 0, dk, dv)
        give_ref[j] = jnp.where(core == 0, dv, dk)
    part_ref[0:1] = jnp.sum(fold(dq * qu_sc[...]), axis=0, keepdims=True)
    part_ref[1:2] = jnp.sum(key_part, axis=0, keepdims=True)


def shared_heads(owner, extra, mine, other):
    vmem = pl.BlockSpec(memory_space=pltpu.VMEM)
    return pl.pallas_call(
        shared_kernel,
        in_specs=[
            pl.BlockSpec(memory_space=pltpu.SMEM),
            vmem,
            vmem,
            vmem,
        ],
        out_shape=[
            jax.ShapeDtypeStruct((SP, SHARE_BACK, DH), bf16),
            jax.ShapeDtypeStruct((SP, TOK, DH), bf16),
            jax.ShapeDtypeStruct((2, DH), f32),
        ],
        scratch_shapes=[
            pltpu.VMEM((SP, SHARE_ROWS, DH), bf16),
            pltpu.VMEM((SP, SHARE_ROWS, DH), bf16),
            pltpu.VMEM((SEQ, DH), bf16),
        ]
        + attention_scratch(SP * QTOK),
        compiler_params=pltpu.CompilerParams(vmem_limit_bytes=40 * MIB),
        cost_estimate=cost(SP * QTOK),
        name="shared_heads",
    )(owner, extra, mine, other)


LAST = slice(SP * DH, INNER)


def unpack_main_kernel(q_ref, k_ref, main_ref, dq_ref, dk_ref, gv_ref, sum_ref):
    for d in range(SP):
        cols = slice(d * DH, (d + 1) * DH)
        dk_ref[:, cols] = main_ref[d, :TOK]
        gv_ref[0, :, cols] = main_ref[d, TOK : 2 * TOK]
        dq_ref[:, cols] = main_ref[d, 2 * TOK : 3 * TOK]
    for i, (raw_ref, grad_ref) in enumerate(((q_ref, dq_ref), (k_ref, dk_ref))):
        raw = raw_ref[0].astype(f32)
        squares = jnp.sum(raw * raw, axis=-1, keepdims=True)
        inner = jnp.sum(
            grad_ref[...].astype(f32) * raw[:, : SP * DH], axis=-1, keepdims=True
        )
        sum_ref[2 * i] = jnp.broadcast_to(squares, (TOK, DH))
        sum_ref[2 * i + 1] = jnp.broadcast_to(inner, (TOK, DH))


def unpack_main(q, k, main_back):
    return pl.pallas_call(
        unpack_main_kernel,
        out_shape=[
            jax.ShapeDtypeStruct((TOK, SP * DH), bf16),
            jax.ShapeDtypeStruct((TOK, SP * DH), bf16),
            jax.ShapeDtypeStruct((1, TOK, SP * DH), bf16),
            jax.ShapeDtypeStruct((4, TOK, DH), f32),
        ],
        compiler_params=pltpu.CompilerParams(vmem_limit_bytes=UNPACK_LIMIT),
        name="unpack_main",
    )(q, k, main_back)


def unpack_kernel(
    owner_ref, q_ref, k_ref, dq_ref, dk_ref, gvm_ref, sum_ref, share_ref, other_ref,
    gq_hbm, gk_hbm, gv_hbm, gain_ref, gq_sc, gk_sc, gv_sc, dqx_sc, dkx_sc, sems,
):
    main_cols = pl.ds(0, SP * DH)
    last_cols = pl.ds(SP * DH, EXTRA_HEADS * DH)
    out_copies = [
        pltpu.make_async_copy(gvm_ref, gv_hbm.at[:, :, main_cols], sems.at[0]),
        pltpu.make_async_copy(gv_sc, gv_hbm.at[:, :, last_cols], sems.at[1]),
        pltpu.make_async_copy(gq_sc, gq_hbm, sems.at[2]),
        pltpu.make_async_copy(gk_sc, gk_hbm, sems.at[3]),
    ]
    out_copies[0].start()
    core = core_index()

    def take(base, first_ref, second_ref):
        for g in range(EXTRA_HEADS):
            cols = slice(g * DH, (g + 1) * DH)
            x = base + 2 * g

            def both(ref):
                return (ref[x, :TOK].astype(f32) + ref[x + 1, :TOK].astype(f32)).astype(bf16)

            dkx_sc[:, cols] = both(first_ref)
            gv_sc[0, :, cols] = both(second_ref)
            for half in range(2):
                for c, ref in enumerate((first_ref, second_ref)):
                    at = (2 * half + c) * QTOK
                    dqx_sc[at : at + QTOK, cols] = ref[x + half, TOK : TOK + QTOK]

    @pl.when(core == 0)
    def _():
        take(0, share_ref, other_ref)

    @pl.when(core == 1)
    def _():
        take(HALF, other_ref, share_ref)

    out_copies[1].start()
    for i, (raw_ref, grad_ref, more_ref, out_ref) in enumerate(
        ((q_ref, dq_ref, dqx_sc, gq_sc), (k_ref, dk_ref, dkx_sc, gk_sc))
    ):
        scale = lax.rsqrt(sum_ref[2 * i] * (1.0 / INNER) + EPSILON)[:, :1]
        raw_last = raw_ref[0, :, LAST].astype(f32)
        grad_last = more_ref[...].astype(f32)
        inner = sum_ref[2 * i + 1][:, :1] + jnp.sum(grad_last * raw_last, axis=-1, keepdims=True)
        back = scale * scale * scale * (1.0 / INNER) * inner
        out_ref[0, :, LAST] = (scale * grad_last - back * raw_last).astype(bf16)
        raw = raw_ref[0, :, : SP * DH].astype(f32)
        out_ref[0, :, : SP * DH] = (scale * grad_ref[...].astype(f32) - back * raw).astype(bf16)
        out_copies[2 + i].start()
    me = lax.axis_index("sp")
    sums = [jnp.zeros((2, DH), f32) for _ in range(2)]
    at = TOK + QTOK
    for head in range(HEADS):
        owner, slot = owner_slot(owner_ref, head)
        members = [(head, 0)] if head < SP else [
            (2 * (head - SP) + d, 1) for d in (0, 1, HALF, HALF + 1)
        ]
        value = jnp.zeros((2, DH), f32)
        for d, kind in members:
            rows = share_ref[d, at : at + 16].astype(f32)
            base = kind * 6
            value += jnp.concatenate(
                [
                    rows[base + 3 * w : base + 3 * w + 1]
                    + rows[base + 3 * w + 1 : base + 3 * w + 2]
                    + rows[base + 3 * w + 2 : base + 3 * w + 3]
                    for w in range(2)
                ],
                axis=0,
            )
        for s in range(2):
            sums[s] = sums[s] + jnp.where((owner == me) & (slot == s), value, 0.0)
    factor = 1.0 / math.sqrt(SP * SEQ)
    for s in range(2):
        gain_ref[0, s] = sums[s] * factor
    for copy in out_copies:
        copy.wait()


def unpack(owner, q, k, dq, dk, gv, sums, share_back, other_back):
    vmem = pl.BlockSpec(memory_space=pltpu.VMEM)
    hbm = pl.BlockSpec(memory_space=pltpu.HBM)
    return pl.pallas_call(
        unpack_kernel,
        in_specs=[pl.BlockSpec(memory_space=pltpu.SMEM)] + [vmem] * 8,
        out_specs=[hbm, hbm, hbm, vmem],
        out_shape=[
            jax.ShapeDtypeStruct((1, TOK, INNER), bf16),
            jax.ShapeDtypeStruct((1, TOK, INNER), bf16),
            jax.ShapeDtypeStruct((1, TOK, INNER), bf16),
            jax.ShapeDtypeStruct((1, 2, 2, DH), f32),
        ],
        scratch_shapes=[
            pltpu.VMEM((1, TOK, INNER), bf16),
            pltpu.VMEM((1, TOK, INNER), bf16),
            pltpu.VMEM((1, TOK, EXTRA_HEADS * DH), bf16),
            pltpu.VMEM((TOK, EXTRA_HEADS * DH), bf16),
            pltpu.VMEM((TOK, EXTRA_HEADS * DH), bf16),
            pltpu.SemaphoreType.DMA((4,)),
        ],
        compiler_params=pltpu.CompilerParams(vmem_limit_bytes=UNPACK_LIMIT),
        name="unpack",
    )(owner, q, k, dq, dk, gv, sums, share_back, other_back)


def add_pair_kernel(keep_ref, got_ref, x_ref, out_ref, same_ref):
    same_ref[...] = x_ref[...]
    for d in range(SP):
        total = keep_ref[d, :TOK].astype(f32) + got_ref[d].astype(f32)
        out_ref[d, :TOK] = total.astype(bf16)
        out_ref[d, TOK:] = keep_ref[d, TOK:]


def add_pair(keep, got, x):
    vmem = pl.BlockSpec(memory_space=pltpu.VMEM)
    return pl.pallas_call(
        add_pair_kernel,
        in_specs=[vmem, vmem, vmem],
        out_shape=[
            jax.ShapeDtypeStruct((SP, SHARE_BACK, DH), bf16),
            jax.ShapeDtypeStruct(x.shape, x.dtype),
        ],
        compiler_params=pltpu.CompilerParams(vmem_limit_bytes=40 * MIB),
        name="add_pair",
    )(keep, got, x)


def add_sums_kernel(sum_ref, pair_ref, after_ref, out_ref):
    rows = []
    for i in range(4):
        rows += [*split3(sum_ref[i : i + 1])]
    extra = stack_rows(rows, 16)
    for d in range(SP):
        out_ref[d, TOK + QTOK :] = extra


def add_sums(sums, pair, after):
    vmem = pl.BlockSpec(memory_space=pltpu.VMEM)
    return pl.pallas_call(
        add_sums_kernel,
        in_specs=[vmem, vmem, pl.BlockSpec(memory_space=pl.ANY)],
        out_specs=vmem,
        out_shape=jax.ShapeDtypeStruct((SP, SHARE_BACK, DH), bf16),
        input_output_aliases={1: 0},
        compiler_params=pltpu.CompilerParams(vmem_limit_bytes=40 * MIB),
        name="add_sums",
    )(sums, pair, after)


def arrived_kernel(x_ref, out_ref):
    out_ref[...] = jnp.zeros_like(out_ref)


def arrived(x):
    return pl.pallas_call(
        arrived_kernel,
        in_specs=[pl.BlockSpec(memory_space=pl.ANY)],
        out_shape=jax.ShapeDtypeStruct((8, DH), f32),
        compiler_params=pltpu.CompilerParams(vmem_limit_bytes=61440 * 1024),
        name="arrived",
    )(x)


def after_kernel(x_ref, before_ref, out_ref):
    pass


def after(x, before, limit):
    anywhere = pl.BlockSpec(memory_space=pl.ANY)
    return pl.pallas_call(
        after_kernel,
        in_specs=[anywhere, anywhere],
        out_specs=anywhere,
        out_shape=jax.ShapeDtypeStruct(x.shape, x.dtype),
        input_output_aliases={0: 0},
        compiler_params=pltpu.CompilerParams(vmem_limit_bytes=limit),
        name="after",
    )(x, before)


def swap(x):
    return lax.ppermute(x, "fsdp", [(i, i ^ 1) for i in range(16)])


def exchange(field):
    return lax.all_to_all(field, "sp", split_axis=0, concat_axis=0, tiled=True)


def fsdp_sum(x, steps):
    across = (6, 7, 4, 5, 2, 3, 0, 1)
    partners = [
        [i ^ 1 for i in range(16)],
        [i ^ 2 for i in range(16)],
        [i ^ 4 for i in range(16)],
        [across[i // 2] * 2 + i % 2 for i in range(16)],
    ]
    for partner in partners[steps]:
        x = x + lax.ppermute(x, "fsdp", list(enumerate(partner)))
    return x


def per_device(query_raw, key_raw, value_in, grad_out, norm_gains, head_owner):
    main_send, rows = pack_main(query_raw, key_raw, value_in, grad_out, norm_gains)
    share_half, give = pack_share(query_raw, key_raw, value_in, grad_out, rows)
    main = exchange(main_send)
    other_half = (1 - core_index()) * HALF
    share_send = lax.dynamic_update_slice(share_half, swap(give), (other_half, 0, 0))
    share = exchange(after(share_send, arrived(main), 60 * MIB))
    main_out, part, extra = main_heads(head_owner, main)
    main_back = exchange(main_out)
    share = after(share, part, 40 * MIB)
    keep, give_back, part_s = shared_heads(head_owner, extra, share, swap(share))
    sums = fsdp_sum(jnp.concatenate([part, part_s], axis=0), slice(0, 2))
    pair, sums = add_pair(keep, swap(give_back), sums)
    sums = fsdp_sum(sums, slice(2, 4))
    share_back = exchange(add_sums(sums, pair, main_back))
    parts = unpack_main(query_raw, key_raw, main_back)
    return tuple(
        unpack(head_owner, query_raw, key_raw, *parts, share_back, swap(share_back))
    )


def solution(mesh):
    return jax.shard_map(
        per_device,
        mesh=mesh,
        in_specs=(
            P("fsdp", "sp", None),
            P("fsdp", "sp", None),
            P("fsdp", "sp", None),
            P("fsdp", "sp", None),
            P("sp", None, None, None),
            P(),
        ),
        out_specs=(
            P("fsdp", "sp", None),
            P("fsdp", "sp", None),
            P("fsdp", "sp", None),
            P("sp", None, None, None),
        ),
        check_vma=False,
    )
```

```python
import functools
import math

import jax
import jax.numpy as jnp
from jax import lax
from jax.experimental import pallas as pl
from jax.experimental.pallas import tpu as pltpu
from jax.sharding import PartitionSpec as P

EPSILON = 1e-06
LOG2E = math.log2(math.e)
f32 = jnp.float32
bf16 = jnp.bfloat16

HEADS = 20
DH = 128
INNER = HEADS * DH
SP = 16
TOK = 128
SEQ = SP * TOK
EXTRA_HEADS = HEADS - SP
HALF = SP // 2
QHALF = TOK // 2
QTOK = TOK // 4
MAIN_ROWS = 4 * TOK + 16
SHARE_ROWS = TOK + QHALF + 16
MAIN_BACK = 3 * TOK
SHARE_BACK = TOK + QTOK + 16
MIB = 2**20
UNPACK_LIMIT = 48 * 1024 * 1024
SCORE_SCALE = DH**-0.5
SAFE = 60.0
CHUNK = 256


def core_index():
    return lax.rem(lax.axis_index("fsdp"), 2)


def split3(x):
    hi = x.astype(bf16).astype(f32)
    mid = (x - hi).astype(bf16).astype(f32)
    return hi, mid, x - hi - mid


def split2(x):
    hi = x.astype(bf16).astype(f32)
    return hi, x - hi


def stack_rows(rows, count):
    if len(rows) < count:
        rows = rows + [jnp.zeros((count - len(rows), rows[0].shape[-1]), f32)]
    return jnp.concatenate(rows, axis=0).astype(bf16)


def contract(a, b, da, db):
    return lax.dot_general(a, b, (((da,), (db,)), ((), ())), preferred_element_type=f32)


def row_scale(raw):
    return lax.rsqrt(jnp.sum(raw * raw, axis=-1, keepdims=True) * (1.0 / INNER) + EPSILON)


def to_row(column):
    return jnp.broadcast_to(column, (TOK, TOK)).T[0:1]


def pack_main_kernel(
    q_hbm, k_hbm, v_hbm, do_hbm, gain_ref, main_ref, row_ref, q_ref, k_ref, v_ref, do_ref, sems
):
    pairs = ((q_hbm, q_ref), (k_hbm, k_ref), (v_hbm, v_ref), (do_hbm, do_ref))
    copies = [
        pltpu.make_async_copy(src, dst, sems.at[i]) for i, (src, dst) in enumerate(pairs)
    ]
    for copy in copies:
        copy.start()
    copies[0].wait()
    q_row = to_row(row_scale(q_ref[0].astype(f32)))
    copies[1].wait()
    k_row = to_row(row_scale(k_ref[0].astype(f32)))
    row_ref[0:1] = q_row
    row_ref[1:2] = k_row
    gains = gain_ref[0]
    rows = [*split2(q_row), *split2(k_row)]
    for slot in range(2):
        for which in range(2):
            rows += [*split3(gains[slot, which : which + 1])]
    extra = stack_rows(rows, 16)
    copies[2].wait()
    copies[3].wait()
    for d in range(SP):
        cols = slice(d * DH, (d + 1) * DH)
        for part, ref in enumerate((q_ref, k_ref, v_ref, do_ref)):
            main_ref[d, part * TOK : (part + 1) * TOK] = ref[0, :, cols]
        main_ref[d, 4 * TOK :] = extra


def pack_main(q, k, v, do, gains):
    hbm = pl.BlockSpec(memory_space=pltpu.HBM)
    return pl.pallas_call(
        pack_main_kernel,
        in_specs=[hbm, hbm, hbm, hbm, pl.BlockSpec(memory_space=pltpu.VMEM)],
        scratch_shapes=[pltpu.VMEM((1, TOK, INNER), bf16)] * 4 + [pltpu.SemaphoreType.DMA((4,))],
        out_shape=[
            jax.ShapeDtypeStruct((SP, MAIN_ROWS, DH), bf16),
            jax.ShapeDtypeStruct((8, DH), f32),
        ],
        compiler_params=pltpu.CompilerParams(vmem_limit_bytes=60 * MIB),
        name="pack_main",
    )(q, k, v, do, gains)


def pack_share_kernel(
    q_hbm, k_hbm, v_hbm, do_hbm, row_ref, share_ref, give_ref, q_ref, k_ref, v_ref, do_ref, sems
):
    pairs = ((q_hbm, q_ref), (k_hbm, k_ref), (v_hbm, v_ref), (do_hbm, do_ref))
    last = pl.ds(SP * DH, EXTRA_HEADS * DH)
    copies = [
        pltpu.make_async_copy(src.at[:, :, last], dst, sems.at[i])
        for i, (src, dst) in enumerate(pairs)
    ]
    for copy in copies:
        copy.start()
    for copy in copies:
        copy.wait()
    q_row = row_ref[0:1]
    k_row = row_ref[1:2]
    core = core_index()

    def fill(out_ref, base, first_ref, second_ref, with_scales):
        for p in range(HALF):
            cols = slice(p // 2 * DH, (p // 2 + 1) * DH)
            half = slice(p % 2 * QHALF, (p % 2 + 1) * QHALF)
            out_ref[base + p, :TOK] = first_ref[0, :, cols]
            out_ref[base + p, TOK : TOK + QHALF] = second_ref[0, half, cols]
            if with_scales:
                q_own = jnp.concatenate([q_row[:, half]] * 2, axis=1)
                tail = stack_rows([*split3(q_own), *split3(k_row)], 16)
            else:
                tail = jnp.zeros((16, DH), bf16)
            out_ref[base + p, TOK + QHALF :] = tail

    @pl.when(core == 0)
    def _():
        fill(share_ref, 0, k_ref, q_ref, True)
        fill(give_ref, 0, v_ref, do_ref, False)

    @pl.when(core == 1)
    def _():
        fill(share_ref, HALF, v_ref, do_ref, False)
        fill(give_ref, 0, k_ref, q_ref, True)


def pack_share(q, k, v, do, rows):
    hbm = pl.BlockSpec(memory_space=pltpu.HBM)
    return pl.pallas_call(
        pack_share_kernel,
        in_specs=[hbm, hbm, hbm, hbm, pl.BlockSpec(memory_space=pltpu.VMEM)],
        scratch_shapes=[pltpu.VMEM((1, TOK, EXTRA_HEADS * DH), bf16)] * 4
        + [pltpu.SemaphoreType.DMA((4,))],
        out_shape=[
            jax.ShapeDtypeStruct((SP, SHARE_ROWS, DH), bf16),
            jax.ShapeDtypeStruct((HALF, SHARE_ROWS, DH), bf16),
        ],
        compiler_params=pltpu.CompilerParams(vmem_limit_bytes=60 * MIB),
        name="pack_share",
    )(q, k, v, do, rows)


def owner_slot(owner_ref, head):
    owner = owner_ref[head]
    slot = jnp.int32(0)
    for other in range(HEADS):
        same = (owner_ref[other] == owner) & (other < head)
        slot = slot + same.astype(jnp.int32)
    return owner, slot


def picked_gains(owner_ref, gain_ref, head):
    owner, slot = owner_slot(owner_ref, head)
    rows = gain_ref[owner].astype(f32)
    sums = []
    for which in range(2):
        both = []
        for s in range(2):
            at = 4 + (s * 2 + which) * 3
            both.append(rows[at : at + 1] + rows[at + 1 : at + 2] + rows[at + 2 : at + 3])
        sums.append(jnp.where(slot == 0, both[0], both[1]))
    return sums


def scale_columns(rows, at, parts):
    return sum(rows[:, at + i] for i in range(parts)).T


def largest_square(x):
    return jnp.max(contract(jnp.ones((8, DH), bf16), x * x, 1, 1))


def fold(x):
    return jnp.sum(x.reshape(x.shape[0] // 8, 8, x.shape[1]), axis=0)


def prepare_keys(key_at, k_cols, gain_k, kn_sc, kt_sc, bound_sm):
    for j in range(SP):
        r = slice(j * TOK, (j + 1) * TOK)
        kn_sc[r] = (key_at(j).astype(f32) * k_cols[:, j : j + 1] * gain_k).astype(bf16)
    bound_sm[0] = largest_square(kn_sc[...])
    kt_sc[...] = kn_sc[...].T


def soften(qn_sc, do, value_at, kn_sc, e_sc, dp_sc, stat_sc, bound_sm):
    qn = qn_sc[...]
    square = largest_square(qn) * bound_sm[0]
    small = square * (SCORE_SCALE * SCORE_SCALE) <= SAFE * SAFE

    def run(top):
        total = delta = None
        for c in range(SEQ // CHUNK):
            r = slice(c * CHUNK, (c + 1) * CHUNK)
            s = contract(kn_sc[r], qn, 1, 1) * (SCORE_SCALE * LOG2E)
            e = jnp.exp2(s if top is None else s - top)
            e_sc[r] = e
            dp = contract(value_at(c), do, 1, 1)
            dp_sc[r] = dp
            total = fold(e) if total is None else total + fold(e)
            delta = fold(e * dp) if delta is None else delta + fold(e * dp)
        inv = 1.0 / jnp.sum(total, axis=0, keepdims=True)
        stat_sc[0:1] = inv
        stat_sc[1:2] = jnp.sum(delta, axis=0, keepdims=True) * inv

    @pl.when(small)
    def _():
        run(None)

    @pl.when(jnp.logical_not(small))
    def _():
        top = None
        for c in range(SEQ // CHUNK):
            r = slice(c * CHUNK, (c + 1) * CHUNK)
            s = contract(kn_sc[r], qn, 1, 1) * (SCORE_SCALE * LOG2E)
            part = jnp.max(s.reshape(CHUNK // 8, 8, s.shape[1]), axis=0)
            top = part if top is None else jnp.maximum(top, part)
        run(jnp.max(top, axis=0, keepdims=True))


def gradients(qn_sc, do, kt_sc, e_sc, dp_sc, stat_sc, store):
    qn = qn_sc[...]
    inv = stat_sc[0:1]
    delta = stat_sc[1:2]
    dq_t = None
    for c in range(SEQ // CHUNK):
        r = slice(c * CHUNK, (c + 1) * CHUNK)
        p = e_sc[r] * inv
        ds = (p * (dp_sc[r] - delta)).astype(bf16)
        store(r, contract(ds, qn, 1, 0), contract(p.astype(bf16), do, 1, 0))
        part = contract(kt_sc[:, r], ds, 1, 0)
        dq_t = part if dq_t is None else dq_t + part
    return dq_t.T * SCORE_SCALE


def attention_scratch(query_rows):
    return [
        pltpu.VMEM((SEQ, query_rows), f32),
        pltpu.VMEM((SEQ, query_rows), f32),
        pltpu.VMEM((8, query_rows), f32),
        pltpu.SMEM((1,), f32),
        pltpu.VMEM((SEQ, DH), bf16),
        pltpu.VMEM((DH, SEQ), bf16),
        pltpu.VMEM((SEQ, DH), f32),
        pltpu.VMEM((SEQ, DH), f32),
        pltpu.VMEM((query_rows, DH), bf16),
        pltpu.VMEM((query_rows, DH), f32),
    ]


def cost(query_rows):
    work = query_rows * SEQ
    return pl.CostEstimate(flops=10 * DH * work, bytes_accessed=4 * 2**20, transcendentals=work)


STEPS = 2


def main_kernel(
    owner_ref, field_hbm, back_hbm, part_ref, extra_ref, field_ref, back_ref, in_sems, sems, qg_acc,
    e_sc, dp_sc, stat_sc, bound_sm, kn_sc, kt_sc, dk_acc, dv_acc, qn_sc, qu_sc,
):
    sources = SP // STEPS
    rows = sources * TOK
    blocks = CHUNK // TOK

    def fetch(part, rows):
        at = (slice(None), pl.ds(part * TOK, rows))
        return pltpu.make_async_copy(field_hbm.at[at], field_ref.at[at], in_sems.at[part])

    fetches = [fetch(part, TOK) for part in range(4)] + [fetch(4, 16)]
    for part in (4, 1, 0, 2, 3):
        fetches[part].start()
    fetches[4].wait()
    extra_ref[...] = field_ref[:, 4 * TOK :]
    gain_q, gain_k = picked_gains(owner_ref, field_ref.at[:, 4 * TOK :], lax.axis_index("sp"))
    scales = field_ref[:, 4 * TOK :].astype(f32)
    q_cols = scale_columns(scales, 0, 2)
    k_cols = scale_columns(scales, 2, 2)
    qg_acc[...] = jnp.zeros_like(qg_acc)

    def key_at(j):
        return field_ref[j, TOK : 2 * TOK]

    def value_at(c):
        return field_ref[c * blocks : (c + 1) * blocks, 2 * TOK : 3 * TOK].reshape(CHUNK, DH)

    fetches[1].wait()

    def query_copy(step):
        at = (pl.ds(step * sources, sources), pl.ds(2 * TOK, TOK))
        return pltpu.make_async_copy(back_ref.at[at], back_hbm.at[at], sems.at[step])

    def key_copy(j):
        at = (j, pl.ds(0, 2 * TOK))
        return pltpu.make_async_copy(back_ref.at[at], back_hbm.at[at], sems.at[STEPS + j])

    prepare_keys(key_at, k_cols, gain_k, kn_sc, kt_sc, bound_sm)
    dk_acc[...] = jnp.zeros_like(dk_acc)
    dv_acc[...] = jnp.zeros_like(dv_acc)

    for part in (0, 2, 3):
        fetches[part].wait()

    @pl.loop(0, STEPS)
    def _(step):
        for b in range(STEPS):

            @pl.when(step == b)
            def _():
                for j in range(sources):
                    at = b * sources + j
                    r = slice(j * TOK, (j + 1) * TOK)
                    unit = field_ref[at, :TOK].astype(f32) * q_cols[:, at : at + 1]
                    qu_sc[r] = unit
                    qn_sc[r] = (unit * gain_q).astype(bf16)

        mine = pl.ds(step * sources, sources)
        do = field_ref[mine, 3 * TOK : 4 * TOK].reshape(rows, DH)
        soften(qn_sc, do, value_at, kn_sc, e_sc, dp_sc, stat_sc, bound_sm)

        def store(r, dk_part, dv_part):
            dk_acc[r] += dk_part
            dv_acc[r] += dv_part

        dq = gradients(qn_sc, do, kt_sc, e_sc, dp_sc, stat_sc, store)
        back_ref[mine, 2 * TOK :] = (dq * gain_q).astype(bf16).reshape(sources, TOK, DH)
        query_copy(step).start()
        qg_acc[...] += fold(dq * qu_sc[...])

    key_part = jnp.zeros((8, DH), f32)
    for j in range(SP):
        r = slice(j * TOK, (j + 1) * TOK)
        dk = dk_acc[r] * SCORE_SCALE
        key_part += fold(dk * (key_at(j).astype(f32) * k_cols[:, j : j + 1]))
        back_ref[j, :TOK] = (dk * gain_k).astype(bf16)
        back_ref[j, TOK : 2 * TOK] = dv_acc[r].astype(bf16)
        key_copy(j).start()
    part_ref[0:1] = jnp.sum(qg_acc[...], axis=0, keepdims=True)
    part_ref[1:2] = jnp.sum(key_part, axis=0, keepdims=True)
    for step in range(STEPS):
        query_copy(step).wait()
    for j in range(SP):
        key_copy(j).wait()


def main_heads(owner, field):
    return pl.pallas_call(
        main_kernel,
        in_specs=[
            pl.BlockSpec(memory_space=pltpu.SMEM),
            pl.BlockSpec(memory_space=pl.ANY),
        ],
        out_shape=[
            jax.ShapeDtypeStruct((SP, MAIN_BACK, DH), bf16),
            jax.ShapeDtypeStruct((2, DH), f32),
            jax.ShapeDtypeStruct((SP, 16, DH), bf16),
        ],
        out_specs=[
            pl.BlockSpec(memory_space=pltpu.HBM),
            pl.BlockSpec(memory_space=pltpu.VMEM),
            pl.BlockSpec(memory_space=pltpu.VMEM),
        ],
        scratch_shapes=[
            pltpu.VMEM((SP, MAIN_ROWS, DH), bf16),
            pltpu.VMEM((SP, MAIN_BACK, DH), bf16),
            pltpu.SemaphoreType.DMA((5,)),
            pltpu.SemaphoreType.DMA((STEPS + SP,)),
            pltpu.VMEM((8, DH), f32),
        ]
        + attention_scratch(SEQ // STEPS),
        compiler_params=pltpu.CompilerParams(vmem_limit_bytes=53760 * 1024),
        cost_estimate=cost(SEQ),
        name="main_heads",
    )(owner, field)


def shared_kernel(
    owner_ref, extra_ref, mine_ref, other_ref, keep_ref, give_ref, part_ref,
    kq_ref, vd_ref, v_sc,
    e_sc, dp_sc, stat_sc, bound_sm, kn_sc, kt_sc, dk_acc, dv_acc, qn_sc, qu_sc,
):
    core = core_index()

    def load(kq_src, vd_src):
        kq_ref[...] = kq_src[...]
        vd_ref[...] = vd_src[...]

    @pl.when(core == 0)
    def _():
        load(mine_ref, other_ref)

    @pl.when(core == 1)
    def _():
        load(other_ref, mine_ref)

    head = SP + lax.rem(lax.axis_index("sp") // 2, EXTRA_HEADS)
    gain_q, gain_k = picked_gains(owner_ref, extra_ref, head)
    scales = kq_ref[:, TOK + QHALF :].astype(f32)
    q_cols = scale_columns(scales, 0, 3)
    q_cols = jnp.where(core == 0, q_cols[:QTOK], q_cols[QTOK:QHALF])
    k_cols = scale_columns(scales, 3, 3)
    prepare_keys(lambda j: kq_ref[j, :TOK], k_cols, gain_k, kn_sc, kt_sc, bound_sm)

    def quarter(ref):
        low = ref[:, TOK : TOK + QTOK]
        high = ref[:, TOK + QTOK : TOK + QHALF]
        return jnp.where(core == 0, low, high)

    q = quarter(kq_ref)
    do = quarter(vd_ref).reshape(SP * QTOK, DH)
    for j in range(SP):
        r = slice(j * QTOK, (j + 1) * QTOK)
        unit = q[j].astype(f32) * q_cols[:, j : j + 1]
        qu_sc[r] = unit
        qn_sc[r] = (unit * gain_q).astype(bf16)
        v_sc[j * TOK : (j + 1) * TOK] = vd_ref[j, :TOK]
    soften(qn_sc, do, lambda c: v_sc[c * CHUNK : (c + 1) * CHUNK], kn_sc, e_sc, dp_sc, stat_sc, bound_sm)

    def store(r, dk_part, dv_part):
        dk_acc[r] = dk_part
        dv_acc[r] = dv_part

    dq = gradients(qn_sc, do, kt_sc, e_sc, dp_sc, stat_sc, store)
    keep_ref[:, TOK : TOK + QTOK] = (dq * gain_q).astype(bf16).reshape(SP, QTOK, DH)
    keep_ref[:, TOK + QTOK :] = jnp.zeros((SP, 16, DH), bf16)
    key_part = jnp.zeros((8, DH), f32)
    for j in range(SP):
        r = slice(j * TOK, (j + 1) * TOK)
        dk = dk_acc[r] * SCORE_SCALE
        key_part += fold(dk * (kq_ref[j, :TOK].astype(f32) * k_cols[:, j : j + 1]))
        dk = (dk * gain_k).astype(bf16)
        dv = dv_acc[r].astype(bf16)

        keep_ref[j, :TOK] = jnp.where(core == 0, dk, dv)
        give_ref[j] = jnp.where(core == 0, dv, dk)
    part_ref[0:1] = jnp.sum(fold(dq * qu_sc[...]), axis=0, keepdims=True)
    part_ref[1:2] = jnp.sum(key_part, axis=0, keepdims=True)


def shared_heads(owner, extra, mine, other):
    vmem = pl.BlockSpec(memory_space=pltpu.VMEM)
    return pl.pallas_call(
        shared_kernel,
        in_specs=[
            pl.BlockSpec(memory_space=pltpu.SMEM),
            vmem,
            vmem,
            vmem,
        ],
        out_shape=[
            jax.ShapeDtypeStruct((SP, SHARE_BACK, DH), bf16),
            jax.ShapeDtypeStruct((SP, TOK, DH), bf16),
            jax.ShapeDtypeStruct((2, DH), f32),
        ],
        scratch_shapes=[
            pltpu.VMEM((SP, SHARE_ROWS, DH), bf16),
            pltpu.VMEM((SP, SHARE_ROWS, DH), bf16),
            pltpu.VMEM((SEQ, DH), bf16),
        ]
        + attention_scratch(SP * QTOK),
        compiler_params=pltpu.CompilerParams(vmem_limit_bytes=40 * MIB),
        cost_estimate=cost(SP * QTOK),
        name="shared_heads",
    )(owner, extra, mine, other)


LAST = slice(SP * DH, INNER)


def unpack_main_kernel(q_ref, k_ref, main_ref, dq_ref, dk_ref, gv_ref, sum_ref):
    for d in range(SP):
        cols = slice(d * DH, (d + 1) * DH)
        dk_ref[:, cols] = main_ref[d, :TOK]
        gv_ref[0, :, cols] = main_ref[d, TOK : 2 * TOK]
        dq_ref[:, cols] = main_ref[d, 2 * TOK : 3 * TOK]
    for i, (raw_ref, grad_ref) in enumerate(((q_ref, dq_ref), (k_ref, dk_ref))):
        raw = raw_ref[0].astype(f32)
        squares = jnp.sum(raw * raw, axis=-1, keepdims=True)
        inner = jnp.sum(
            grad_ref[...].astype(f32) * raw[:, : SP * DH], axis=-1, keepdims=True
        )
        sum_ref[2 * i] = jnp.broadcast_to(squares, (TOK, DH))
        sum_ref[2 * i + 1] = jnp.broadcast_to(inner, (TOK, DH))


def unpack_main(q, k, main_back):
    return pl.pallas_call(
        unpack_main_kernel,
        out_shape=[
            jax.ShapeDtypeStruct((TOK, SP * DH), bf16),
            jax.ShapeDtypeStruct((TOK, SP * DH), bf16),
            jax.ShapeDtypeStruct((1, TOK, SP * DH), bf16),
            jax.ShapeDtypeStruct((4, TOK, DH), f32),
        ],
        compiler_params=pltpu.CompilerParams(vmem_limit_bytes=UNPACK_LIMIT),
        name="unpack_main",
    )(q, k, main_back)


def unpack_kernel(
    owner_ref, q_ref, k_ref, dq_ref, dk_ref, gvm_ref, sum_ref, share_ref, other_ref,
    gq_hbm, gk_hbm, gv_hbm, gain_ref, gq_sc, gk_sc, gv_sc, dqx_sc, dkx_sc, sems,
):
    main_cols = pl.ds(0, SP * DH)
    last_cols = pl.ds(SP * DH, EXTRA_HEADS * DH)
    out_copies = [
        pltpu.make_async_copy(gvm_ref, gv_hbm.at[:, :, main_cols], sems.at[0]),
        pltpu.make_async_copy(gv_sc, gv_hbm.at[:, :, last_cols], sems.at[1]),
        pltpu.make_async_copy(gq_sc, gq_hbm, sems.at[2]),
        pltpu.make_async_copy(gk_sc, gk_hbm, sems.at[3]),
    ]
    out_copies[0].start()
    core = core_index()

    def take(first, second):
        for g in range(EXTRA_HEADS):
            cols = slice(g * DH, (g + 1) * DH)
            x = 2 * g

            def both(source):
                ref, base = source
                return (ref[base + x, :TOK].astype(f32) + ref[base + x + 1, :TOK].astype(f32)).astype(bf16)

            dkx_sc[:, cols] = both(first)
            gv_sc[0, :, cols] = both(second)
            for half in range(2):
                for c, (ref, base) in enumerate((first, second)):
                    at = (2 * half + c) * QTOK
                    dqx_sc[at : at + QTOK, cols] = ref[base + x + half, TOK : TOK + QTOK]

    @pl.when(core == 0)
    def _():
        take((share_ref, 0), (other_ref, 0))

    @pl.when(core == 1)
    def _():
        take((other_ref, 0), (share_ref, HALF))

    out_copies[1].start()
    for i, (raw_ref, grad_ref, more_ref, out_ref) in enumerate(
        ((q_ref, dq_ref, dqx_sc, gq_sc), (k_ref, dk_ref, dkx_sc, gk_sc))
    ):
        scale = lax.rsqrt(sum_ref[2 * i] * (1.0 / INNER) + EPSILON)[:, :1]
        raw_last = raw_ref[0, :, LAST].astype(f32)
        grad_last = more_ref[...].astype(f32)
        inner = sum_ref[2 * i + 1][:, :1] + jnp.sum(grad_last * raw_last, axis=-1, keepdims=True)
        back = scale * scale * scale * (1.0 / INNER) * inner
        out_ref[0, :, LAST] = (scale * grad_last - back * raw_last).astype(bf16)
        raw = raw_ref[0, :, : SP * DH].astype(f32)
        out_ref[0, :, : SP * DH] = (scale * grad_ref[...].astype(f32) - back * raw).astype(bf16)
        out_copies[2 + i].start()
    me = lax.axis_index("sp")
    sums = [jnp.zeros((2, DH), f32) for _ in range(2)]
    at = TOK + QTOK
    for head in range(HEADS):
        owner, slot = owner_slot(owner_ref, head)
        members = [(head, 0)] if head < SP else [
            (2 * (head - SP) + d, 1) for d in (0, 1, HALF, HALF + 1)
        ]
        value = jnp.zeros((2, DH), f32)
        for d, kind in members:
            rows = share_ref[d, at : at + 16].astype(f32)
            base = kind * 6
            value += jnp.concatenate(
                [
                    rows[base + 3 * w : base + 3 * w + 1]
                    + rows[base + 3 * w + 1 : base + 3 * w + 2]
                    + rows[base + 3 * w + 2 : base + 3 * w + 3]
                    for w in range(2)
                ],
                axis=0,
            )
        for s in range(2):
            sums[s] = sums[s] + jnp.where((owner == me) & (slot == s), value, 0.0)
    factor = 1.0 / math.sqrt(SP * SEQ)
    for s in range(2):
        gain_ref[0, s] = sums[s] * factor
    for copy in out_copies:
        copy.wait()


def unpack(owner, q, k, dq, dk, gv, sums, share_back, other_back):
    vmem = pl.BlockSpec(memory_space=pltpu.VMEM)
    hbm = pl.BlockSpec(memory_space=pltpu.HBM)
    return pl.pallas_call(
        unpack_kernel,
        in_specs=[pl.BlockSpec(memory_space=pltpu.SMEM)] + [vmem] * 8,
        out_specs=[hbm, hbm, hbm, vmem],
        out_shape=[
            jax.ShapeDtypeStruct((1, TOK, INNER), bf16),
            jax.ShapeDtypeStruct((1, TOK, INNER), bf16),
            jax.ShapeDtypeStruct((1, TOK, INNER), bf16),
            jax.ShapeDtypeStruct((1, 2, 2, DH), f32),
        ],
        scratch_shapes=[
            pltpu.VMEM((1, TOK, INNER), bf16),
            pltpu.VMEM((1, TOK, INNER), bf16),
            pltpu.VMEM((1, TOK, EXTRA_HEADS * DH), bf16),
            pltpu.VMEM((TOK, EXTRA_HEADS * DH), bf16),
            pltpu.VMEM((TOK, EXTRA_HEADS * DH), bf16),
            pltpu.SemaphoreType.DMA((4,)),
        ],
        compiler_params=pltpu.CompilerParams(vmem_limit_bytes=UNPACK_LIMIT),
        name="unpack",
    )(owner, q, k, dq, dk, gv, sums, share_back, other_back)


def add_pair_kernel(keep_ref, got_ref, x_ref, out_ref, same_ref):
    same_ref[...] = x_ref[...]
    for d in range(SP):
        total = keep_ref[d, :TOK].astype(f32) + got_ref[d].astype(f32)
        out_ref[d, :TOK] = total.astype(bf16)
        out_ref[d, TOK:] = keep_ref[d, TOK:]


def add_pair(keep, got, x):
    vmem = pl.BlockSpec(memory_space=pltpu.VMEM)
    return pl.pallas_call(
        add_pair_kernel,
        in_specs=[vmem, vmem, vmem],
        out_shape=[
            jax.ShapeDtypeStruct((SP, SHARE_BACK, DH), bf16),
            jax.ShapeDtypeStruct(x.shape, x.dtype),
        ],
        compiler_params=pltpu.CompilerParams(vmem_limit_bytes=40 * MIB),
        name="add_pair",
    )(keep, got, x)


def add_sums_kernel(sum_ref, pair_ref, after_ref, out_ref):
    rows = []
    for i in range(4):
        rows += [*split3(sum_ref[i : i + 1])]
    extra = stack_rows(rows, 16)
    for d in range(SP):
        out_ref[d, TOK + QTOK :] = extra


def add_sums(sums, pair, after):
    vmem = pl.BlockSpec(memory_space=pltpu.VMEM)
    return pl.pallas_call(
        add_sums_kernel,
        in_specs=[vmem, vmem, pl.BlockSpec(memory_space=pl.ANY)],
        out_specs=vmem,
        out_shape=jax.ShapeDtypeStruct((SP, SHARE_BACK, DH), bf16),
        input_output_aliases={1: 0},
        compiler_params=pltpu.CompilerParams(vmem_limit_bytes=40 * MIB),
        name="add_sums",
    )(sums, pair, after)


def after_kernel(x_ref, before_ref, out_ref):
    pass


def after(x, before):
    anywhere = pl.BlockSpec(memory_space=pl.ANY)
    return pl.pallas_call(
        after_kernel,
        in_specs=[anywhere, anywhere],
        out_specs=anywhere,
        out_shape=jax.ShapeDtypeStruct(x.shape, x.dtype),
        input_output_aliases={0: 0},
        compiler_params=pltpu.CompilerParams(vmem_limit_bytes=40 * MIB),
        name="after",
    )(x, before)


def swap(x):
    return lax.ppermute(x, "fsdp", [(i, i ^ 1) for i in range(16)])


def exchange(field):
    return lax.all_to_all(field, "sp", split_axis=0, concat_axis=0, tiled=True)


def fsdp_sum(x, steps):
    across = (6, 7, 4, 5, 2, 3, 0, 1)
    partners = [
        [i ^ 1 for i in range(16)],
        [i ^ 2 for i in range(16)],
        [i ^ 4 for i in range(16)],
        [across[i // 2] * 2 + i % 2 for i in range(16)],
    ]
    for partner in partners[steps]:
        x = x + lax.ppermute(x, "fsdp", list(enumerate(partner)))
    return x


def per_device(query_raw, key_raw, value_in, grad_out, norm_gains, head_owner):
    main_send, rows = pack_main(query_raw, key_raw, value_in, grad_out, norm_gains)
    share_half, give = pack_share(query_raw, key_raw, value_in, grad_out, rows)
    main = exchange(main_send)
    other_half = (1 - core_index()) * HALF
    nothing = main[0, 4 * TOK, 0] * 0
    share_send = lax.dynamic_update_slice(share_half, swap(give) + nothing, (other_half, 0, 0))
    share = exchange(share_send)
    main_out, part, extra = main_heads(head_owner, main)
    main_back = exchange(main_out)
    share = after(share, part)
    keep, give_back, part_s = shared_heads(head_owner, extra, share, swap(share))
    sums = fsdp_sum(jnp.concatenate([part, part_s], axis=0), slice(0, 2))
    pair, sums = add_pair(keep, swap(give_back), sums)
    sums = fsdp_sum(sums, slice(2, 4))
    share_back = exchange(add_sums(sums, pair, main_back))
    wanted = lax.dynamic_slice_in_dim(share_back, other_half, HALF, 0)
    parts = unpack_main(query_raw, key_raw, main_back)
    return tuple(
        unpack(head_owner, query_raw, key_raw, *parts, share_back, swap(wanted))
    )


def solution(mesh):
    return jax.shard_map(
        per_device,
        mesh=mesh,
        in_specs=(
            P("fsdp", "sp", None),
            P("fsdp", "sp", None),
            P("fsdp", "sp", None),
            P("fsdp", "sp", None),
            P("sp", None, None, None),
            P(),
        ),
        out_specs=(
            P("fsdp", "sp", None),
            P("fsdp", "sp", None),
            P("fsdp", "sp", None),
            P("sp", None, None, None),
        ),
        check_vma=False,
    )
```
